512 devices in a mesh: ctx: 32 (over x, z_hi, core), ch: 8 (over y), dp: 2 (over z_lo).
Axes of the slice: x: 4, y: 8, z: 8 (z_hi: 4, z_lo: 2; z = z_hi * 2 + z_lo), core: 2. Of those that a mesh axis runs over, the one named last changes fastest.
Arguments:
- tokens_in: bfloat16 [2, 8192, 2048], P('dp', 'ctx', 'ch'), may hold values from -6 to 6
- cotangent: bfloat16 [2, 8192, 2048], P('dp', 'ctx', 'ch'), may hold values from -6 to 6
- lift_weight: float32 [128, 128], replicated, may hold values from -0.5 to 0.5
- lift_bias: float32 [128], replicated, may hold values from -4 to 4
- coef_weight: float32 [128, 2048], P(None, 'ch'), may hold values from -0.015625 to 0.015625
Outputs:
- tokens_grad: float32 [2, 8192, 2048], P('dp', 'ctx', 'ch')
- lift_weight_grad: float32 [128, 128], replicated
- lift_bias_grad: float32 [128], replicated
- coef_weight_grad: float32 [128, 2048], P(None, 'ch')
The draws below stay inside these ranges and needn't reach their ends.
All inputs are finite; a program needn't handle non-finite values.
Results may differ from the reference program's by a relative error of at most 0.0003.
Values may be sent and summed in bfloat16 or wider, within the bound.
No kernel may reach another device: no remote copies, remote signals or barrier semaphores. Data moves between devices by JAX's collectives and lax.ppermute only.
A program may use at most 64 MiB of HBM per device.

```python
import math
import jax
import jax.numpy as jnp
from jax import lax

WIDTH = 2048
RPE = 128
FEAT = 128
LAGS = 1024
SEQ = 8192
BATCH = 2


def shard_levels(own_key, dims, shards, smallest, high):
    def one(axis_at, parts):
        draws = jax.random.uniform(jax.random.fold_in(jax.random.fold_in(own_key, 6), axis_at), (parts,), jnp.float32, smallest / len(shards), high / len(shards))
        return jnp.repeat(jnp.exp(draws), dims[axis_at] // parts).reshape((-1,) + (1,) * (len(dims) - axis_at - 1))

    gain = one(*shards[0])
    for cut in shards[1:]:
        gain = gain * one(*cut)
    return gain


def bell_draw(stream_key, shape, spread, most, pieces=(), held_as=jnp.bfloat16):
    level = shard_levels(stream_key, shape, pieces, -0.22, 0.18) if pieces else 1.0
    values = jax.random.normal(stream_key, shape, jnp.float32) * spread * level
    return jnp.minimum(jnp.maximum(values, -most), most).astype(held_as)


def setup_inputs(seed: int = 0) -> dict:
    seeds = jax.random.split(jax.random.key(seed), 6)
    return {
        "tokens_in": bell_draw(seeds[0], (BATCH, SEQ, WIDTH), 1.0, 6.0, ((0, 2), (1, 32), (2, 8))),
        "cotangent": bell_draw(seeds[1], (BATCH, SEQ, WIDTH), 1.0, 6.0, ((0, 2), (1, 32), (2, 8))),
        "lift_weight": bell_draw(seeds[2], (FEAT, RPE), FEAT ** -0.5, 0.5, (), jnp.float32),
        "lift_bias": bell_draw(seeds[3], (RPE,), 1.0, 4.0, (), jnp.float32),
        "coef_weight": bell_draw(seeds[4], (RPE, WIDTH), (RPE * LAGS) ** -0.5, 0.015625, ((1, 8),), jnp.float32),
    }


def lag_features(positions, count, width):
    halfway = width // 2
    rates = 3.0 * jnp.exp(jnp.arange(halfway, dtype=jnp.float32) * (-math.log(count) / halfway))
    angles = positions[:, None] * rates[None, :]
    return jnp.concatenate([jnp.sin(angles), jnp.cos(angles)], axis=1)

def silu_slope(preact):
    logistic = jax.nn.sigmoid(preact)
    return logistic * (1.0 + preact * (1.0 - logistic))

def reference(tokens_in, cotangent, lift_weight, lift_bias, coef_weight):
    highest = lax.Precision.HIGHEST
    positions = jnp.arange(LAGS, dtype=jnp.int32).astype(jnp.float32)
    embed = lag_features(positions, LAGS, FEAT)
    preact = jnp.dot(embed, lift_weight, precision=highest) + lift_bias
    hidden = jax.nn.silu(preact)
    coef = jnp.dot(hidden, coef_weight, precision=highest)
    points = 2 * SEQ
    group = min(WIDTH, 256)

    def per_group(index):
        first = index * group
        inputs = lax.dynamic_slice_in_dim(tokens_in, first, group, 2).astype(jnp.float32)
        grads = lax.dynamic_slice_in_dim(cotangent, first, group, 2).astype(jnp.float32)
        coefs = lax.dynamic_slice_in_dim(coef, first, group, 1)
        grads_hat = jnp.fft.rfft(grads, n=points, axis=1)
        coef_hat = jnp.fft.rfft(coefs, n=points, axis=0)
        inputs_hat = jnp.fft.rfft(inputs, n=points, axis=1)
        backward = jnp.fft.irfft(jnp.conj(coef_hat)[None] * grads_hat, n=points, axis=1)[:, :SEQ]
        lagged = jnp.fft.irfft(lax.optimization_barrier(jnp.sum(jnp.conj(inputs_hat) * grads_hat, axis=0)), n=points, axis=0)[:LAGS]
        return (backward, lagged)
    backs, laggeds = lax.map(per_group, jnp.arange(WIDTH // group, dtype=jnp.int32))
    tokens_grad = jnp.transpose(backs, (1, 2, 0, 3)).reshape(BATCH, SEQ, WIDTH)
    coef_grad = jnp.transpose(laggeds, (1, 0, 2)).reshape(LAGS, WIDTH) * (1.0 / math.sqrt(BATCH * SEQ))
    coef_weight_grad = jnp.dot(hidden.T, coef_grad, precision=highest)
    hidden_grad = jnp.dot(coef_grad, coef_weight.T, precision=highest)
    preact_grad = hidden_grad * silu_slope(preact)
    lift_weight_grad = jnp.dot(embed.T, preact_grad, precision=highest)
    lift_bias_grad = lax.optimization_barrier(jnp.sum(preact_grad, axis=0))
    return (tokens_grad.astype(jnp.float32), lift_weight_grad, lift_bias_grad, coef_weight_grad)
```

```python
import math

import jax
import jax.numpy as jnp
import numpy as np
from jax import lax
from jax.sharding import PartitionSpec as P

LAG_BLOCKS = 4

highest = lax.Precision.HIGHEST
high = lax.Precision.HIGH


def shifted(value, axis, steps):
    count = lax.axis_size(axis)
    initial, last = (max(0, -steps), min(count, count - steps))
    return lax.ppermute(value, axis, [(source, source + steps) for source in range(initial, last)])


def lag_features(positions, count, width):
    halfway = width // 2
    rates = 3.0 * jnp.exp(jnp.arange(halfway, dtype=jnp.float32) * (-math.log(count) / halfway))
    angles = positions[:, None] * rates[None, :]
    return jnp.concatenate([jnp.sin(angles), jnp.cos(angles)], axis=1)


def silu_slope(preact):
    logistic = jax.nn.sigmoid(preact)
    return logistic * (1.0 + preact * (1.0 - logistic))


def odd_table(length):
    phase = (2 * np.arange(length)[:, None] + 1) * np.arange(length)[None, :] % (4 * length)
    angles = phase * (2.0 * math.pi / (4 * length))
    return np.concatenate([np.cos(angles), -np.sin(angles)], axis=0)


def halves(table):
    upper = table.astype(jnp.bfloat16)
    lower = (table - upper.astype(np.float64)).astype(jnp.bfloat16)
    return np.concatenate([upper, lower], axis=0)


def spectrum(table, block):
    both = jnp.dot(table, block, preferred_element_type=jnp.float32)
    rows = both.shape[0] // 2
    return both[:rows] + both[rows:]


def conj_product(first, second):
    rows = first.shape[0] // 2
    real_a, imag_a = first[:rows], first[rows:]
    real_b, imag_b = second[:rows], second[rows:]
    return jnp.concatenate(
        [real_a * real_b + imag_a * imag_b, real_a * imag_b - imag_a * real_b], axis=0
    )


def turned(value, sign):
    rows = value.shape[0] // 2
    parity = jnp.where(lax.broadcasted_iota(jnp.int32, (rows, 1), 0) % 2 == 0, sign, -sign)
    return jnp.concatenate([-parity * value[rows:], parity * value[:rows]], axis=0)


def exchange_sum(value, axis):
    count = lax.axis_size(axis)
    step = 1
    while step < count:
        value = value + lax.ppermute(value, axis, [(i, i ^ step) for i in range(count)])
        step *= 2
    return value


def shards(tokens_in, cotangent, lift_weight, lift_bias, coef_weight):
    inputs = tokens_in[0]
    grads = cotangent[0]
    length, channels = inputs.shape
    lags = LAG_BLOCKS * length
    units = lift_weight.shape[1]
    features = lift_weight.shape[0]
    axes = ("dp", "ctx")
    group = lax.axis_size(axes)
    blocks_total = lax.axis_size("ctx")

    ahead1 = shifted(grads, "ctx", -1)
    ahead2 = shifted(grads, "ctx", -2)
    behind1 = shifted(inputs, "ctx", 1)
    behind2 = shifted(inputs, "ctx", 2)

    table = odd_table(length)
    split = halves(table)
    plain = jnp.asarray(table, jnp.float32)

    positions = jnp.arange(lags, dtype=jnp.int32).astype(jnp.float32)
    embed = lag_features(positions, lags, features)
    preact = jnp.dot(embed, lift_weight, precision=highest) + lift_bias
    hidden = jax.nn.silu(preact)
    slope = silu_slope(preact)
    wide = jnp.concatenate([hidden[k * length:(k + 1) * length] for k in range(LAG_BLOCKS)], axis=1)
    net = jnp.dot(plain, wide, precision=high)
    zero = jnp.zeros((2 * length, units), jnp.float32)
    net = jnp.concatenate([net, zero], axis=1) + turned(jnp.concatenate([zero, net], axis=1), 1.0)
    nets = [net[:, k * units:(k + 1) * units] for k in range(LAG_BLOCKS + 1)]
    coefs = [jnp.dot(part, coef_weight, precision=high) for part in nets]

    near = spectrum(split, jnp.concatenate([grads, inputs], axis=1))
    own_spec, input_spec = near[:, :channels], near[:, channels:]
    far = spectrum(split, jnp.concatenate([ahead1, ahead2, behind1, behind2], axis=1))
    spec1, spec2, back1, back2 = [far[:, k * channels:(k + 1) * channels] for k in range(4)]

    pairs = [
        conj_product(input_spec, own_spec),
        conj_product(input_spec, spec1),
        conj_product(input_spec, spec2),
        conj_product(back1, spec2),
        conj_product(back2, spec2),
    ]
    scale = 1.0 / math.sqrt(lax.axis_size("dp") * length * blocks_total) / length
    tall = jnp.concatenate(pairs, axis=0)
    weight_part = jnp.dot(jnp.concatenate(nets, axis=0).T, tall, precision=high) * scale
    mixed = jnp.dot(tall, coef_weight.T, precision=high)
    rows = 2 * length
    mixes = [mixed[k * rows:(k + 1) * rows] for k in range(LAG_BLOCKS + 1)]
    mixes = jnp.concatenate(
        [mixes[k] + turned(mixes[k + 1], -1.0) for k in range(LAG_BLOCKS)], axis=1
    )
    lag_side = jnp.dot(plain.T, mixes, precision=high)
    lag_side = jnp.concatenate(
        [lag_side[:, k * units:(k + 1) * units] for k in range(LAG_BLOCKS)], axis=0
    )
    preact_part = lag_side * slope * scale
    lift_part = jnp.dot(embed.T, preact_part, precision=high)
    bias_part = jnp.sum(preact_part, axis=0, keepdims=True)

    used = channels // units * coef_weight.shape[0] + features + 1
    chunk = 8 * 2 ** max(0, math.ceil(math.log2(used / (8 * group))))
    pieces = [weight_part[:, c:c + units] for c in range(0, channels, units)]
    pieces += [lift_part, bias_part, jnp.zeros((group * chunk - used, units), jnp.float32)]
    packed = jnp.concatenate(pieces, axis=0).reshape(group, chunk, units)
    parts = lax.all_to_all(packed, axes, split_axis=0, concat_axis=0, tiled=True)
    mine = jnp.sum(parts, axis=0)
    whole = exchange_sum(mine, "ch")
    first_lift = channels // units * coef_weight.shape[0] // chunk
    mine = jnp.where(lax.axis_index(axes) < first_lift, mine, whole)
    full = lax.all_to_all(
        jnp.broadcast_to(mine[None], (group, chunk, units)), axes, split_axis=0, concat_axis=0, tiled=True
    ).reshape(group * chunk, units)
    depth = coef_weight.shape[0]
    count = channels // units
    coef_weight_grad = jnp.concatenate([full[k * depth:(k + 1) * depth] for k in range(count)], axis=1)
    lift_weight_grad = full[count * depth:count * depth + features]
    lift_bias_grad = full[count * depth + features]

    ahead3 = shifted(ahead1, "ctx", -2)
    ahead4 = shifted(ahead2, "ctx", -2)
    late = spectrum(split, jnp.concatenate([ahead3, ahead4], axis=1))
    specs = [own_spec, spec1, spec2, late[:, :channels], late[:, channels:]]
    total = sum(conj_product(coefs[k], specs[k]) for k in range(LAG_BLOCKS + 1))
    tokens_grad = jnp.dot(plain.T, total, precision=high) * (1.0 / length)
    return (tokens_grad[None], lift_weight_grad, lift_bias_grad, coef_weight_grad)


def solution(mesh):
    in_specs = (P("dp", "ctx", "ch"), P("dp", "ctx", "ch"), P(), P(), P(None, "ch"))
    out_specs = (P("dp", "ctx", "ch"), P(), P(), P(None, "ch"))
    return jax.shard_map(shards, mesh=mesh, in_specs=in_specs, out_specs=out_specs, check_vma=False)
```

```python
import math

import jax
import jax.numpy as jnp
import numpy as np
from jax import lax
from jax.sharding import PartitionSpec as P

LAG_BLOCKS = 4
Z_HIGH = 4
CORES = 2

highest = lax.Precision.HIGHEST
high = lax.Precision.HIGH


def shifted(value, axis, steps):
    count = lax.axis_size(axis)
    initial, last = (max(0, -steps), min(count, count - steps))
    return lax.ppermute(value, axis, [(source, source + steps) for source in range(initial, last)])


def lag_features(positions, count, width):
    halfway = width // 2
    rates = 3.0 * jnp.exp(jnp.arange(halfway, dtype=jnp.float32) * (-math.log(count) / halfway))
    angles = positions[:, None] * rates[None, :]
    return jnp.concatenate([jnp.sin(angles), jnp.cos(angles)], axis=1)


def silu_slope(preact):
    logistic = jax.nn.sigmoid(preact)
    return logistic * (1.0 + preact * (1.0 - logistic))


def odd_table(length):
    phase = (2 * np.arange(length)[:, None] + 1) * np.arange(length)[None, :] % (4 * length)
    angles = phase * (2.0 * math.pi / (4 * length))
    return np.concatenate([np.cos(angles), -np.sin(angles)], axis=0)


def halves(table):
    upper = table.astype(jnp.bfloat16)
    lower = (table - upper.astype(np.float64)).astype(jnp.bfloat16)
    return np.concatenate([upper, lower], axis=0)


def spectrum(table, block):
    both = jnp.dot(table, block, preferred_element_type=jnp.float32)
    rows = both.shape[0] // 2
    return both[:rows] + both[rows:]


def conj_product(first, second):
    rows = first.shape[0] // 2
    real_a, imag_a = first[:rows], first[rows:]
    real_b, imag_b = second[:rows], second[rows:]
    return jnp.concatenate(
        [real_a * real_b + imag_a * imag_b, real_a * imag_b - imag_a * real_b], axis=0
    )


def turned(value, sign):
    rows = value.shape[0] // 2
    parity = jnp.where(lax.broadcasted_iota(jnp.int32, (rows, 1), 0) % 2 == 0, sign, -sign)
    return jnp.concatenate([-parity * value[rows:], parity * value[:rows]], axis=0)


def swapped(value):
    count = lax.axis_size("ctx")
    return lax.ppermute(value, "ctx", [(i, i ^ 1) for i in range(count)])


def device_groups():
    count = lax.axis_size("ctx")
    rows = lax.axis_size("dp")
    wide = count // (CORES * Z_HIGH)
    owners = [
        [(x * Z_HIGH + z) * CORES + c for x in range(wide) for c in range(CORES)]
        for z in range(Z_HIGH)
    ]
    runs = [
        [d * count + (x * Z_HIGH + z) * CORES + c for z in range(Z_HIGH) for d in range(rows)]
        for x in range(wide)
        for c in range(CORES)
    ]
    return owners, runs


def repeated(value, count):
    return jnp.broadcast_to(value[None], (count,) + value.shape)


def exchanged(value, axes, groups):
    return lax.all_to_all(
        value, axes, split_axis=0, concat_axis=0, axis_index_groups=groups, tiled=True
    )


def shards(tokens_in, cotangent, lift_weight, lift_bias, coef_weight):
    inputs = tokens_in[0]
    grads = cotangent[0]
    length, channels = inputs.shape
    lags = LAG_BLOCKS * length
    units = lift_weight.shape[1]
    features = lift_weight.shape[0]
    blocks_total = lax.axis_size("ctx")

    core = lax.axis_index("ctx") % CORES
    ahead2 = shifted(grads, "ctx", -CORES)
    behind2 = shifted(inputs, "ctx", CORES)
    near_swap = swapped(jnp.where(core == 0, inputs, grads))
    far_swap = swapped(jnp.where(core == 0, ahead2, behind2))
    ahead1 = jnp.where(core == 0, near_swap, far_swap)
    behind1 = jnp.where(core == 0, far_swap, near_swap)
    later = shifted(jnp.concatenate([ahead1, ahead2], axis=1), "ctx", -CORES)

    table = odd_table(length)
    split = halves(table)
    plain = jnp.asarray(table, jnp.float32)

    positions = jnp.arange(lags, dtype=jnp.int32).astype(jnp.float32)
    embed = lag_features(positions, lags, features)
    preact = jnp.dot(embed, lift_weight, precision=highest) + lift_bias
    hidden = jax.nn.silu(preact)
    slope = silu_slope(preact)
    wide = jnp.concatenate([hidden[k * length:(k + 1) * length] for k in range(LAG_BLOCKS)], axis=1)
    net = jnp.dot(plain, wide, precision=high)
    zero = jnp.zeros((2 * length, units), jnp.float32)
    net = jnp.concatenate([net, zero], axis=1) + turned(jnp.concatenate([zero, net], axis=1), 1.0)
    nets = [net[:, k * units:(k + 1) * units] for k in range(LAG_BLOCKS + 1)]
    coefs = [jnp.dot(part, coef_weight, precision=high) for part in nets]

    near = spectrum(split, jnp.concatenate([grads, inputs], axis=1))
    own_spec, input_spec = near[:, :channels], near[:, channels:]
    far = spectrum(split, jnp.concatenate([ahead1, ahead2, behind1, behind2], axis=1))
    spec1, spec2, back1, back2 = [far[:, k * channels:(k + 1) * channels] for k in range(4)]

    pairs = [
        conj_product(input_spec, own_spec),
        conj_product(input_spec, spec1),
        conj_product(input_spec, spec2),
        conj_product(back1, spec2),
        conj_product(back2, spec2),
    ]
    scale = 1.0 / math.sqrt(lax.axis_size("dp") * length * blocks_total) / length
    tall = jnp.concatenate(pairs, axis=0)
    weight_part = jnp.dot(jnp.concatenate(nets, axis=0).T, tall, precision=high) * scale
    mixed = jnp.dot(tall, coef_weight.T, precision=high)
    rows = 2 * length
    mixes = [mixed[k * rows:(k + 1) * rows] for k in range(LAG_BLOCKS + 1)]
    mixes = jnp.concatenate(
        [mixes[k] + turned(mixes[k + 1], -1.0) for k in range(LAG_BLOCKS)], axis=1
    )
    lag_side = jnp.dot(plain.T, mixes, precision=high)
    lag_side = jnp.concatenate(
        [lag_side[:, k * units:(k + 1) * units] for k in range(LAG_BLOCKS)], axis=0
    )
    preact_part = lag_side * slope * scale
    lift_part = jnp.dot(embed.T, preact_part, precision=high)
    bias_part = jnp.sum(preact_part, axis=0, keepdims=True)

    owners, runs = device_groups()
    shares = len(owners[0])
    depth = coef_weight.shape[0]
    count = channels // units
    sides = jnp.concatenate([weight_part[:, k * units:(k + 1) * units] for k in range(count)], axis=0)
    packed = jnp.concatenate(
        [
            sides.reshape(shares, -1, units),
            lift_part.reshape(shares, -1, units),
            jnp.broadcast_to(bias_part[None], (shares, 8, units)),
        ],
        axis=1,
    )
    split_at = count * depth // shares
    lift_at = split_at + features // shares
    mine = jnp.sum(exchanged(packed, "ctx", owners), axis=0)
    mine = jnp.sum(exchanged(repeated(mine, len(runs[0])), ("dp", "ctx"), runs), axis=0)
    lower = jnp.sum(exchanged(repeated(mine[split_at:], lax.axis_size("ch")), "ch", None), axis=0)
    full = exchanged(repeated(jnp.concatenate([mine[:split_at], lower], axis=0), shares), "ctx", owners)
    sides = full[:, :split_at].reshape(count * depth, units)
    coef_weight_grad = jnp.concatenate([sides[k * depth:(k + 1) * depth] for k in range(count)], axis=1)
    lift_weight_grad = full[:, split_at:lift_at].reshape(features, units)
    lift_bias_grad = full[0, lift_at]

    late = spectrum(split, later)
    specs = [own_spec, spec1, spec2, late[:, :channels], late[:, channels:]]
    total = sum(conj_product(coefs[k], specs[k]) for k in range(LAG_BLOCKS + 1))
    tokens_grad = jnp.dot(plain.T, total, precision=high) * (1.0 / length)
    return (tokens_grad[None], lift_weight_grad, lift_bias_grad, coef_weight_grad)


def solution(mesh):
    in_specs = (P("dp", "ctx", "ch"), P("dp", "ctx", "ch"), P(), P(), P(None, "ch"))
    out_specs = (P("dp", "ctx", "ch"), P(), P(), P(None, "ch"))
    return jax.shard_map(shards, mesh=mesh, in_specs=in_specs, out_specs=out_specs, check_vma=False)
```

```python
import math

import jax
import jax.numpy as jnp
import numpy as np
from jax import lax
from jax.experimental import pallas as pl
from jax.experimental.pallas import tpu as pltpu
from jax.sharding import PartitionSpec as P

LAG_BLOCKS = 4
Z_HIGH = 4
CORES = 2
TILE = 8

highest = lax.Precision.HIGHEST
high = lax.Precision.HIGH


def shifted(value, axis, steps):
    count = lax.axis_size(axis)
    initial, last = (max(0, -steps), min(count, count - steps))
    return lax.ppermute(value, axis, [(source, source + steps) for source in range(initial, last)])


def swapped(value):
    count = lax.axis_size("ctx")
    return lax.ppermute(value, "ctx", [(i, i ^ 1) for i in range(count)])


def lag_features(count, width):
    halfway = width // 2
    rates = np.float32(3.0) * np.exp(np.arange(halfway, dtype=np.float32) * np.float32(-math.log(count) / halfway))
    angles = np.arange(count, dtype=np.float32)[:, None] * rates[None, :].astype(np.float32)
    angles = angles.astype(np.float32).astype(np.float64)
    return np.concatenate([np.sin(angles), np.cos(angles)], axis=1)


def silu_slope(preact):
    logistic = jax.nn.sigmoid(preact)
    return logistic * (1.0 + preact * (1.0 - logistic))


def odd_table(length):
    phase = (2 * np.arange(length)[:, None] + 1) * np.arange(length)[None, :] % (4 * length)
    angles = phase * (2.0 * math.pi / (4 * length))
    return np.concatenate([np.cos(angles), -np.sin(angles)], axis=0)


def halves(table):
    upper = table.astype(jnp.bfloat16)
    lower = (table - upper.astype(np.float64)).astype(jnp.bfloat16)
    return np.concatenate([upper, lower], axis=0)


def turned(value, axis):
    rows = value.shape[axis] // 2
    shape = [1, 1]
    shape[axis] = rows
    parity = jnp.where(lax.broadcasted_iota(jnp.int32, shape, axis) % 2 == 0, 1.0, -1.0)
    real, imag = jnp.split(value, 2, axis=axis)
    return jnp.concatenate([-parity * imag, parity * real], axis=axis)


def device_groups():
    count, rows, lines = lax.axis_size("ctx"), lax.axis_size("dp"), lax.axis_size("ch")
    wide = count // (CORES * Z_HIGH)
    planes = [
        [d * count + (x * Z_HIGH + z) * CORES + c for x in range(wide) for z in range(Z_HIGH) for d in range(rows)]
        for c in range(CORES)
    ]
    columns = [
        [(s * CORES + c) * lines + y for c in range(CORES) for y in range(lines)]
        for s in range(wide * Z_HIGH)
    ]
    return planes, columns


def exchanged(value, axes, groups):
    return lax.all_to_all(
        value, axes, split_axis=0, concat_axis=0, axis_index_groups=groups, tiled=True
    )


def parts(value):
    upper = value.astype(jnp.bfloat16)
    return upper, (value - upper.astype(jnp.float32)).astype(jnp.bfloat16)


def times(first, second):
    return jnp.dot(first, second, preferred_element_type=jnp.float32)


def times_stacked(stacked, second):
    rows = stacked.shape[0] // 2
    upper, lower = parts(second)
    both = times(stacked, upper)
    return both[:rows] + both[rows:] + times(stacked[:rows], lower)


def spectrum(table, block):
    both = times(table, block)
    rows = both.shape[0] // 2
    return both[:rows], both[rows:], rows // 2


def packed_spectrum(table, block):
    upper, lower, rows = spectrum(table, block)
    total = upper + lower
    return total[:rows], total[rows:]


def conj_product(first, second):
    real_a, imag_a = first
    real_b, imag_b = second
    return real_a * real_b + imag_a * imag_b, real_a * imag_b - imag_a * real_b


def lag_kernel(scale, own, lift_rows, c0, c1, c2, x0, x1, x2, split, inverse, embed, net, weight, slope, out):
    units, channels = weight.shape
    length = c0.shape[0]
    table = split[...]
    cots = [packed_spectrum(table, ref[...]) for ref in (c0, c1, c2)]
    ins = [packed_spectrum(table, ref[...]) for ref in (x0, x1, x2)]
    weight_hi, weight_lo = parts(weight[...])
    weights = jnp.concatenate([weight_hi, weight_lo], axis=0)
    last = (((1,), (1,)), ((), ()))
    coef = jnp.zeros((units, channels), jnp.float32)
    mixes = []
    for k, (i, j) in enumerate([(0, 0), (0, 1), (0, 2), (1, 2), (2, 2)]):
        pair = jnp.concatenate(conj_product(ins[i], cots[j]), axis=0)
        upper, lower = parts(pair)
        net_hi, net_lo = parts(net[k * units:(k + 1) * units, :])
        both = times(jnp.concatenate([net_hi, net_lo], axis=0), upper)
        coef = coef + (both[:units] + both[units:] + times(net_hi, lower))
        both = lax.dot_general(upper, weights, last, preferred_element_type=jnp.float32)
        mixes.append(
            both[:, :units]
            + both[:, units:]
            + lax.dot_general(lower, weight_hi, last, preferred_element_type=jnp.float32)
        )
    sides = jnp.concatenate(
        [mixes[k] - turned(mixes[k + 1], 0) for k in range(LAG_BLOCKS)], axis=1
    )
    lagged = times_stacked(inverse[...], sides)
    grads = jnp.concatenate(
        [lagged[:, k * units:(k + 1) * units] for k in range(LAG_BLOCKS)], axis=0
    ) * (slope[...] * scale)
    lift = times_stacked(embed[...], grads)
    bias = jnp.sum(grads, axis=0, keepdims=True)
    owners = out.shape[0]
    coef = coef * scale
    pieces = [coef[:, k * units:(k + 1) * units] for k in range(channels // units)]
    out[:, :own, :] = jnp.concatenate(pieces, axis=0).reshape(owners, own, units)
    used = lift.shape[0] // lift_rows
    out[:used, own:, :] = lift.reshape(used, lift_rows, units)
    out[used, own:, :] = jnp.broadcast_to(bias, (lift_rows, units))
    if used + 1 < owners:
        out[used + 1:, own:, :] = jnp.zeros((owners - used - 1, lift_rows, units), jnp.float32)


def tokens_kernel(c0, c1, c2, later, split, inverse, net, weight, out):
    length, channels = c0.shape
    units = weight.shape[0]
    table = split[...]
    weight_hi, weight_lo = parts(weight[...])
    doubled = jnp.concatenate([weight_hi, weight_hi], axis=0)
    blocks = [c0[...], c1[...], c2[...], later[:, :channels], later[:, channels:]]
    total = None
    for k, block in enumerate(blocks):
        net_hi, net_lo = parts(net[:, k * units:(k + 1) * units])
        coef = times(jnp.concatenate([net_hi, net_lo], axis=1), doubled) + times(net_hi, weight_lo)
        term = conj_product((coef[:length], coef[length:]), packed_spectrum(table, block))
        total = term if total is None else (total[0] + term[0], total[1] + term[1])
    out[...] = times_stacked(inverse[...], jnp.concatenate(total, axis=0)) * (1.0 / length)


def first_sum_kernel(value, out):
    total = jnp.sum(value[...], axis=0)
    out[...] = jnp.broadcast_to(total[None], out.shape)


def second_sum_kernel(own, line, value, out):
    slots = value.shape[0]
    lines = slots // CORES
    place = line[0]
    coef = value[place, :own, :]
    for c in range(1, CORES):
        coef = coef + value[c * lines + place, :own, :]
    rest = jnp.sum(value[:, own:, :], axis=0)
    out[:, :own, :] = jnp.broadcast_to(coef[None], (out.shape[0],) + coef.shape)
    out[:, own:, :] = jnp.broadcast_to(rest[None], (out.shape[0],) + rest.shape)


def unpack_kernel(own, value, coef, lift, bias):
    owners, _, units = value.shape
    depth = coef.shape[0]
    each = depth // own
    for k in range(coef.shape[1] // units):
        coef[:, k * units:(k + 1) * units] = value[k * each:(k + 1) * each, :own, :].reshape(depth, units)
    rows = value.shape[1] - own
    used = lift.shape[0] // rows
    lift[...] = value[:used, own:, :].reshape(lift.shape)
    bias[...] = value[used, own:own + 1, :]


def called(kernel, shapes, *operands, **options):
    return pl.pallas_call(
        kernel,
        out_shape=shapes,
        compiler_params=pltpu.CompilerParams(vmem_limit_bytes=48 * 2 ** 20),
        **options,
    )(*operands)


def shards(tokens_in, cotangent, lift_weight, lift_bias, coef_weight):
    inputs = tokens_in[0]
    grads = cotangent[0]
    length, channels = inputs.shape
    lags = LAG_BLOCKS * length
    features, units = lift_weight.shape
    depth = coef_weight.shape[0]
    blocks_total = lax.axis_size("ctx")

    core = lax.axis_index("ctx") % CORES
    ahead2 = shifted(grads, "ctx", -CORES)
    behind2 = shifted(inputs, "ctx", CORES)
    near_swap = swapped(jnp.where(core == 0, inputs, grads))
    far_swap = swapped(jnp.where(core == 0, ahead2, behind2))
    ahead1 = jnp.where(core == 0, near_swap, far_swap)
    behind1 = jnp.where(core == 0, far_swap, near_swap)

    table = odd_table(length)
    split = jnp.asarray(halves(table))
    inverse = jnp.asarray(halves(table.T))
    plain = jnp.asarray(table, jnp.float32)
    features_table = lag_features(lags, features)
    embed = jnp.asarray(features_table, jnp.float32)
    embed_turned = jnp.asarray(halves(features_table.T))

    preact = jnp.dot(embed, lift_weight, precision=highest) + lift_bias
    hidden = jax.nn.silu(preact)
    slope = silu_slope(preact)
    wide = jnp.concatenate([hidden[k * length:(k + 1) * length] for k in range(LAG_BLOCKS)], axis=1)
    net = jnp.dot(plain, wide, precision=high)
    zero = jnp.zeros((2 * length, units), jnp.float32)
    net = jnp.concatenate([net, zero], axis=1) + turned(jnp.concatenate([zero, net], axis=1), 0)
    net_turned = lax.dot_general(wide, plain, (((0,), (1,)), ((), ())), precision=high)
    net_turned = jnp.concatenate([net_turned, zero.T], axis=0) + turned(
        jnp.concatenate([zero.T, net_turned], axis=0), 1
    )

    planes, columns = device_groups()
    owners, slots = len(planes[0]), len(columns[0])
    own = channels // units * depth // owners
    lift_rows = TILE * 2 ** max(0, math.ceil(math.log2((features + TILE) / (TILE * owners))))
    scale = 1.0 / math.sqrt(lax.axis_size("dp") * length * blocks_total) / length

    def rows_of(count):
        return jax.ShapeDtypeStruct((count, own + lift_rows, units), jnp.float32)

    packed = called(
        lambda *refs: lag_kernel(scale, own, lift_rows, *refs),
        rows_of(owners),
        grads, ahead1, ahead2, inputs, behind1, behind2,
        split, inverse, embed_turned, net_turned, coef_weight, slope,
    )
    summed = exchanged(packed, ("dp", "ctx"), planes)
    both = jnp.concatenate([ahead1, ahead2], axis=1)
    summed, both = lax.optimization_barrier((summed, both))
    later = shifted(both, "ctx", -CORES)
    summed = exchanged(called(first_sum_kernel, rows_of(slots), summed), ("ctx", "ch"), columns)
    line = lax.axis_index("ch").astype(jnp.int32).reshape(1)
    spread = called(
        lambda *refs: second_sum_kernel(own, *refs),
        rows_of(owners),
        line, summed,
        in_specs=[pl.BlockSpec(memory_space=pltpu.SMEM), pl.BlockSpec(memory_space=pltpu.VMEM)],
    )
    full = exchanged(spread, ("dp", "ctx"), planes)
    coef_weight_grad, lift_weight_grad, lift_bias_grad = called(
        lambda *refs: unpack_kernel(own, *refs),
        (
            jax.ShapeDtypeStruct((depth, channels), jnp.float32),
            jax.ShapeDtypeStruct((features, units), jnp.float32),
            jax.ShapeDtypeStruct((1, units), jnp.float32),
        ),
        full,
    )
    tokens_grad = called(
        tokens_kernel,
        jax.ShapeDtypeStruct((length, channels), jnp.float32),
        grads, ahead1, ahead2, later, split, inverse, net, coef_weight,
    )
    return (tokens_grad[None], lift_weight_grad, lift_bias_grad[0], coef_weight_grad)


def solution(mesh):
    in_specs = (P("dp", "ctx", "ch"), P("dp", "ctx", "ch"), P(), P(), P(None, "ch"))
    out_specs = (P("dp", "ctx", "ch"), P(), P(), P(None, "ch"))
    return jax.shard_map(shards, mesh=mesh, in_specs=in_specs, out_specs=out_specs, check_vma=False)
```

```python
import math

import jax
import jax.numpy as jnp
import numpy as np
from jax import lax
from jax.experimental import pallas as pl
from jax.experimental.pallas import tpu as pltpu
from jax.sharding import PartitionSpec as P

LAG_BLOCKS = 4
Z_HIGH = 4
CORES = 2
TILE = 8

highest = lax.Precision.HIGHEST


def shifted(value, axis, steps):
    count = lax.axis_size(axis)
    initial, last = (max(0, -steps), min(count, count - steps))
    return lax.ppermute(value, axis, [(source, source + steps) for source in range(initial, last)])


def swapped(value):
    count = lax.axis_size("ctx")
    return lax.ppermute(value, "ctx", [(i, i ^ 1) for i in range(count)])


def lag_features(count, width):
    halfway = width // 2
    rates = np.float32(3.0) * np.exp(np.arange(halfway, dtype=np.float32) * np.float32(-math.log(count) / halfway))
    angles = np.arange(count, dtype=np.float32)[:, None] * rates[None, :].astype(np.float32)
    angles = angles.astype(np.float32).astype(np.float64)
    return np.concatenate([np.sin(angles), np.cos(angles)], axis=1)


def odd_table(length):
    phase = (2 * np.arange(length)[:, None] + 1) * np.arange(length)[None, :] % (4 * length)
    angles = phase * (2.0 * math.pi / (4 * length))
    return np.concatenate([np.cos(angles), -np.sin(angles)], axis=0)


def halves(table):
    upper = table.astype(jnp.bfloat16)
    lower = (table - upper.astype(np.float64)).astype(jnp.bfloat16)
    return np.concatenate([upper, lower], axis=0)


def turned(value, axis):
    rows = value.shape[axis] // 2
    shape = [1, 1]
    shape[axis] = rows
    parity = jnp.where(lax.broadcasted_iota(jnp.int32, shape, axis) % 2 == 0, 1.0, -1.0)
    real, imag = jnp.split(value, 2, axis=axis)
    return jnp.concatenate([-parity * imag, parity * real], axis=axis)


def device_groups():
    count, rows, lines = lax.axis_size("ctx"), lax.axis_size("dp"), lax.axis_size("ch")
    wide = count // (CORES * Z_HIGH)
    planes = [
        [d * count + (x * Z_HIGH + z) * CORES + c for x in range(wide) for z in range(Z_HIGH) for d in range(rows)]
        for c in range(CORES)
    ]
    columns = [
        [(s * CORES + c) * lines + y for c in range(CORES) for y in range(lines)]
        for s in range(wide * Z_HIGH)
    ]
    return planes, columns


def exchanged(value, axes, groups):
    return lax.all_to_all(
        value, axes, split_axis=0, concat_axis=0, axis_index_groups=groups, tiled=True
    )


def parts(value):
    upper = value.astype(jnp.bfloat16)
    return upper, (value - upper.astype(jnp.float32)).astype(jnp.bfloat16)


def times(first, second):
    return jnp.dot(first, second, preferred_element_type=jnp.float32)


def times_stacked(stacked, second):
    rows = stacked.shape[0] // 2
    upper, lower = parts(second)
    both = times(stacked, upper)
    return both[:rows] + both[rows:] + times(stacked[:rows], lower)


def spectrum(table, block):
    both = times(table, block)
    rows = both.shape[0] // 2
    return both[:rows], both[rows:], rows // 2


def packed_spectrum(table, block):
    upper, lower, rows = spectrum(table, block)
    total = upper + lower
    return total[:rows], total[rows:]


def conj_product(first, second):
    real_a, imag_a = first
    real_b, imag_b = second
    return real_a * real_b + imag_a * imag_b, real_a * imag_b - imag_a * real_b


def network_kernel(embed, lift_weight, lift_bias, inverse, net, slope):
    units = lift_weight.shape[1]
    length = inverse.shape[0] // 2
    preact = jnp.dot(
        embed[...], lift_weight[...], precision=highest, preferred_element_type=jnp.float32
    ) + lift_bias[...]
    logistic = jax.nn.sigmoid(preact)
    hidden = preact * logistic
    slope[...] = logistic * (1.0 + preact * (1.0 - logistic))
    rows = jnp.concatenate(
        [hidden[k * length:(k + 1) * length].T for k in range(LAG_BLOCKS)], axis=0
    )
    upper, lower = parts(rows)
    count = rows.shape[0]
    both = times(jnp.concatenate([upper, lower], axis=0), inverse[:length, :])
    plain = both[:count] + both[count:] + times(upper, inverse[length:, :])
    moved = turned(plain, 1)
    net[:units, :] = plain[:units]
    net[units:count, :] = plain[units:] + moved[:-units]
    net[count:, :] = moved[-units:]


def chosen(first, core, one, other):
    return tuple(jnp.where(core == first, a, b) for a, b in zip(one, other))


def lag_kernel(scale, own, lift_rows, core_ref, c0, near, c2, far, x0, x2, split, inverse, embed, net, weight, slope, out):
    units, channels = weight.shape
    table = split[...]
    core = core_ref[0]
    own_spec, near_spec, ahead_spec, far_spec, in_spec, back_spec = [
        packed_spectrum(table, ref[...]) for ref in (c0, near, c2, far, x0, x2)
    ]
    products = [
        (in_spec, own_spec),
        (in_spec, chosen(0, core, near_spec, far_spec)),
        (in_spec, ahead_spec),
        (chosen(0, core, in_spec, back_spec), far_spec),
        (back_spec, ahead_spec),
    ]
    weight_hi, weight_lo = parts(weight[...])
    weights = jnp.concatenate([weight_hi, weight_lo], axis=0)
    last = (((1,), (1,)), ((), ()))
    coef = jnp.zeros((units, channels), jnp.float32)
    mixes = []
    for k, (first, second) in enumerate(products):
        pair = jnp.concatenate(conj_product(first, second), axis=0)
        upper, lower = parts(pair)
        net_hi, net_lo = parts(net[k * units:(k + 1) * units, :])
        both = times(jnp.concatenate([net_hi, net_lo], axis=0), upper)
        coef = coef + (both[:units] + both[units:] + times(net_hi, lower))
        both = lax.dot_general(upper, weights, last, preferred_element_type=jnp.float32)
        mixes.append(
            both[:, :units]
            + both[:, units:]
            + lax.dot_general(lower, weight_hi, last, preferred_element_type=jnp.float32)
        )
    sides = jnp.concatenate(
        [mixes[k] - turned(mixes[k + 1], 0) for k in range(LAG_BLOCKS)], axis=1
    )
    lagged = times_stacked(inverse[...], sides)
    grads = jnp.concatenate(
        [lagged[:, k * units:(k + 1) * units] for k in range(LAG_BLOCKS)], axis=0
    ) * (slope[...] * scale)
    lift = times_stacked(embed[...], grads)
    bias = jnp.sum(grads, axis=0, keepdims=True)
    owners = out.shape[0]
    coef = coef * scale
    pieces = [coef[:, k * units:(k + 1) * units] for k in range(channels // units)]
    out[:, :own, :] = jnp.concatenate(pieces, axis=0).reshape(owners, own, units)
    used = lift.shape[0] // lift_rows
    out[:used, own:, :] = lift.reshape(used, lift_rows, units)
    out[used, own:, :] = jnp.broadcast_to(bias, (lift_rows, units))
    if used + 1 < owners:
        out[used + 1:, own:, :] = jnp.zeros((owners - used - 1, lift_rows, units), jnp.float32)


def tokens_kernel(core_ref, c0, near, c2, far, swap, c4, split, inverse, net, weight, out):
    length, channels = c0.shape
    units = weight.shape[0]
    table = split[...]
    core = core_ref[0]
    weight_hi, weight_lo = parts(weight[...])
    doubled = jnp.concatenate([weight_hi, weight_hi], axis=0)
    own_spec, near_spec, ahead_spec, far_spec, swap_spec, last_spec = [
        packed_spectrum(table, ref[...]) for ref in (c0, near, c2, far, swap, c4)
    ]
    specs = [
        own_spec,
        chosen(0, core, near_spec, far_spec),
        ahead_spec,
        chosen(0, core, far_spec, swap_spec),
        last_spec,
    ]
    total = None
    for k, spec in enumerate(specs):
        net_hi, net_lo = parts(net[k * units:(k + 1) * units, :].T)
        coef = times(jnp.concatenate([net_hi, net_lo], axis=1), doubled) + times(net_hi, weight_lo)
        term = conj_product((coef[:length], coef[length:]), spec)
        total = term if total is None else (total[0] + term[0], total[1] + term[1])
    out[...] = times_stacked(inverse[...], jnp.concatenate(total, axis=0)) * (1.0 / length)


def first_sum_kernel(value, block, out, same):
    total = jnp.sum(value[...], axis=0)
    out[...] = jnp.broadcast_to(total[None], out.shape)
    same[...] = block[...]


def second_sum_kernel(own, line, value, relayed, out):
    slots = value.shape[0]
    lines = slots // CORES
    place = line[0]
    coef = value[place, :own, :]
    for c in range(1, CORES):
        coef = coef + value[c * lines + place, :own, :]
    rest = jnp.sum(value[:, own:, :], axis=0)
    out[:, :own, :] = jnp.broadcast_to(coef[None], (out.shape[0],) + coef.shape)
    out[:, own:, :] = jnp.broadcast_to(rest[None], (out.shape[0],) + rest.shape)


def unpack_kernel(own, value, coef, lift, bias):
    owners, _, units = value.shape
    depth = coef.shape[0]
    each = depth // own
    for k in range(coef.shape[1] // units):
        coef[:, k * units:(k + 1) * units] = value[k * each:(k + 1) * each, :own, :].reshape(depth, units)
    rows = value.shape[1] - own
    used = lift.shape[0] // rows
    lift[...] = value[:used, own:, :].reshape(lift.shape)
    bias[...] = value[used, own:own + 1, :]


def called(kernel, shapes, *operands, **options):
    return pl.pallas_call(
        kernel,
        out_shape=shapes,
        compiler_params=pltpu.CompilerParams(vmem_limit_bytes=48 * 2 ** 20),
        **options,
    )(*operands)


def shards(tokens_in, cotangent, lift_weight, lift_bias, coef_weight):
    inputs = tokens_in[0]
    grads = cotangent[0]
    length, channels = inputs.shape
    lags = LAG_BLOCKS * length
    features, units = lift_weight.shape
    depth = coef_weight.shape[0]
    blocks_total = lax.axis_size("ctx")

    core = (lax.axis_index("ctx") % CORES).astype(jnp.int32).reshape(1)
    ahead2 = shifted(grads, "ctx", -CORES)
    behind2 = shifted(inputs, "ctx", CORES)
    near = swapped(grads)
    far = swapped(ahead2)

    table = odd_table(length)
    split = jnp.asarray(halves(table))
    inverse = jnp.asarray(halves(table.T))
    features_table = lag_features(lags, features)
    embed = jnp.asarray(features_table, jnp.float32)
    embed_turned = jnp.asarray(halves(features_table.T))
    net, slope = called(
        network_kernel,
        (
            jax.ShapeDtypeStruct(((LAG_BLOCKS + 1) * units, 2 * length), jnp.float32),
            jax.ShapeDtypeStruct((lags, units), jnp.float32),
        ),
        embed, lift_weight, lift_bias[None], inverse,
    )

    planes, columns = device_groups()
    owners, slots = len(planes[0]), len(columns[0])
    own = channels // units * depth // owners
    lift_rows = TILE * 2 ** max(0, math.ceil(math.log2((features + TILE) / (TILE * owners))))
    scale = 1.0 / math.sqrt(lax.axis_size("dp") * length * blocks_total) / length

    def rows_of(count):
        return jax.ShapeDtypeStruct((count, own + lift_rows, units), jnp.float32)

    scalar = pl.BlockSpec(memory_space=pltpu.SMEM)
    whole = pl.BlockSpec(memory_space=pltpu.VMEM)
    packed = called(
        lambda *refs: lag_kernel(scale, own, lift_rows, *refs),
        rows_of(owners),
        core, grads, near, ahead2, far, inputs, behind2,
        split, inverse, embed_turned, net, coef_weight, slope,
        in_specs=[scalar] + [whole] * 12,
    )
    summed = exchanged(packed, ("dp", "ctx"), planes)
    summed, ahead2 = called(
        first_sum_kernel,
        (rows_of(slots), jax.ShapeDtypeStruct(ahead2.shape, ahead2.dtype)),
        summed, ahead2,
    )
    last = shifted(ahead2, "ctx", -CORES)
    summed = exchanged(summed, ("ctx", "ch"), columns)
    line = lax.axis_index("ch").astype(jnp.int32).reshape(1)
    spread = called(
        lambda *refs: second_sum_kernel(own, *refs),
        rows_of(owners),
        line, summed, last,
        in_specs=[scalar, whole, pl.BlockSpec(memory_space=pl.ANY)],
    )
    swap = swapped(last)
    full = exchanged(spread, ("dp", "ctx"), planes)
    coef_weight_grad, lift_weight_grad, lift_bias_grad = called(
        lambda *refs: unpack_kernel(own, *refs),
        (
            jax.ShapeDtypeStruct((depth, channels), jnp.float32),
            jax.ShapeDtypeStruct((features, units), jnp.float32),
            jax.ShapeDtypeStruct((1, units), jnp.float32),
        ),
        full,
    )
    tokens_grad = called(
        tokens_kernel,
        jax.ShapeDtypeStruct((length, channels), jnp.float32),
        core, grads, near, ahead2, far, swap, last, split, inverse, net, coef_weight,
        in_specs=[scalar] + [whole] * 10,
    )
    return (tokens_grad[None], lift_weight_grad, lift_bias_grad[0], coef_weight_grad)


def solution(mesh):
    in_specs = (P("dp", "ctx", "ch"), P("dp", "ctx", "ch"), P(), P(), P(None, "ch"))
    out_specs = (P("dp", "ctx", "ch"), P(), P(), P(None, "ch"))
    return jax.shard_map(shards, mesh=mesh, in_specs=in_specs, out_specs=out_specs, check_vma=False)
```

```python
import math

import jax
import jax.numpy as jnp
import numpy as np
from jax import lax
from jax.experimental import pallas as pl
from jax.experimental.pallas import tpu as pltpu
from jax.sharding import PartitionSpec as P

LAG_BLOCKS = 4
Z_HIGH = 4
CORES = 2
TILE = 8

highest = lax.Precision.HIGHEST


def shifted(value, axis, steps):
    count = lax.axis_size(axis)
    initial, last = (max(0, -steps), min(count, count - steps))
    return lax.ppermute(value, axis, [(source, source + steps) for source in range(initial, last)])


def swapped(value):
    count = lax.axis_size("ctx")
    return lax.ppermute(value, "ctx", [(i, i ^ 1) for i in range(count)])


def lag_features(count, width):
    halfway = width // 2
    rates = np.float32(3.0) * np.exp(np.arange(halfway, dtype=np.float32) * np.float32(-math.log(count) / halfway))
    angles = np.arange(count, dtype=np.float32)[:, None] * rates[None, :].astype(np.float32)
    angles = angles.astype(np.float32).astype(np.float64)
    return np.concatenate([np.sin(angles), np.cos(angles)], axis=1)


def odd_table(length):
    phase = (2 * np.arange(length)[:, None] + 1) * np.arange(length)[None, :] % (4 * length)
    angles = phase * (2.0 * math.pi / (4 * length))
    return np.concatenate([np.cos(angles), -np.sin(angles)], axis=0)


def halves(table):
    upper = table.astype(jnp.bfloat16)
    lower = (table - upper.astype(np.float64)).astype(jnp.bfloat16)
    return np.concatenate([upper, lower], axis=0)


def turned(value, axis):
    rows = value.shape[axis] // 2
    shape = [1, 1]
    shape[axis] = rows
    parity = jnp.where(lax.broadcasted_iota(jnp.int32, shape, axis) % 2 == 0, 1.0, -1.0)
    real, imag = jnp.split(value, 2, axis=axis)
    return jnp.concatenate([-parity * imag, parity * real], axis=axis)


def device_groups():
    count, rows, lines = lax.axis_size("ctx"), lax.axis_size("dp"), lax.axis_size("ch")
    wide = count // (CORES * Z_HIGH)
    planes = [
        [d * count + (x * Z_HIGH + z) * CORES + c for x in range(wide) for z in range(Z_HIGH) for d in range(rows)]
        for c in range(CORES)
    ]
    columns = [
        [(s * CORES + c) * lines + y for c in range(CORES) for y in range(lines)]
        for s in range(wide * Z_HIGH)
    ]
    return planes, columns


def exchanged(value, axes, groups):
    return lax.all_to_all(
        value, axes, split_axis=0, concat_axis=0, axis_index_groups=groups, tiled=True
    )


def parts(value):
    upper = value.astype(jnp.bfloat16)
    return upper, (value - upper.astype(jnp.float32)).astype(jnp.bfloat16)


def times(first, second):
    return jnp.dot(first, second, preferred_element_type=jnp.float32)


def times_stacked(stacked, second):
    rows = stacked.shape[0] // 2
    upper, lower = parts(second)
    both = times(stacked, upper)
    return both[:rows] + both[rows:] + times(stacked[:rows], lower)


def spectrum(table, block):
    both = times(table, block)
    rows = both.shape[0] // 2
    return both[:rows], both[rows:], rows // 2


def packed_spectrum(table, block):
    upper, lower, rows = spectrum(table, block)
    total = upper + lower
    return total[:rows], total[rows:]


def conj_product(first, second):
    real_a, imag_a = first
    real_b, imag_b = second
    return real_a * real_b + imag_a * imag_b, real_a * imag_b - imag_a * real_b


def pair_products(first, second, net, weight):
    units = weight.shape[0]
    pair = jnp.concatenate(conj_product(first, second), axis=0)
    upper, lower = parts(pair)
    net_hi, net_lo = parts(net)
    both = times(jnp.concatenate([net_hi, net_lo], axis=0), upper)
    coef = both[:units] + both[units:] + times(net_hi, lower)
    weight_hi, weight_lo = parts(weight)
    last = (((1,), (1,)), ((), ()))
    both = lax.dot_general(
        upper, jnp.concatenate([weight_hi, weight_lo], axis=0), last, preferred_element_type=jnp.float32
    )
    mix = both[:, :units] + both[:, units:] + lax.dot_general(
        lower, weight_hi, last, preferred_element_type=jnp.float32
    )
    return coef, mix


def started(sems, pairs):
    copies = [
        pltpu.make_async_copy(source, target, sems.at[i]) for i, (source, target) in enumerate(pairs)
    ]
    for copy in copies:
        copy.start()
    return copies


def prepare_kernel(
    embed_in, lift_weight_in, lift_bias_in, inverse_in, split_in, c0_in, x0_in, weight_in,
    net, slope, coef, mix,
    embed, lift_weight, lift_bias, inverse, split, c0, x0, weight, sems,
):
    copies = started(
        sems,
        [
            (embed_in, embed), (lift_weight_in, lift_weight), (lift_bias_in, lift_bias),
            (inverse_in, inverse), (split_in, split), (c0_in, c0), (x0_in, x0), (weight_in, weight),
        ],
    )
    units = lift_weight.shape[1]
    length = inverse.shape[0] // 2
    for copy in copies[:3]:
        copy.wait()
    preact = jnp.dot(
        embed[...], lift_weight[...], precision=highest, preferred_element_type=jnp.float32
    ) + lift_bias[...]
    logistic = jax.nn.sigmoid(preact)
    hidden = preact * logistic
    slope[...] = logistic * (1.0 + preact * (1.0 - logistic))
    rows = jnp.concatenate(
        [hidden[k * length:(k + 1) * length].T for k in range(LAG_BLOCKS)], axis=0
    )
    upper, lower = parts(rows)
    count = rows.shape[0]
    copies[3].wait()
    both = times(jnp.concatenate([upper, lower], axis=0), inverse[:length, :])
    plain = both[:count] + both[count:] + times(upper, inverse[length:, :])
    moved = turned(plain, 1)
    net[:units, :] = plain[:units]
    net[units:count, :] = plain[units:] + moved[:-units]
    net[count:, :] = moved[-units:]
    for copy in copies[4:]:
        copy.wait()
    own = packed_spectrum(split[...], c0[...])
    source = packed_spectrum(split[...], x0[...])
    coef[...], mix[...] = pair_products(source, own, plain[:units], weight[...])


def join_kernel(c0, c2, tokens, net, out, sems):
    length = c0.shape[0]
    for copy in started(sems, [(c0, out.at[pl.ds(0, length)]), (c2, out.at[pl.ds(length, length)])]):
        copy.wait()


def chosen(core, one, other):
    return tuple(jnp.where(core == 0, a, b) for a, b in zip(one, other))


def halved(ref):
    rows = ref.shape[0] // 2
    return ref[:rows, :], ref[rows:, :]


def lag_kernel(
    scale, own, lift_rows,
    core_ref, c2, swaps, x2, first_coef, first_mix, net, slope,
    x0_in, split_in, weight_in, inverse_in, embed_in, out, same,
    x0, split, weight, inverse, embed, packed, sems,
):
    copies = started(
        sems,
        [
            (split_in, split), (x0_in, x0), (weight_in, weight), (inverse_in, inverse), (embed_in, embed),
            (c2, same),
        ],
    )
    units, channels = weight.shape
    length = c2.shape[0]
    core = core_ref[0]
    copies[0].wait()
    table = split[...]
    near_spec, far_spec, ahead_spec, back_spec = [
        packed_spectrum(table, block) for block in (swaps[:length, :], swaps[length:, :], c2[...], x2[...])
    ]
    for copy in copies[1:]:
        copy.wait()
    in_spec = packed_spectrum(table, x0[...])
    products = [
        (in_spec, chosen(core, near_spec, far_spec)),
        (in_spec, ahead_spec),
        (chosen(core, in_spec, back_spec), far_spec),
        (back_spec, ahead_spec),
    ]
    coef = first_coef[...]
    mixes = [first_mix[...]]
    for k, (first, second) in enumerate(products, 1):
        part, mix = pair_products(first, second, net[k * units:(k + 1) * units, :], weight[...])
        coef = coef + part
        mixes.append(mix)
    sides = jnp.concatenate(
        [mixes[k] - turned(mixes[k + 1], 0) for k in range(LAG_BLOCKS)], axis=1
    )
    lagged = times_stacked(inverse[...], sides)
    grads = jnp.concatenate(
        [lagged[:, k * units:(k + 1) * units] for k in range(LAG_BLOCKS)], axis=0
    ) * (slope[...] * scale)
    lift = times_stacked(embed[...], grads)
    bias = jnp.sum(grads, axis=0, keepdims=True)
    owners = packed.shape[0]
    coef = coef * scale
    pieces = [coef[:, k * units:(k + 1) * units] for k in range(channels // units)]
    packed[:, :own, :] = jnp.concatenate(pieces, axis=0).reshape(owners, own, units)
    used = lift.shape[0] // lift_rows
    packed[:used, own:, :] = lift.reshape(used, lift_rows, units)
    packed[used, own:, :] = jnp.broadcast_to(bias, (lift_rows, units))
    if used + 1 < owners:
        packed[used + 1:, own:, :] = jnp.zeros((owners - used - 1, lift_rows, units), jnp.float32)
    copy = pltpu.make_async_copy(packed, out, sems.at[len(copies)])
    copy.start()
    copy.wait()


def early_tokens_kernel(
    core_ref, swaps, net, c0_in, c2_in, split_in, weight_in, out, coefs_out,
    c0, c2, split, weight, total_kept, coefs, sems,
):
    copies = started(sems, [(split_in, split), (c0_in, c0), (c2_in, c2), (weight_in, weight)])
    length = c2.shape[0]
    units = weight.shape[0]
    core = core_ref[0]
    for copy in copies:
        copy.wait()
    table = split[...]
    weight_hi, weight_lo = parts(weight[...])
    doubled = jnp.concatenate([weight_hi, weight_hi], axis=0)
    own_spec, near_spec, far_spec, ahead_spec = [
        packed_spectrum(table, block) for block in (c0[...], swaps[:length, :], swaps[length:, :], c2[...])
    ]
    specs = [own_spec, chosen(core, near_spec, far_spec), ahead_spec, far_spec]
    total = None
    for k in range(LAG_BLOCKS + 1):
        net_hi, net_lo = parts(net[k * units:(k + 1) * units, :].T)
        coef = times(jnp.concatenate([net_hi, net_lo], axis=1), doubled) + times(net_hi, weight_lo)
        if k >= LAG_BLOCKS - 1:
            coefs[k - LAG_BLOCKS + 1] = coef
        if k == LAG_BLOCKS:
            break
        term = conj_product((coef[:length], coef[length:]), specs[k])
        if k == LAG_BLOCKS - 1:
            term = chosen(core, term, (jnp.zeros_like(term[0]), jnp.zeros_like(term[1])))
        total = term if total is None else (total[0] + term[0], total[1] + term[1])
    total_kept[...] = jnp.concatenate(total, axis=0)
    copies = [
        pltpu.make_async_copy(total_kept, out, sems.at[0]),
        pltpu.make_async_copy(coefs, coefs_out, sems.at[1]),
    ]
    for copy in copies:
        copy.start()
    for copy in copies:
        copy.wait()


def late_tokens_kernel(
    core_ref, swap, last, early_in, coefs_in, split_in, inverse_in, out, early, coefs, split, inverse, sems
):
    copies = started(
        sems, [(split_in, split), (coefs_in, coefs), (early_in, early), (inverse_in, inverse)]
    )
    core = core_ref[0]
    for copy in copies:
        copy.wait()
    table = split[...]
    swap_term = conj_product(halved(coefs.at[0]), packed_spectrum(table, swap[...]))
    last_term = conj_product(halved(coefs.at[1]), packed_spectrum(table, last[...]))
    swap_term = chosen(core, (jnp.zeros_like(swap_term[0]), jnp.zeros_like(swap_term[1])), swap_term)
    total = [a + b + c for a, b, c in zip(halved(early), swap_term, last_term)]
    length = swap.shape[0]
    out[...] = times_stacked(inverse[...], jnp.concatenate(total, axis=0)) * (1.0 / length)


def first_sum_kernel(value, block, early, out, same, sems):
    copies = started(sems, [(block, same)])
    total = jnp.sum(value[...], axis=0)
    out[...] = jnp.broadcast_to(total[None], out.shape)
    copies[0].wait()


def second_sum_kernel(own, line, value, relayed, out):
    slots = value.shape[0]
    lines = slots // CORES
    place = line[0]
    coef = value[place, :own, :]
    for c in range(1, CORES):
        coef = coef + value[c * lines + place, :own, :]
    rest = jnp.sum(value[:, own:, :], axis=0)
    out[:, :own, :] = jnp.broadcast_to(coef[None], (out.shape[0],) + coef.shape)
    out[:, own:, :] = jnp.broadcast_to(rest[None], (out.shape[0],) + rest.shape)


def unpack_kernel(own, value, coef, lift, bias):
    owners, _, units = value.shape
    depth = coef.shape[0]
    each = depth // own
    for k in range(coef.shape[1] // units):
        coef[:, k * units:(k + 1) * units] = value[k * each:(k + 1) * each, :own, :].reshape(depth, units)
    rows = value.shape[1] - own
    used = lift.shape[0] // rows
    lift[...] = value[:used, own:, :].reshape(lift.shape)
    bias[...] = value[used, own:own + 1, :]


def called(kernel, mebibytes, shapes, *operands, **options):
    return pl.pallas_call(
        kernel,
        out_shape=shapes,
        compiler_params=pltpu.CompilerParams(vmem_limit_bytes=mebibytes * 2 ** 20),
        **options,
    )(*operands)


def shards(tokens_in, cotangent, lift_weight, lift_bias, coef_weight):
    inputs = tokens_in[0]
    grads = cotangent[0]
    length, channels = inputs.shape
    lags = LAG_BLOCKS * length
    features, units = lift_weight.shape
    depth = coef_weight.shape[0]
    blocks_total = lax.axis_size("ctx")

    core = (lax.axis_index("ctx") % CORES).astype(jnp.int32).reshape(1)
    ahead2 = shifted(grads, "ctx", -CORES)
    behind2 = shifted(inputs, "ctx", CORES)

    def real(*shape):
        return jax.ShapeDtypeStruct(shape, jnp.float32)

    def like(value):
        return jax.ShapeDtypeStruct(value.shape, value.dtype)

    scalar = pl.BlockSpec(memory_space=pltpu.SMEM)
    whole = pl.BlockSpec(memory_space=pltpu.VMEM)
    table = odd_table(length)
    split = jnp.asarray(halves(table))
    inverse = jnp.asarray(halves(table.T))
    features_table = lag_features(lags, features)
    embed = jnp.asarray(features_table, jnp.float32)
    embed_turned = jnp.asarray(halves(features_table.T))

    def held(value):
        return pltpu.with_memory_space_constraint(value, pltpu.HBM)

    def room(value):
        return pltpu.VMEM(value.shape, value.dtype)

    def sems(count):
        return pltpu.SemaphoreType.DMA((count,))

    far_off = pl.BlockSpec(memory_space=pltpu.HBM)
    either = pl.BlockSpec(memory_space=pl.ANY)
    bias_row = lift_bias[None]
    first_operands = (embed, lift_weight, bias_row, inverse, split, grads, inputs, coef_weight)
    net, slope, coef, mix = called(
        prepare_kernel,
        24,
        (
            real((LAG_BLOCKS + 1) * units, 2 * length),
            real(lags, units),
            real(depth, channels),
            real(2 * length, units),
        ),
        *[held(value) for value in first_operands],
        in_specs=[far_off] * 8,
        scratch_shapes=[room(value) for value in first_operands] + [sems(8)],
    )
    joined = called(
        join_kernel, 8, jax.ShapeDtypeStruct((2 * length, channels), grads.dtype),
        held(grads), ahead2, behind2, net,
        in_specs=[far_off] + [either] * 3,
        out_specs=either,
        scratch_shapes=[sems(2)],
    )
    swaps = swapped(joined)

    planes, columns = device_groups()
    owners, slots = len(planes[0]), len(columns[0])
    own = channels // units * depth // owners
    lift_rows = TILE * 2 ** max(0, math.ceil(math.log2((features + TILE) / (TILE * owners))))
    scale = 1.0 / math.sqrt(lax.axis_size("dp") * length * blocks_total) / length

    def rows_of(count):
        return real(count, own + lift_rows, units)

    packed, ahead2 = called(
        lambda *refs: lag_kernel(scale, own, lift_rows, *refs),
        32,
        (pltpu.HBM((owners, own + lift_rows, units), jnp.float32), pltpu.HBM(ahead2.shape, ahead2.dtype)),
        core, ahead2, swaps, behind2, coef, mix, net, slope,
        *[held(value) for value in (inputs, split, coef_weight, inverse, embed_turned)],
        in_specs=[scalar] + [whole] * 7 + [far_off] * 5,
        out_specs=[far_off] * 2,
        scratch_shapes=[room(value) for value in (inputs, split, coef_weight, inverse, embed_turned)]
        + [pltpu.VMEM((owners, own + lift_rows, units), jnp.float32), sems(7)],
    )
    summed = exchanged(packed, ("dp", "ctx"), planes)
    kept = ((2 * length, channels), (2, 2 * length, channels))
    early, coefs = called(
        early_tokens_kernel,
        24,
        tuple(pltpu.HBM(shape, jnp.float32) for shape in kept),
        core, swaps, net,
        *[held(value) for value in (grads, ahead2, split, coef_weight)],
        in_specs=[scalar] + [whole] * 2 + [far_off] * 4,
        out_specs=[far_off] * 2,
        scratch_shapes=[room(value) for value in (grads, ahead2, split, coef_weight)]
        + [pltpu.VMEM(shape, jnp.float32) for shape in kept]
        + [sems(4)],
    )
    summed, ahead2 = called(
        first_sum_kernel,
        8,
        (rows_of(slots), pltpu.HBM(ahead2.shape, ahead2.dtype)),
        summed, held(ahead2), held(early),
        in_specs=[whole, far_off, far_off],
        out_specs=[whole, far_off],
        scratch_shapes=[sems(1)],
    )
    last = shifted(ahead2, "ctx", -CORES)
    summed = exchanged(summed, ("ctx", "ch"), columns)
    line = lax.axis_index("ch").astype(jnp.int32).reshape(1)
    spread = called(
        lambda *refs: second_sum_kernel(own, *refs),
        8,
        rows_of(owners),
        line, summed, last,
        in_specs=[scalar, whole, either],
    )
    swap = swapped(last)
    full = exchanged(spread, ("dp", "ctx"), planes)
    coef_weight_grad, lift_weight_grad, lift_bias_grad = called(
        lambda *refs: unpack_kernel(own, *refs),
        8,
        (
            jax.ShapeDtypeStruct((depth, channels), jnp.float32),
            jax.ShapeDtypeStruct((features, units), jnp.float32),
            jax.ShapeDtypeStruct((1, units), jnp.float32),
        ),
        full,
    )
    tokens_grad = called(
        late_tokens_kernel,
        16,
        real(length, channels),
        core, swap, last,
        *[held(value) for value in (early, coefs, split, inverse)],
        in_specs=[scalar] + [whole] * 2 + [far_off] * 4,
        scratch_shapes=[room(value) for value in (early, coefs, split, inverse)] + [sems(4)],
    )
    return (tokens_grad[None], lift_weight_grad, lift_bias_grad[0], coef_weight_grad)


def solution(mesh):
    in_specs = (P("dp", "ctx", "ch"), P("dp", "ctx", "ch"), P(), P(), P(None, "ch"))
    out_specs = (P("dp", "ctx", "ch"), P(), P(), P(None, "ch"))
    return jax.shard_map(shards, mesh=mesh, in_specs=in_specs, out_specs=out_specs, check_vma=False)
```

```python
import math

import jax
import jax.numpy as jnp
import numpy as np
from jax import lax
from jax.experimental import pallas as pl
from jax.experimental.pallas import tpu as pltpu
from jax.sharding import PartitionSpec as P

LAG_BLOCKS = 4
Z_HIGH = 4
CORES = 2
TILE = 8

highest = lax.Precision.HIGHEST


def shifted(value, axis, steps):
    count = lax.axis_size(axis)
    initial, last = (max(0, -steps), min(count, count - steps))
    return lax.ppermute(value, axis, [(source, source + steps) for source in range(initial, last)])


def swapped(value):
    count = lax.axis_size("ctx")
    return lax.ppermute(value, "ctx", [(i, i ^ 1) for i in range(count)])


def lag_features(count, width):
    halfway = width // 2
    rates = np.float32(3.0) * np.exp(np.arange(halfway, dtype=np.float32) * np.float32(-math.log(count) / halfway))
    angles = np.arange(count, dtype=np.float32)[:, None] * rates[None, :].astype(np.float32)
    angles = angles.astype(np.float32).astype(np.float64)
    return np.concatenate([np.sin(angles), np.cos(angles)], axis=1)


def odd_table(length):
    phase = (2 * np.arange(length)[:, None] + 1) * np.arange(length)[None, :] % (4 * length)
    angles = phase * (2.0 * math.pi / (4 * length))
    return np.concatenate([np.cos(angles), -np.sin(angles)], axis=0)


def halves(table):
    upper = table.astype(jnp.bfloat16)
    lower = (table - upper.astype(np.float64)).astype(jnp.bfloat16)
    return np.concatenate([upper, lower], axis=0)


def turned(value, axis):
    rows = value.shape[axis] // 2
    shape = [1, 1]
    shape[axis] = rows
    parity = jnp.where(lax.broadcasted_iota(jnp.int32, shape, axis) % 2 == 0, 1.0, -1.0)
    real, imag = jnp.split(value, 2, axis=axis)
    return jnp.concatenate([-parity * imag, parity * real], axis=axis)


def device_groups():
    count, rows, lines = lax.axis_size("ctx"), lax.axis_size("dp"), lax.axis_size("ch")
    wide = count // (CORES * Z_HIGH)
    planes = [
        [d * count + (x * Z_HIGH + z) * CORES + c for x in range(wide) for z in range(Z_HIGH) for d in range(rows)]
        for c in range(CORES)
    ]
    columns = [
        [(s * CORES + c) * lines + y for c in range(CORES) for y in range(lines)]
        for s in range(wide * Z_HIGH)
    ]
    return planes, columns


def exchanged(value, axes, groups):
    return lax.all_to_all(
        value, axes, split_axis=0, concat_axis=0, axis_index_groups=groups, tiled=True
    )


def parts(value):
    upper = value.astype(jnp.bfloat16)
    return upper, (value - upper.astype(jnp.float32)).astype(jnp.bfloat16)


def times(first, second):
    return jnp.dot(first, second, preferred_element_type=jnp.float32)


def times_stacked(stacked, second):
    rows = stacked.shape[0] // 2
    upper, lower = parts(second)
    both = times(stacked, upper)
    return both[:rows] + both[rows:] + times(stacked[:rows], lower)


def spectrum(table, block):
    both = times(table, block)
    rows = both.shape[0] // 2
    return both[:rows], both[rows:], rows // 2


def packed_spectrum(table, block):
    upper, lower, rows = spectrum(table, block)
    total = upper + lower
    return total[:rows], total[rows:]


def conj_product(first, second):
    real_a, imag_a = first
    real_b, imag_b = second
    return real_a * real_b + imag_a * imag_b, real_a * imag_b - imag_a * real_b


def pair_products(first, second, net, weight):
    units = weight.shape[0]
    pair = jnp.concatenate(conj_product(first, second), axis=0)
    upper, lower = parts(pair)
    net_hi, net_lo = parts(net)
    both = times(jnp.concatenate([net_hi, net_lo], axis=0), upper)
    coef = both[:units] + both[units:] + times(net_hi, lower)
    weight_hi, weight_lo = parts(weight)
    last = (((1,), (1,)), ((), ()))
    both = lax.dot_general(
        upper, jnp.concatenate([weight_hi, weight_lo], axis=0), last, preferred_element_type=jnp.float32
    )
    mix = both[:, :units] + both[:, units:] + lax.dot_general(
        lower, weight_hi, last, preferred_element_type=jnp.float32
    )
    return coef, mix


def started(sems, pairs):
    copies = [
        pltpu.make_async_copy(source, target, sems.at[i]) for i, (source, target) in enumerate(pairs)
    ]
    for copy in copies:
        copy.start()
    return copies


def prepare_kernel(
    embed_in, lift_weight_in, lift_bias_in, inverse_in, split_in, c0_in, x0_in, weight_in,
    net, slope, coef, mix,
    embed, lift_weight, lift_bias, inverse, split, c0, x0, weight, sems,
):
    copies = started(
        sems,
        [
            (embed_in, embed), (lift_weight_in, lift_weight), (lift_bias_in, lift_bias),
            (inverse_in, inverse), (split_in, split), (c0_in, c0), (x0_in, x0), (weight_in, weight),
        ],
    )
    units = lift_weight.shape[1]
    length = inverse.shape[0] // 2
    for copy in copies[:3]:
        copy.wait()
    preact = jnp.dot(
        embed[...], lift_weight[...], precision=highest, preferred_element_type=jnp.float32
    ) + lift_bias[...]
    logistic = jax.nn.sigmoid(preact)
    hidden = preact * logistic
    slope[...] = logistic * (1.0 + preact * (1.0 - logistic))
    rows = jnp.concatenate(
        [hidden[k * length:(k + 1) * length].T for k in range(LAG_BLOCKS)], axis=0
    )
    upper, lower = parts(rows)
    count = rows.shape[0]
    copies[3].wait()
    both = times(jnp.concatenate([upper, lower], axis=0), inverse[:length, :])
    plain = both[:count] + both[count:] + times(upper, inverse[length:, :])
    moved = turned(plain, 1)
    net[:units, :] = plain[:units]
    net[units:count, :] = plain[units:] + moved[:-units]
    net[count:, :] = moved[-units:]
    for copy in copies[4:]:
        copy.wait()
    own = packed_spectrum(split[...], c0[...])
    source = packed_spectrum(split[...], x0[...])
    coef[...], mix[...] = pair_products(source, own, plain[:units], weight[...])


def halved(ref):
    rows = ref.shape[0] // 2
    return ref[:rows, :], ref[rows:, :]


def lag_kernel(
    scale, own, lift_rows,
    c1, c2, x2, first_coef, first_mix, net, slope,
    x0_in, split_in, weight_in, inverse_in, embed_in, out, same,
    x0, split, weight, inverse, embed, packed, sems,
):
    copies = started(
        sems,
        [
            (split_in, split), (x0_in, x0), (weight_in, weight), (inverse_in, inverse), (embed_in, embed),
            (c2, same),
        ],
    )
    units, channels = weight.shape
    copies[0].wait()
    table = split[...]
    next_spec, ahead_spec, back_spec = [packed_spectrum(table, ref[...]) for ref in (c1, c2, x2)]
    for copy in copies[1:3]:
        copy.wait()
    in_spec = packed_spectrum(table, x0[...])
    products = [
        (in_spec, next_spec),
        (in_spec, ahead_spec),
        (back_spec, next_spec),
        (back_spec, ahead_spec),
    ]
    coef = first_coef[...]
    mixes = [first_mix[...]]
    for k, (first, second) in enumerate(products, 1):
        part, mix = pair_products(first, second, net[k * units:(k + 1) * units, :], weight[...])
        coef = coef + part
        mixes.append(mix)
    for copy in copies[3:]:
        copy.wait()
    sides = jnp.concatenate(
        [mixes[k] - turned(mixes[k + 1], 0) for k in range(LAG_BLOCKS)], axis=1
    )
    lagged = times_stacked(inverse[...], sides)
    grads = jnp.concatenate(
        [lagged[:, k * units:(k + 1) * units] for k in range(LAG_BLOCKS)], axis=0
    ) * (slope[...] * scale)
    lift = times_stacked(embed[...], grads)
    bias = jnp.sum(grads, axis=0, keepdims=True)
    owners = packed.shape[0]
    coef = coef * scale
    pieces = [coef[:, k * units:(k + 1) * units] for k in range(channels // units)]
    packed[:, :own, :] = jnp.concatenate(pieces, axis=0).reshape(owners, own, units)
    used = lift.shape[0] // lift_rows
    packed[:used, own:, :] = lift.reshape(used, lift_rows, units)
    packed[used, own:, :] = jnp.broadcast_to(bias, (lift_rows, units))
    if used + 1 < owners:
        packed[used + 1:, own:, :] = jnp.zeros((owners - used - 1, lift_rows, units), jnp.float32)
    copy = pltpu.make_async_copy(packed, out, sems.at[len(copies)])
    copy.start()
    copy.wait()


def early_tokens_kernel(
    c1, net, c0_in, c2_in, split_in, weight_in, out, coefs_out,
    c0, c2, split, weight, total_kept, coefs, sems,
):
    copies = started(sems, [(split_in, split), (c0_in, c0), (c2_in, c2), (weight_in, weight)])
    length = c2.shape[0]
    units = weight.shape[0]
    for copy in copies:
        copy.wait()
    table = split[...]
    weight_hi, weight_lo = parts(weight[...])
    doubled = jnp.concatenate([weight_hi, weight_hi], axis=0)
    specs = [packed_spectrum(table, ref[...]) for ref in (c0, c1, c2)]
    total = None
    for k in range(LAG_BLOCKS + 1):
        net_hi, net_lo = parts(net[k * units:(k + 1) * units, :].T)
        coef = times(jnp.concatenate([net_hi, net_lo], axis=1), doubled) + times(net_hi, weight_lo)
        if k >= len(specs):
            coefs[k - len(specs)] = coef
            continue
        term = conj_product((coef[:length], coef[length:]), specs[k])
        total = term if total is None else (total[0] + term[0], total[1] + term[1])
    total_kept[...] = jnp.concatenate(total, axis=0)
    copies = [
        pltpu.make_async_copy(total_kept, out, sems.at[0]),
        pltpu.make_async_copy(coefs, coefs_out, sems.at[1]),
    ]
    for copy in copies:
        copy.start()
    for copy in copies:
        copy.wait()


def late_tokens_kernel(c3, c4, early_in, coefs_in, split_in, inverse_in, out, early, coefs, split, inverse, sems):
    copies = started(
        sems, [(split_in, split), (coefs_in, coefs), (early_in, early), (inverse_in, inverse)]
    )
    copies[0].wait()
    table = split[...]
    specs = [packed_spectrum(table, ref[...]) for ref in (c3, c4)]
    copies[1].wait()
    terms = [conj_product(halved(coefs.at[k]), spec) for k, spec in enumerate(specs)]
    copies[2].wait()
    total = [a + b + c for a, b, c in zip(halved(early), *terms)]
    copies[3].wait()
    length = c3.shape[0]
    out[...] = times_stacked(inverse[...], jnp.concatenate(total, axis=0)) * (1.0 / length)


def first_sum_kernel(value, block, early, out, same, sems):
    copies = started(sems, [(block, same)])
    total = jnp.sum(value[...], axis=0)
    out[...] = jnp.broadcast_to(total[None], out.shape)
    copies[0].wait()


def second_sum_kernel(own, line, core, value, relayed, block, out, swap):
    swap[...] = jnp.where(core[0] == 0, relayed[...].astype(jnp.float32), block[...].astype(jnp.float32)).astype(
        swap.dtype
    )
    slots = value.shape[0]
    lines = slots // CORES
    place = line[0]
    coef = value[place, :own, :]
    for c in range(1, CORES):
        coef = coef + value[c * lines + place, :own, :]
    rest = jnp.sum(value[:, own:, :], axis=0)
    out[:, :own, :] = jnp.broadcast_to(coef[None], (out.shape[0],) + coef.shape)
    out[:, own:, :] = jnp.broadcast_to(rest[None], (out.shape[0],) + rest.shape)


def unpack_kernel(own, value, coef, lift, bias):
    owners, _, units = value.shape
    depth = coef.shape[0]
    each = depth // own
    for k in range(coef.shape[1] // units):
        coef[:, k * units:(k + 1) * units] = value[k * each:(k + 1) * each, :own, :].reshape(depth, units)
    rows = value.shape[1] - own
    used = lift.shape[0] // rows
    lift[...] = value[:used, own:, :].reshape(lift.shape)
    bias[...] = value[used, own:own + 1, :]


def called(kernel, mebibytes, shapes, *operands, **options):
    return pl.pallas_call(
        kernel,
        out_shape=shapes,
        compiler_params=pltpu.CompilerParams(vmem_limit_bytes=mebibytes * 2 ** 20),
        **options,
    )(*operands)


def shards(tokens_in, cotangent, lift_weight, lift_bias, coef_weight):
    inputs = tokens_in[0]
    grads = cotangent[0]
    length, channels = inputs.shape
    lags = LAG_BLOCKS * length
    features, units = lift_weight.shape
    depth = coef_weight.shape[0]
    blocks_total = lax.axis_size("ctx")

    core = (lax.axis_index("ctx") % CORES).astype(jnp.int32).reshape(1)
    ahead2 = shifted(grads, "ctx", -CORES)
    ahead1 = shifted(grads, "ctx", -1)
    behind2 = shifted(inputs, "ctx", CORES)

    def real(*shape):
        return jax.ShapeDtypeStruct(shape, jnp.float32)

    def like(value):
        return jax.ShapeDtypeStruct(value.shape, value.dtype)

    scalar = pl.BlockSpec(memory_space=pltpu.SMEM)
    whole = pl.BlockSpec(memory_space=pltpu.VMEM)
    table = odd_table(length)
    split = jnp.asarray(halves(table))
    inverse = jnp.asarray(halves(table.T))
    features_table = lag_features(lags, features)
    embed = jnp.asarray(features_table, jnp.float32)
    embed_turned = jnp.asarray(halves(features_table.T))

    def held(value):
        return pltpu.with_memory_space_constraint(value, pltpu.HBM)

    def room(value):
        return pltpu.VMEM(value.shape, value.dtype)

    def sems(count):
        return pltpu.SemaphoreType.DMA((count,))

    far_off = pl.BlockSpec(memory_space=pltpu.HBM)
    bias_row = lift_bias[None]
    first_operands = (embed, lift_weight, bias_row, inverse, split, grads, inputs, coef_weight)
    net, slope, coef, mix = called(
        prepare_kernel,
        24,
        (
            real((LAG_BLOCKS + 1) * units, 2 * length),
            real(lags, units),
            real(depth, channels),
            real(2 * length, units),
        ),
        *[held(value) for value in first_operands],
        in_specs=[far_off] * 8,
        scratch_shapes=[room(value) for value in first_operands] + [sems(8)],
    )
    planes, columns = device_groups()
    owners, slots = len(planes[0]), len(columns[0])
    own = channels // units * depth // owners
    lift_rows = TILE * 2 ** max(0, math.ceil(math.log2((features + TILE) / (TILE * owners))))
    scale = 1.0 / math.sqrt(lax.axis_size("dp") * length * blocks_total) / length

    def rows_of(count):
        return real(count, own + lift_rows, units)

    packed, ahead2 = called(
        lambda *refs: lag_kernel(scale, own, lift_rows, *refs),
        32,
        (pltpu.HBM((owners, own + lift_rows, units), jnp.float32), pltpu.HBM(ahead2.shape, ahead2.dtype)),
        ahead1, ahead2, behind2, coef, mix, net, slope,
        *[held(value) for value in (inputs, split, coef_weight, inverse, embed_turned)],
        in_specs=[whole] * 7 + [far_off] * 5,
        out_specs=[far_off] * 2,
        scratch_shapes=[room(value) for value in (inputs, split, coef_weight, inverse, embed_turned)]
        + [pltpu.VMEM((owners, own + lift_rows, units), jnp.float32), sems(7)],
    )
    summed = exchanged(packed, ("dp", "ctx"), planes)
    kept = ((2 * length, channels), (2, 2 * length, channels))
    early, coefs = called(
        early_tokens_kernel,
        24,
        tuple(pltpu.HBM(shape, jnp.float32) for shape in kept),
        ahead1, net,
        *[held(value) for value in (grads, ahead2, split, coef_weight)],
        in_specs=[whole] * 2 + [far_off] * 4,
        out_specs=[far_off] * 2,
        scratch_shapes=[room(value) for value in (grads, ahead2, split, coef_weight)]
        + [pltpu.VMEM(shape, jnp.float32) for shape in kept]
        + [sems(4)],
    )
    summed, ahead2 = called(
        first_sum_kernel,
        8,
        (rows_of(slots), like(ahead2)),
        summed, held(ahead2), held(early),
        in_specs=[whole, far_off, far_off],
        scratch_shapes=[sems(1)],
    )
    last = shifted(ahead2, "ctx", -CORES)
    summed = exchanged(summed, ("ctx", "ch"), columns)
    line = lax.axis_index("ch").astype(jnp.int32).reshape(1)
    spread, swap = called(
        lambda *refs: second_sum_kernel(own, *refs),
        8,
        (rows_of(owners), like(last)),
        line, core, summed, last, ahead2,
        in_specs=[scalar] * 2 + [whole] * 3,
    )
    ahead3 = swapped(swap)
    full = exchanged(spread, ("dp", "ctx"), planes)
    coef_weight_grad, lift_weight_grad, lift_bias_grad = called(
        lambda *refs: unpack_kernel(own, *refs),
        8,
        (
            jax.ShapeDtypeStruct((depth, channels), jnp.float32),
            jax.ShapeDtypeStruct((features, units), jnp.float32),
            jax.ShapeDtypeStruct((1, units), jnp.float32),
        ),
        full,
    )
    tokens_grad = called(
        late_tokens_kernel,
        16,
        real(length, channels),
        ahead3, last,
        *[held(value) for value in (early, coefs, split, inverse)],
        in_specs=[whole] * 2 + [far_off] * 4,
        scratch_shapes=[room(value) for value in (early, coefs, split, inverse)] + [sems(4)],
    )
    return (tokens_grad[None], lift_weight_grad, lift_bias_grad[0], coef_weight_grad)


def solution(mesh):
    in_specs = (P("dp", "ctx", "ch"), P("dp", "ctx", "ch"), P(), P(), P(None, "ch"))
    out_specs = (P("dp", "ctx", "ch"), P(), P(), P(None, "ch"))
    return jax.shard_map(shards, mesh=mesh, in_specs=in_specs, out_specs=out_specs, check_vma=False)
```

```python
import math

import jax
import jax.numpy as jnp
import numpy as np
from jax import lax
from jax.experimental import pallas as pl
from jax.experimental.pallas import tpu as pltpu
from jax.sharding import PartitionSpec as P

LAG_BLOCKS = 4
Z_HIGH = 4
CORES = 2
TILE = 8

highest = lax.Precision.HIGHEST


def shifted(value, axis, steps):
    count = lax.axis_size(axis)
    initial, last = (max(0, -steps), min(count, count - steps))
    return lax.ppermute(value, axis, [(source, source + steps) for source in range(initial, last)])


def swapped(value):
    count = lax.axis_size("ctx")
    return lax.ppermute(value, "ctx", [(i, i ^ 1) for i in range(count)])


def lag_features(count, width):
    halfway = width // 2
    rates = np.float32(3.0) * np.exp(np.arange(halfway, dtype=np.float32) * np.float32(-math.log(count) / halfway))
    angles = np.arange(count, dtype=np.float32)[:, None] * rates[None, :].astype(np.float32)
    angles = angles.astype(np.float32).astype(np.float64)
    return np.concatenate([np.sin(angles), np.cos(angles)], axis=1)


def odd_table(length):
    phase = (2 * np.arange(length)[:, None] + 1) * np.arange(length)[None, :] % (4 * length)
    angles = phase * (2.0 * math.pi / (4 * length))
    return np.concatenate([np.cos(angles), -np.sin(angles)], axis=0)


def halves(table):
    upper = table.astype(jnp.bfloat16)
    lower = (table - upper.astype(np.float64)).astype(jnp.bfloat16)
    return np.concatenate([upper, lower], axis=0)


def turned(value, axis):
    rows = value.shape[axis] // 2
    shape = [1, 1]
    shape[axis] = rows
    parity = jnp.where(lax.broadcasted_iota(jnp.int32, shape, axis) % 2 == 0, 1.0, -1.0)
    real, imag = jnp.split(value, 2, axis=axis)
    return jnp.concatenate([-parity * imag, parity * real], axis=axis)


def device_groups():
    count, rows, lines = lax.axis_size("ctx"), lax.axis_size("dp"), lax.axis_size("ch")
    wide = count // (CORES * Z_HIGH)
    planes = [
        [d * count + (x * Z_HIGH + z) * CORES + c for x in range(wide) for z in range(Z_HIGH) for d in range(rows)]
        for c in range(CORES)
    ]
    columns = [
        [(s * CORES + c) * lines + y for c in range(CORES) for y in range(lines)]
        for s in range(wide * Z_HIGH)
    ]
    return planes, columns


def exchanged(value, axes, groups):
    return lax.all_to_all(
        value, axes, split_axis=0, concat_axis=0, axis_index_groups=groups, tiled=True
    )


def parts(value):
    upper = value.astype(jnp.bfloat16)
    return upper, (value - upper.astype(jnp.float32)).astype(jnp.bfloat16)


def times(first, second):
    return jnp.dot(first, second, preferred_element_type=jnp.float32)


def times_stacked(stacked, second):
    rows = stacked.shape[0] // 2
    upper, lower = parts(second)
    both = times(stacked, upper)
    return both[:rows] + both[rows:] + times(stacked[:rows], lower)


def spectrum(table, block):
    both = times(table, block)
    rows = both.shape[0] // 2
    return both[:rows], both[rows:], rows // 2


def packed_spectrum(table, block):
    upper, lower, rows = spectrum(table, block)
    total = upper + lower
    return total[:rows], total[rows:]


def conj_product(first, second):
    real_a, imag_a = first
    real_b, imag_b = second
    return real_a * real_b + imag_a * imag_b, real_a * imag_b - imag_a * real_b


def pair_products(first, second, net, weight):
    units = weight.shape[0]
    pair = jnp.concatenate(conj_product(first, second), axis=0)
    upper, lower = parts(pair)
    net_hi, net_lo = parts(net)
    both = times(jnp.concatenate([net_hi, net_lo], axis=0), upper)
    coef = both[:units] + both[units:] + times(net_hi, lower)
    weight_hi, weight_lo = parts(weight)
    last = (((1,), (1,)), ((), ()))
    both = lax.dot_general(
        upper, jnp.concatenate([weight_hi, weight_lo], axis=0), last, preferred_element_type=jnp.float32
    )
    mix = both[:, :units] + both[:, units:] + lax.dot_general(
        lower, weight_hi, last, preferred_element_type=jnp.float32
    )
    return coef, mix


def started(sems, pairs):
    copies = [
        pltpu.make_async_copy(source, target, sems.at[i]) for i, (source, target) in enumerate(pairs)
    ]
    for copy in copies:
        copy.start()
    return copies


def prepare_kernel(
    embed_in, lift_weight_in, lift_bias_in, inverse_in, split_in, c0_in, x0_in, weight_in,
    net, slope, coef, mix, split,
    embed, lift_weight, lift_bias, inverse, c0, x0, weight, sems,
):
    copies = started(
        sems,
        [
            (embed_in, embed), (lift_weight_in, lift_weight), (lift_bias_in, lift_bias),
            (inverse_in, inverse), (split_in, split), (c0_in, c0), (x0_in, x0), (weight_in, weight),
        ],
    )
    units = lift_weight.shape[1]
    length = inverse.shape[0] // 2
    for copy in copies[:3]:
        copy.wait()
    preact = jnp.dot(
        embed[...], lift_weight[...], precision=highest, preferred_element_type=jnp.float32
    ) + lift_bias[...]
    logistic = jax.nn.sigmoid(preact)
    hidden = preact * logistic
    slope[...] = logistic * (1.0 + preact * (1.0 - logistic))
    rows = jnp.concatenate(
        [hidden[k * length:(k + 1) * length].T for k in range(LAG_BLOCKS)], axis=0
    )
    upper, lower = parts(rows)
    count = rows.shape[0]
    copies[3].wait()
    both = times(jnp.concatenate([upper, lower], axis=0), inverse[:length, :])
    plain = both[:count] + both[count:] + times(upper, inverse[length:, :])
    moved = turned(plain, 1)
    net[:units, :] = plain[:units]
    net[units:count, :] = plain[units:] + moved[:-units]
    net[count:, :] = moved[-units:]
    for copy in copies[4:]:
        copy.wait()
    own = packed_spectrum(split[...], c0[...])
    source = packed_spectrum(split[...], x0[...])
    coef[...], mix[...] = pair_products(source, own, plain[:units], weight[...])


def halved(ref):
    rows = ref.shape[0] // 2
    return ref[:rows, :], ref[rows:, :]


def lag_kernel(
    scale, own, lift_rows,
    c2, x2, c1, first_coef, first_mix, net, slope, split,
    x0_in, weight_in, inverse_in, embed_in, out, same,
    x0, weight, inverse, embed, coef_rows, other_rows, sems,
):
    copies = started(
        sems,
        [(x0_in, x0), (weight_in, weight), (inverse_in, inverse), (embed_in, embed), (c1, same)],
    )
    units, channels = weight.shape
    table = split[...]
    next_spec, ahead_spec, back_spec = [packed_spectrum(table, ref[...]) for ref in (c1, c2, x2)]
    for copy in copies[:2]:
        copy.wait()
    in_spec = packed_spectrum(table, x0[...])
    products = [
        (in_spec, next_spec),
        (in_spec, ahead_spec),
        (back_spec, next_spec),
        (back_spec, ahead_spec),
    ]
    coef = first_coef[...]
    mixes = [first_mix[...]]
    for k, (first, second) in enumerate(products, 1):
        part, mix = pair_products(first, second, net[k * units:(k + 1) * units, :], weight[...])
        coef = coef + part
        mixes.append(mix)
    owners = out.shape[0]
    coef = coef * scale
    pieces = [coef[:, k * units:(k + 1) * units] for k in range(channels // units)]
    coef_rows[...] = jnp.concatenate(pieces, axis=0).reshape(owners, own, units)
    coef_copy = pltpu.make_async_copy(coef_rows, out.at[:, pl.ds(0, own), :], sems.at[len(copies)])
    coef_copy.start()
    for copy in copies[2:]:
        copy.wait()
    sides = jnp.concatenate(
        [mixes[k] - turned(mixes[k + 1], 0) for k in range(LAG_BLOCKS)], axis=1
    )
    lagged = times_stacked(inverse[...], sides)
    grads = jnp.concatenate(
        [lagged[:, k * units:(k + 1) * units] for k in range(LAG_BLOCKS)], axis=0
    ) * (slope[...] * scale)
    lift = times_stacked(embed[...], grads)
    bias = jnp.sum(grads, axis=0, keepdims=True)
    used = lift.shape[0] // lift_rows
    other_rows[:used] = lift.reshape(used, lift_rows, units)
    other_rows[used] = jnp.broadcast_to(bias, (lift_rows, units))
    if used + 1 < owners:
        other_rows[used + 1:] = jnp.zeros((owners - used - 1, lift_rows, units), jnp.float32)
    other_copy = pltpu.make_async_copy(
        other_rows, out.at[:, pl.ds(own, lift_rows), :], sems.at[len(copies) + 1]
    )
    other_copy.start()
    coef_copy.wait()
    other_copy.wait()


def early_tokens_kernel(
    c2, net, split, c0_in, c1_in, weight_in, behind, out, coefs_out, same,
    c0, c1, weight, total_kept, coefs, sems,
):
    copies = started(sems, [(c0_in, c0), (c1_in, c1), (weight_in, weight)])
    length = c2.shape[0]
    units = weight.shape[0]
    for copy in copies:
        copy.wait()
    table = split[...]
    weight_hi, weight_lo = parts(weight[...])
    doubled = jnp.concatenate([weight_hi, weight_hi], axis=0)
    specs = [packed_spectrum(table, ref[...]) for ref in (c0, c1, c2)]
    total = None
    for k in range(LAG_BLOCKS + 1):
        net_hi, net_lo = parts(net[k * units:(k + 1) * units, :].T)
        coef = times(jnp.concatenate([net_hi, net_lo], axis=1), doubled) + times(net_hi, weight_lo)
        if k >= len(specs):
            coefs[k - len(specs)] = coef
            continue
        term = conj_product((coef[:length], coef[length:]), specs[k])
        total = term if total is None else (total[0] + term[0], total[1] + term[1])
    total_kept[...] = jnp.concatenate(total, axis=0)
    for copy in started(sems, [(total_kept, out), (coefs, coefs_out), (c2, same)]):
        copy.wait()


def late_tokens_kernel(c3, c4, split, early_in, coefs_in, inverse_in, out, early, coefs, inverse, sems):
    copies = started(sems, [(coefs_in, coefs), (early_in, early), (inverse_in, inverse)])
    table = split[...]
    specs = [packed_spectrum(table, ref[...]) for ref in (c3, c4)]
    copies[0].wait()
    terms = [conj_product(halved(coefs.at[k]), spec) for k, spec in enumerate(specs)]
    copies[1].wait()
    total = [a + b + c for a, b, c in zip(halved(early), *terms)]
    copies[2].wait()
    length = c3.shape[0]
    out[...] = times_stacked(inverse[...], jnp.concatenate(total, axis=0)) * (1.0 / length)


def first_sum_kernel(value, early, out):
    total = jnp.sum(value[...], axis=0)
    out[...] = jnp.broadcast_to(total[None], out.shape)


def choose_kernel(core, relayed, block, out):
    out[...] = jnp.where(core[0] == 0, relayed[...].astype(jnp.float32), block[...].astype(jnp.float32)).astype(
        out.dtype
    )


def second_sum_kernel(own, line, value, block, out, same):
    same[...] = block[...]
    slots = value.shape[0]
    lines = slots // CORES
    place = line[0]
    coef = value[place, :own, :]
    for c in range(1, CORES):
        coef = coef + value[c * lines + place, :own, :]
    rest = jnp.sum(value[:, own:, :], axis=0)
    out[:, :own, :] = jnp.broadcast_to(coef[None], (out.shape[0],) + coef.shape)
    out[:, own:, :] = jnp.broadcast_to(rest[None], (out.shape[0],) + rest.shape)


def unpack_kernel(own, value, coef, lift, bias):
    owners, _, units = value.shape
    depth = coef.shape[0]
    each = depth // own
    for k in range(coef.shape[1] // units):
        coef[:, k * units:(k + 1) * units] = value[k * each:(k + 1) * each, :own, :].reshape(depth, units)
    rows = value.shape[1] - own
    used = lift.shape[0] // rows
    lift[...] = value[:used, own:, :].reshape(lift.shape)
    bias[...] = value[used, own:own + 1, :]


def called(kernel, mebibytes, shapes, *operands, **options):
    return pl.pallas_call(
        kernel,
        out_shape=shapes,
        compiler_params=pltpu.CompilerParams(vmem_limit_bytes=mebibytes * 2 ** 20),
        **options,
    )(*operands)


def shards(tokens_in, cotangent, lift_weight, lift_bias, coef_weight):
    inputs = tokens_in[0]
    grads = cotangent[0]
    length, channels = inputs.shape
    lags = LAG_BLOCKS * length
    features, units = lift_weight.shape
    depth = coef_weight.shape[0]
    blocks_total = lax.axis_size("ctx")

    core = (lax.axis_index("ctx") % CORES).astype(jnp.int32).reshape(1)
    ahead2 = shifted(grads, "ctx", -CORES)
    behind2 = shifted(inputs, "ctx", CORES)
    ahead1 = shifted(grads, "ctx", -1)

    def real(*shape):
        return jax.ShapeDtypeStruct(shape, jnp.float32)

    def like(value):
        return jax.ShapeDtypeStruct(value.shape, value.dtype)

    scalar = pl.BlockSpec(memory_space=pltpu.SMEM)
    whole = pl.BlockSpec(memory_space=pltpu.VMEM)
    table = odd_table(length)
    split = jnp.asarray(halves(table))
    inverse = jnp.asarray(halves(table.T))
    features_table = lag_features(lags, features)
    embed = jnp.asarray(features_table, jnp.float32)
    embed_turned = jnp.asarray(halves(features_table.T))

    def held(value):
        return pltpu.with_memory_space_constraint(value, pltpu.HBM)

    def room(value):
        return pltpu.VMEM(value.shape, value.dtype)

    def sems(count):
        return pltpu.SemaphoreType.DMA((count,))

    far_off = pl.BlockSpec(memory_space=pltpu.HBM)
    bias_row = lift_bias[None]
    first_operands = (embed, lift_weight, bias_row, inverse, split, grads, inputs, coef_weight)
    net, slope, coef, mix, split = called(
        prepare_kernel,
        24,
        (
            real((LAG_BLOCKS + 1) * units, 2 * length),
            real(lags, units),
            real(depth, channels),
            real(2 * length, units),
            like(split),
        ),
        *[held(value) for value in first_operands],
        in_specs=[far_off] * 8,
        scratch_shapes=[room(value) for value in first_operands if value is not split] + [sems(8)],
    )
    planes, columns = device_groups()
    owners, slots = len(planes[0]), len(columns[0])
    own = channels // units * depth // owners
    lift_rows = TILE * 2 ** max(0, math.ceil(math.log2((features + TILE) / (TILE * owners))))
    scale = 1.0 / math.sqrt(lax.axis_size("dp") * length * blocks_total) / length

    def rows_of(count):
        return real(count, own + lift_rows, units)

    packed, ahead1 = called(
        lambda *refs: lag_kernel(scale, own, lift_rows, *refs),
        32,
        (pltpu.HBM((owners, own + lift_rows, units), jnp.float32), pltpu.HBM(ahead1.shape, ahead1.dtype)),
        ahead2, behind2, ahead1, coef, mix, net, slope, split,
        *[held(value) for value in (inputs, coef_weight, inverse, embed_turned)],
        in_specs=[whole] * 8 + [far_off] * 4,
        out_specs=[far_off] * 2,
        scratch_shapes=[room(value) for value in (inputs, coef_weight, inverse, embed_turned)]
        + [pltpu.VMEM((owners, rows, units), jnp.float32) for rows in (own, lift_rows)]
        + [sems(7)],
    )
    summed = exchanged(packed, ("dp", "ctx"), planes)
    kept = ((2 * length, channels), (2, 2 * length, channels))
    early, coefs, ahead2 = called(
        early_tokens_kernel,
        24,
        tuple(pltpu.HBM(shape, jnp.float32) for shape in kept) + (pltpu.HBM(ahead2.shape, ahead2.dtype),),
        ahead2, net, split,
        *[held(value) for value in (grads, ahead1, coef_weight)],
        behind2,
        in_specs=[whole] * 3 + [far_off] * 3 + [pl.BlockSpec(memory_space=pl.ANY)],
        out_specs=[far_off] * 3,
        scratch_shapes=[room(value) for value in (grads, ahead1, coef_weight)]
        + [pltpu.VMEM(shape, jnp.float32) for shape in kept]
        + [sems(3)],
    )
    summed = called(
        first_sum_kernel,
        8,
        rows_of(slots),
        summed, held(early),
        in_specs=[whole, far_off],
    )
    last = shifted(ahead2, "ctx", -CORES)
    ahead3 = swapped(
        called(choose_kernel, 8, like(last), core, last, ahead2, in_specs=[scalar] + [whole] * 2)
    )
    summed = exchanged(summed, ("ctx", "ch"), columns)
    line = lax.axis_index("ch").astype(jnp.int32).reshape(1)
    spread, ahead3 = called(
        lambda *refs: second_sum_kernel(own, *refs),
        8,
        (rows_of(owners), like(last)),
        line, summed, ahead3,
        in_specs=[scalar] + [whole] * 2,
    )
    full = exchanged(spread, ("dp", "ctx"), planes)
    coef_weight_grad, lift_weight_grad, lift_bias_grad = called(
        lambda *refs: unpack_kernel(own, *refs),
        8,
        (
            jax.ShapeDtypeStruct((depth, channels), jnp.float32),
            jax.ShapeDtypeStruct((features, units), jnp.float32),
            jax.ShapeDtypeStruct((1, units), jnp.float32),
        ),
        full,
    )
    tokens_grad = called(
        late_tokens_kernel,
        16,
        real(length, channels),
        ahead3, last, split,
        *[held(value) for value in (early, coefs, inverse)],
        in_specs=[whole] * 3 + [far_off] * 3,
        scratch_shapes=[room(value) for value in (early, coefs, inverse)] + [sems(3)],
    )
    return (tokens_grad[None], lift_weight_grad, lift_bias_grad[0], coef_weight_grad)


def solution(mesh):
    in_specs = (P("dp", "ctx", "ch"), P("dp", "ctx", "ch"), P(), P(), P(None, "ch"))
    out_specs = (P("dp", "ctx", "ch"), P(), P(), P(None, "ch"))
    return jax.shard_map(shards, mesh=mesh, in_specs=in_specs, out_specs=out_specs, check_vma=False)
```

```python
import math

import jax
import jax.numpy as jnp
import numpy as np
from jax import lax
from jax.experimental import pallas as pl
from jax.experimental.pallas import tpu as pltpu
from jax.sharding import PartitionSpec as P

LAG_BLOCKS = 4
Z_HIGH = 4
CORES = 2
TILE = 8

highest = lax.Precision.HIGHEST


def shifted(value, axis, steps):
    count = lax.axis_size(axis)
    initial, last = (max(0, -steps), min(count, count - steps))
    return lax.ppermute(value, axis, [(source, source + steps) for source in range(initial, last)])


def moved(value, even, odd):
    count = lax.axis_size("ctx")
    pairs = [(i, i + (odd if i % CORES else even)) for i in range(count)]
    return lax.ppermute(value, "ctx", [(i, j) for i, j in pairs if i != j and 0 <= j < count])


def swapped(value):
    count = lax.axis_size("ctx")
    return lax.ppermute(value, "ctx", [(i, i ^ 1) for i in range(count)])


def lag_features(count, width):
    halfway = width // 2
    rates = np.float32(3.0) * np.exp(np.arange(halfway, dtype=np.float32) * np.float32(-math.log(count) / halfway))
    angles = np.arange(count, dtype=np.float32)[:, None] * rates[None, :].astype(np.float32)
    angles = angles.astype(np.float32).astype(np.float64)
    return np.concatenate([np.sin(angles), np.cos(angles)], axis=1)


def odd_table(length):
    phase = (2 * np.arange(length)[:, None] + 1) * np.arange(length)[None, :] % (4 * length)
    angles = phase * (2.0 * math.pi / (4 * length))
    return np.concatenate([np.cos(angles), -np.sin(angles)], axis=0)


def halves(table):
    upper = table.astype(jnp.bfloat16)
    lower = (table - upper.astype(np.float64)).astype(jnp.bfloat16)
    return np.concatenate([upper, lower], axis=0)


def turned(value, axis):
    rows = value.shape[axis] // 2
    shape = [1, 1]
    shape[axis] = rows
    parity = jnp.where(lax.broadcasted_iota(jnp.int32, shape, axis) % 2 == 0, 1.0, -1.0)
    real, imag = jnp.split(value, 2, axis=axis)
    return jnp.concatenate([-parity * imag, parity * real], axis=axis)


def device_groups():
    count, rows, lines = lax.axis_size("ctx"), lax.axis_size("dp"), lax.axis_size("ch")
    wide = count // (CORES * Z_HIGH)
    planes = [
        [d * count + (x * Z_HIGH + z) * CORES + c for x in range(wide) for z in range(Z_HIGH) for d in range(rows)]
        for c in range(CORES)
    ]
    columns = [
        [(s * CORES + c) * lines + y for c in range(CORES) for y in range(lines)]
        for s in range(wide * Z_HIGH)
    ]
    return planes, columns


def exchanged(value, axes, groups):
    return lax.all_to_all(
        value, axes, split_axis=0, concat_axis=0, axis_index_groups=groups, tiled=True
    )


def parts(value):
    upper = value.astype(jnp.bfloat16)
    return upper, (value - upper.astype(jnp.float32)).astype(jnp.bfloat16)


def times(first, second):
    return jnp.dot(first, second, preferred_element_type=jnp.float32)


def times_stacked(stacked, second):
    rows = stacked.shape[0] // 2
    upper, lower = parts(second)
    both = times(stacked, upper)
    return both[:rows] + both[rows:] + times(stacked[:rows], lower)


def spectrum(table, block):
    both = times(table, block)
    rows = both.shape[0] // 2
    return both[:rows], both[rows:], rows // 2


def packed_spectrum(table, block):
    upper, lower, rows = spectrum(table, block)
    total = upper + lower
    return total[:rows], total[rows:]


def conj_product(first, second):
    real_a, imag_a = first
    real_b, imag_b = second
    return real_a * real_b + imag_a * imag_b, real_a * imag_b - imag_a * real_b


def pair_products(first, second, net, weight):
    units = weight.shape[0]
    pair = jnp.concatenate(conj_product(first, second), axis=0)
    upper, lower = parts(pair)
    net_hi, net_lo = parts(net)
    both = times(jnp.concatenate([net_hi, net_lo], axis=0), upper)
    coef = both[:units] + both[units:] + times(net_hi, lower)
    weight_hi, weight_lo = parts(weight)
    last = (((1,), (1,)), ((), ()))
    both = lax.dot_general(
        upper, jnp.concatenate([weight_hi, weight_lo], axis=0), last, preferred_element_type=jnp.float32
    )
    mix = both[:, :units] + both[:, units:] + lax.dot_general(
        lower, weight_hi, last, preferred_element_type=jnp.float32
    )
    return coef, mix


def started(sems, pairs):
    copies = [
        pltpu.make_async_copy(source, target, sems.at[i]) for i, (source, target) in enumerate(pairs)
    ]
    for copy in copies:
        copy.start()
    return copies


def selected(flag, one, other):
    return jnp.where(flag, one.astype(jnp.float32), other.astype(jnp.float32)).astype(one.dtype)


def prepare_kernel(
    core, embed_in, lift_weight_in, lift_bias_in, inverse_in, split_in, c0_in, x0_in, weight_in,
    net, slope, coef, mix, split, crossing,
    embed, lift_weight, lift_bias, inverse, c0, x0, weight, sems,
):
    copies = started(
        sems,
        [
            (embed_in, embed), (lift_weight_in, lift_weight), (lift_bias_in, lift_bias),
            (inverse_in, inverse), (split_in, split), (c0_in, c0), (x0_in, x0), (weight_in, weight),
        ],
    )
    units = lift_weight.shape[1]
    length = inverse.shape[0] // 2
    for copy in copies[5:7]:
        copy.wait()
    crossing[...] = selected(core[0] == 0, x0[...], c0[...])
    for copy in copies[:3]:
        copy.wait()
    preact = jnp.dot(
        embed[...], lift_weight[...], precision=highest, preferred_element_type=jnp.float32
    ) + lift_bias[...]
    logistic = jax.nn.sigmoid(preact)
    hidden = preact * logistic
    slope[...] = logistic * (1.0 + preact * (1.0 - logistic))
    rows = jnp.concatenate(
        [hidden[k * length:(k + 1) * length].T for k in range(LAG_BLOCKS)], axis=0
    )
    upper, lower = parts(rows)
    count = rows.shape[0]
    copies[3].wait()
    both = times(jnp.concatenate([upper, lower], axis=0), inverse[:length, :])
    plain = both[:count] + both[count:] + times(upper, inverse[length:, :])
    moved = turned(plain, 1)
    net[:units, :] = plain[:units]
    net[units:count, :] = plain[units:] + moved[:-units]
    net[count:, :] = moved[-units:]
    copies[4].wait()
    copies[7].wait()
    own = packed_spectrum(split[...], c0[...])
    source = packed_spectrum(split[...], x0[...])
    coef[...], mix[...] = pair_products(source, own, plain[:units], weight[...])


def swap_kernel(core, first_cots, crossing, first_tokens, out):
    out[...] = selected(core[0] == 0, first_cots[...], crossing[...])


def halved(ref):
    rows = ref.shape[0] // 2
    return ref[:rows, :], ref[rows:, :]


def lag_kernel(
    scale, own, lift_rows,
    core, first_cots, crossed, first_tokens, c1, first_coef, first_mix, net, slope, split,
    x0_in, weight_in, inverse_in, embed_in, out, same1, same2,
    x0, weight, inverse, embed, c2, coef_rows, other_rows, sems,
):
    c2[...] = selected(core[0] == 0, first_cots[...], crossed[...])
    copies = started(
        sems,
        [(x0_in, x0), (weight_in, weight), (inverse_in, inverse), (embed_in, embed), (c1, same1), (c2, same2)],
    )
    units, channels = weight.shape
    table = split[...]
    x2 = selected(core[0] == 0, crossed[...], first_tokens[...])
    next_spec, ahead_spec, back_spec = [packed_spectrum(table, block) for block in (c1[...], c2[...], x2)]
    for copy in copies[:2]:
        copy.wait()
    in_spec = packed_spectrum(table, x0[...])
    products = [
        (in_spec, next_spec),
        (in_spec, ahead_spec),
        (back_spec, next_spec),
        (back_spec, ahead_spec),
    ]
    coef = first_coef[...]
    mixes = [first_mix[...]]
    for k, (first, second) in enumerate(products, 1):
        part, mix = pair_products(first, second, net[k * units:(k + 1) * units, :], weight[...])
        coef = coef + part
        mixes.append(mix)
    owners = out.shape[0]
    coef = coef * scale
    pieces = [coef[:, k * units:(k + 1) * units] for k in range(channels // units)]
    coef_rows[...] = jnp.concatenate(pieces, axis=0).reshape(owners, own, units)
    coef_copy = pltpu.make_async_copy(coef_rows, out.at[:, pl.ds(0, own), :], sems.at[len(copies)])
    coef_copy.start()
    for copy in copies[2:]:
        copy.wait()
    sides = jnp.concatenate(
        [mixes[k] - turned(mixes[k + 1], 0) for k in range(LAG_BLOCKS)], axis=1
    )
    lagged = times_stacked(inverse[...], sides)
    grads = jnp.concatenate(
        [lagged[:, k * units:(k + 1) * units] for k in range(LAG_BLOCKS)], axis=0
    ) * (slope[...] * scale)
    lift = times_stacked(embed[...], grads)
    bias = jnp.sum(grads, axis=0, keepdims=True)
    used = lift.shape[0] // lift_rows
    other_rows[:used] = lift.reshape(used, lift_rows, units)
    other_rows[used] = jnp.broadcast_to(bias, (lift_rows, units))
    if used + 1 < owners:
        other_rows[used + 1:] = jnp.zeros((owners - used - 1, lift_rows, units), jnp.float32)
    other_copy = pltpu.make_async_copy(
        other_rows, out.at[:, pl.ds(own, lift_rows), :], sems.at[len(copies) + 1]
    )
    other_copy.start()
    coef_copy.wait()
    other_copy.wait()


def early_tokens_kernel(
    net, split, c0_in, c1_in, c2_in, weight_in, out, coefs_out, same,
    c0, c1, c2, weight, total_kept, coefs, sems,
):
    copies = started(sems, [(c0_in, c0), (c1_in, c1), (c2_in, c2), (weight_in, weight)])
    length = c2.shape[0]
    units = weight.shape[0]
    for copy in copies:
        copy.wait()
    table = split[...]
    weight_hi, weight_lo = parts(weight[...])
    doubled = jnp.concatenate([weight_hi, weight_hi], axis=0)
    specs = [packed_spectrum(table, ref[...]) for ref in (c0, c1, c2)]
    total = None
    for k in range(LAG_BLOCKS + 1):
        net_hi, net_lo = parts(net[k * units:(k + 1) * units, :].T)
        coef = times(jnp.concatenate([net_hi, net_lo], axis=1), doubled) + times(net_hi, weight_lo)
        if k >= len(specs):
            coefs[k - len(specs)] = coef
            continue
        term = conj_product((coef[:length], coef[length:]), specs[k])
        total = term if total is None else (total[0] + term[0], total[1] + term[1])
    total_kept[...] = jnp.concatenate(total, axis=0)
    for copy in started(sems, [(total_kept, out), (coefs, coefs_out), (c2, same)]):
        copy.wait()


def late_tokens_kernel(c3, c4, split, early_in, coefs_in, inverse_in, out, early, coefs, inverse, sems):
    copies = started(sems, [(coefs_in, coefs), (early_in, early), (inverse_in, inverse)])
    table = split[...]
    specs = [packed_spectrum(table, ref[...]) for ref in (c3, c4)]
    copies[0].wait()
    terms = [conj_product(halved(coefs.at[k]), spec) for k, spec in enumerate(specs)]
    copies[1].wait()
    total = [a + b + c for a, b, c in zip(halved(early), *terms)]
    copies[2].wait()
    length = c3.shape[0]
    out[...] = times_stacked(inverse[...], jnp.concatenate(total, axis=0)) * (1.0 / length)


def first_sum_kernel(value, early, out):
    total = jnp.sum(value[...], axis=0)
    out[...] = jnp.broadcast_to(total[None], out.shape)


def choose_kernel(core, relayed, block, out):
    out[...] = selected(core[0] == 0, relayed[...], block[...])


def second_sum_kernel(own, line, value, block, out, same):
    same[...] = block[...]
    slots = value.shape[0]
    lines = slots // CORES
    place = line[0]
    coef = value[place, :own, :]
    for c in range(1, CORES):
        coef = coef + value[c * lines + place, :own, :]
    rest = jnp.sum(value[:, own:, :], axis=0)
    out[:, :own, :] = jnp.broadcast_to(coef[None], (out.shape[0],) + coef.shape)
    out[:, own:, :] = jnp.broadcast_to(rest[None], (out.shape[0],) + rest.shape)


def unpack_kernel(own, value, coef, lift, bias):
    owners, _, units = value.shape
    depth = coef.shape[0]
    each = depth // own
    for k in range(coef.shape[1] // units):
        coef[:, k * units:(k + 1) * units] = value[k * each:(k + 1) * each, :own, :].reshape(depth, units)
    rows = value.shape[1] - own
    used = lift.shape[0] // rows
    lift[...] = value[:used, own:, :].reshape(lift.shape)
    bias[...] = value[used, own:own + 1, :]


def called(kernel, mebibytes, shapes, *operands, **options):
    return pl.pallas_call(
        kernel,
        out_shape=shapes,
        compiler_params=pltpu.CompilerParams(vmem_limit_bytes=mebibytes * 2 ** 20),
        **options,
    )(*operands)


def shards(tokens_in, cotangent, lift_weight, lift_bias, coef_weight):
    inputs = tokens_in[0]
    grads = cotangent[0]
    length, channels = inputs.shape
    lags = LAG_BLOCKS * length
    features, units = lift_weight.shape
    depth = coef_weight.shape[0]
    blocks_total = lax.axis_size("ctx")

    core = (lax.axis_index("ctx") % CORES).astype(jnp.int32).reshape(1)
    first_cots = moved(grads, -CORES, 0)
    first_tokens = moved(inputs, 0, CORES)

    def real(*shape):
        return jax.ShapeDtypeStruct(shape, jnp.float32)

    def like(value):
        return jax.ShapeDtypeStruct(value.shape, value.dtype)

    scalar = pl.BlockSpec(memory_space=pltpu.SMEM)
    whole = pl.BlockSpec(memory_space=pltpu.VMEM)
    table = odd_table(length)
    split = jnp.asarray(halves(table))
    inverse = jnp.asarray(halves(table.T))
    features_table = lag_features(lags, features)
    embed = jnp.asarray(features_table, jnp.float32)
    embed_turned = jnp.asarray(halves(features_table.T))

    def held(value):
        return pltpu.with_memory_space_constraint(value, pltpu.HBM)

    def room(value):
        return pltpu.VMEM(value.shape, value.dtype)

    def sems(count):
        return pltpu.SemaphoreType.DMA((count,))

    far_off = pl.BlockSpec(memory_space=pltpu.HBM)
    bias_row = lift_bias[None]
    first_operands = (embed, lift_weight, bias_row, inverse, split, grads, inputs, coef_weight)
    net, slope, coef, mix, split, crossing = called(
        prepare_kernel,
        24,
        (
            real((LAG_BLOCKS + 1) * units, 2 * length),
            real(lags, units),
            real(depth, channels),
            real(2 * length, units),
            like(split),
            like(grads),
        ),
        core,
        *[held(value) for value in first_operands],
        in_specs=[scalar] + [far_off] * 8,
        scratch_shapes=[room(value) for value in first_operands if value is not split] + [sems(8)],
    )
    crossed = moved(crossing, CORES, -CORES)
    ahead1 = swapped(
        called(
            swap_kernel, 8, like(grads), core, first_cots, crossing, first_tokens,
            in_specs=[scalar] + [whole] * 2 + [pl.BlockSpec(memory_space=pl.ANY)],
        )
    )

    planes, columns = device_groups()
    owners, slots = len(planes[0]), len(columns[0])
    own = channels // units * depth // owners
    lift_rows = TILE * 2 ** max(0, math.ceil(math.log2((features + TILE) / (TILE * owners))))
    scale = 1.0 / math.sqrt(lax.axis_size("dp") * length * blocks_total) / length

    def rows_of(count):
        return real(count, own + lift_rows, units)

    packed, ahead1, ahead2 = called(
        lambda *refs: lag_kernel(scale, own, lift_rows, *refs),
        32,
        (
            pltpu.HBM((owners, own + lift_rows, units), jnp.float32),
            pltpu.HBM(grads.shape, grads.dtype),
            pltpu.HBM(grads.shape, grads.dtype),
        ),
        core, first_cots, crossed, first_tokens, ahead1, coef, mix, net, slope, split,
        *[held(value) for value in (inputs, coef_weight, inverse, embed_turned)],
        in_specs=[scalar] + [whole] * 9 + [far_off] * 4,
        out_specs=[far_off] * 3,
        scratch_shapes=[room(value) for value in (inputs, coef_weight, inverse, embed_turned, grads)]
        + [pltpu.VMEM((owners, rows, units), jnp.float32) for rows in (own, lift_rows)]
        + [sems(8)],
    )
    summed = exchanged(packed, ("dp", "ctx"), planes)
    kept = ((2 * length, channels), (2, 2 * length, channels))
    early, coefs, ahead2 = called(
        early_tokens_kernel,
        24,
        tuple(pltpu.HBM(shape, jnp.float32) for shape in kept) + (pltpu.HBM(ahead2.shape, ahead2.dtype),),
        net, split,
        *[held(value) for value in (grads, ahead1, ahead2, coef_weight)],
        in_specs=[whole] * 2 + [far_off] * 4,
        out_specs=[far_off] * 3,
        scratch_shapes=[room(value) for value in (grads, ahead1, ahead2, coef_weight)]
        + [pltpu.VMEM(shape, jnp.float32) for shape in kept]
        + [sems(4)],
    )
    summed = called(
        first_sum_kernel,
        8,
        rows_of(slots),
        summed, held(early),
        in_specs=[whole, far_off],
    )
    last = shifted(ahead2, "ctx", -CORES)
    ahead3 = swapped(
        called(choose_kernel, 8, like(last), core, last, ahead2, in_specs=[scalar] + [whole] * 2)
    )
    summed = exchanged(summed, ("ctx", "ch"), columns)
    line = lax.axis_index("ch").astype(jnp.int32).reshape(1)
    spread, ahead3 = called(
        lambda *refs: second_sum_kernel(own, *refs),
        8,
        (rows_of(owners), like(last)),
        line, summed, ahead3,
        in_specs=[scalar] + [whole] * 2,
    )
    full = exchanged(spread, ("dp", "ctx"), planes)
    coef_weight_grad, lift_weight_grad, lift_bias_grad = called(
        lambda *refs: unpack_kernel(own, *refs),
        8,
        (
            jax.ShapeDtypeStruct((depth, channels), jnp.float32),
            jax.ShapeDtypeStruct((features, units), jnp.float32),
            jax.ShapeDtypeStruct((1, units), jnp.float32),
        ),
        full,
    )
    tokens_grad = called(
        late_tokens_kernel,
        16,
        real(length, channels),
        ahead3, last, split,
        *[held(value) for value in (early, coefs, inverse)],
        in_specs=[whole] * 3 + [far_off] * 3,
        scratch_shapes=[room(value) for value in (early, coefs, inverse)] + [sems(3)],
    )
    return (tokens_grad[None], lift_weight_grad, lift_bias_grad[0], coef_weight_grad)


def solution(mesh):
    in_specs = (P("dp", "ctx", "ch"), P("dp", "ctx", "ch"), P(), P(), P(None, "ch"))
    out_specs = (P("dp", "ctx", "ch"), P(), P(), P(None, "ch"))
    return jax.shard_map(shards, mesh=mesh, in_specs=in_specs, out_specs=out_specs, check_vma=False)
```

```python
import math

import jax
import jax.numpy as jnp
import numpy as np
from jax import lax
from jax.experimental import pallas as pl
from jax.experimental.pallas import tpu as pltpu
from jax.sharding import PartitionSpec as P

LAG_BLOCKS = 4
Z_HIGH = 4
CORES = 2


def shifted(value, axis, steps):
    count = lax.axis_size(axis)
    initial, last = (max(0, -steps), min(count, count - steps))
    return lax.ppermute(value, axis, [(source, source + steps) for source in range(initial, last)])


def swapped(value):
    count = lax.axis_size("ctx")
    return lax.ppermute(value, "ctx", [(i, i ^ 1) for i in range(count)])


def lag_features(count, width):
    halfway = width // 2
    rates = np.float32(3.0) * np.exp(np.arange(halfway, dtype=np.float32) * np.float32(-math.log(count) / halfway))
    angles = np.arange(count, dtype=np.float32)[:, None] * rates[None, :].astype(np.float32)
    angles = angles.astype(np.float32).astype(np.float64)
    return np.concatenate([np.sin(angles), np.cos(angles)], axis=1)


def odd_table(length):
    phase = (2 * np.arange(length)[:, None] + 1) * np.arange(length)[None, :] % (4 * length)
    angles = phase * (2.0 * math.pi / (4 * length))
    return np.concatenate([np.cos(angles), -np.sin(angles)], axis=0)


def halves(table):
    upper = table.astype(jnp.bfloat16)
    lower = (table - upper.astype(np.float64)).astype(jnp.bfloat16)
    return np.concatenate([upper, lower], axis=0)


def turned(value, axis):
    rows = value.shape[axis] // 2
    shape = [1, 1]
    shape[axis] = rows
    parity = jnp.where(lax.broadcasted_iota(jnp.int32, shape, axis) % 2 == 0, 1.0, -1.0)
    real, imag = jnp.split(value, 2, axis=axis)
    return jnp.concatenate([-parity * imag, parity * real], axis=axis)


def device_groups():
    count, rows, lines = lax.axis_size("ctx"), lax.axis_size("dp"), lax.axis_size("ch")
    wide = count // (CORES * Z_HIGH)
    planes = [
        [d * count + (x * Z_HIGH + z) * CORES + c for x in range(wide) for z in range(Z_HIGH) for d in range(rows)]
        for c in range(CORES)
    ]
    columns = [
        [(s * CORES + c) * lines + y for c in range(CORES) for y in range(lines)]
        for s in range(wide * Z_HIGH)
    ]
    return planes, columns


def exchanged(value, axes, groups):
    chunks = value.reshape(len(groups[0]), 1, -1)
    return lax.all_to_all(
        chunks, axes, split_axis=0, concat_axis=0, axis_index_groups=groups, tiled=True
    ).reshape(value.shape)


def parts(value):
    upper = value.astype(jnp.bfloat16)
    return upper, (value - upper.astype(jnp.float32)).astype(jnp.bfloat16)


def times(first, second):
    return jnp.dot(first, second, preferred_element_type=jnp.float32)


def times_stacked(stacked, second):
    rows = stacked.shape[0] // 2
    upper, lower = parts(second)
    both = times(stacked, upper)
    return both[:rows] + both[rows:] + times(stacked[:rows], lower)


def spectrum(table, block):
    both = times(table, block)
    rows = both.shape[0] // 2
    return both[:rows], both[rows:], rows // 2


def packed_spectrum(table, block):
    upper, lower, rows = spectrum(table, block)
    total = upper + lower
    return total[:rows], total[rows:]


def conj_product(first, second):
    real_a, imag_a = first
    real_b, imag_b = second
    return real_a * real_b + imag_a * imag_b, real_a * imag_b - imag_a * real_b


def pair_products(first, second, net, weight):
    units = weight.shape[0]
    pair = jnp.concatenate(conj_product(first, second), axis=0)
    upper, lower = parts(pair)
    net_hi, net_lo = parts(net)
    both = times(jnp.concatenate([net_hi, net_lo], axis=0), upper)
    coef = both[:units] + both[units:] + times(net_hi, lower)
    weight_hi, weight_lo = parts(weight)
    last = (((1,), (1,)), ((), ()))
    both = lax.dot_general(
        upper, jnp.concatenate([weight_hi, weight_lo], axis=0), last, preferred_element_type=jnp.float32
    )
    mix = both[:, :units] + both[:, units:] + lax.dot_general(
        lower, weight_hi, last, preferred_element_type=jnp.float32
    )
    return coef, mix


def started(sems, pairs):
    copies = [
        pltpu.make_async_copy(source, target, sems.at[i]) for i, (source, target) in enumerate(pairs)
    ]
    for copy in copies:
        copy.start()
    return copies


def prepare_kernel(
    embed_in, lift_weight_in, lift_bias_in, inverse_in, split_in, c0_in, x0_in, weight_in,
    net, slope, coef, mix, split,
    embed, lift_weight, lift_bias, inverse, c0, x0, weight, sems,
):
    copies = started(
        sems,
        [
            (embed_in, embed), (lift_weight_in, lift_weight), (lift_bias_in, lift_bias),
            (inverse_in, inverse), (split_in, split), (c0_in, c0), (x0_in, x0), (weight_in, weight),
        ],
    )
    units = lift_weight.shape[1]
    length = inverse.shape[0] // 2
    for copy in copies[:3]:
        copy.wait()
    features = lift_weight.shape[0]
    lift_hi, lift_lo = parts(lift_weight[...])
    preact = (
        times(embed[...], jnp.concatenate([lift_hi, lift_hi], axis=0))
        + times(embed[:, :features], lift_lo)
        + lift_bias[...]
    )
    logistic = jax.nn.sigmoid(preact)
    hidden = preact * logistic
    slope[...] = logistic * (1.0 + preact * (1.0 - logistic))
    rows = jnp.concatenate(
        [hidden[k * length:(k + 1) * length].T for k in range(LAG_BLOCKS)], axis=0
    )
    upper, lower = parts(rows)
    count = rows.shape[0]
    copies[3].wait()
    both = times(jnp.concatenate([upper, lower], axis=0), inverse[:length, :])
    plain = both[:count] + both[count:] + times(upper, inverse[length:, :])
    moved = turned(plain, 1)
    net[:units, :] = plain[:units]
    net[units:count, :] = plain[units:] + moved[:-units]
    net[count:, :] = moved[-units:]
    for copy in copies[4:]:
        copy.wait()
    own = packed_spectrum(split[...], c0[...])
    source = packed_spectrum(split[...], x0[...])
    coef[...], mix[...] = pair_products(source, own, plain[:units], weight[...])


def halved(ref):
    rows = ref.shape[0] // 2
    return ref[:rows, :], ref[rows:, :]


def lag_kernel(
    scale, own,
    c2, x2, c1, first_coef, first_mix, net, slope, split,
    x0_in, weight_in, inverse_in, embed_in, out, same,
    x0, weight, inverse, embed, packed, sems,
):
    copies = started(
        sems,
        [(x0_in, x0), (weight_in, weight), (inverse_in, inverse), (embed_in, embed), (c1, same)],
    )
    units, channels = weight.shape
    table = split[...]
    next_spec, ahead_spec, back_spec = [packed_spectrum(table, ref[...]) for ref in (c1, c2, x2)]
    for copy in copies[:2]:
        copy.wait()
    in_spec = packed_spectrum(table, x0[...])
    products = [
        (in_spec, next_spec),
        (in_spec, ahead_spec),
        (back_spec, next_spec),
        (back_spec, ahead_spec),
    ]
    coef = first_coef[...]
    mixes = [first_mix[...]]
    for k, (first, second) in enumerate(products, 1):
        part, mix = pair_products(first, second, net[k * units:(k + 1) * units, :], weight[...])
        coef = coef + part
        mixes.append(mix)
    coef = coef * scale
    sides = jnp.concatenate([coef[:, k * units:(k + 1) * units] for k in range(channels // units)], axis=0)
    owners = sides.shape[0] // own
    chunk = packed.shape[0] // owners
    for o in range(owners):
        packed[o * chunk:o * chunk + own, :] = sides[o * own:(o + 1) * own]
    for copy in copies[2:]:
        copy.wait()
    sides = jnp.concatenate(
        [mixes[k] - turned(mixes[k + 1], 0) for k in range(LAG_BLOCKS)], axis=1
    )
    lagged = times_stacked(inverse[...], sides)
    grads = jnp.concatenate(
        [lagged[:, k * units:(k + 1) * units] for k in range(LAG_BLOCKS)], axis=0
    ) * (slope[...] * scale)
    lift = times_stacked(embed[...], grads)
    bias = jnp.sum(grads, axis=0, keepdims=True)
    lift_rows = chunk - own - 1
    for o in range(owners):
        packed[o * chunk + own:(o + 1) * chunk - 1, :] = lift[o * lift_rows:(o + 1) * lift_rows]
        packed[(o + 1) * chunk - 1:(o + 1) * chunk, :] = bias
    copy = pltpu.make_async_copy(packed, out, sems.at[len(copies)])
    copy.start()
    copy.wait()


def early_tokens_kernel(
    c2, net, split, c0_in, c1_in, weight_in, behind, out, coefs_out, same,
    c0, c1, weight, total_kept, coefs, sems,
):
    copies = started(sems, [(c0_in, c0), (c1_in, c1), (weight_in, weight)])
    length = c2.shape[0]
    units = weight.shape[0]
    for copy in copies:
        copy.wait()
    table = split[...]
    weight_hi, weight_lo = parts(weight[...])
    doubled = jnp.concatenate([weight_hi, weight_hi], axis=0)
    specs = [packed_spectrum(table, ref[...]) for ref in (c0, c1, c2)]
    total = None
    for k in range(LAG_BLOCKS + 1):
        net_hi, net_lo = parts(net[k * units:(k + 1) * units, :].T)
        coef = times(jnp.concatenate([net_hi, net_lo], axis=1), doubled) + times(net_hi, weight_lo)
        if k >= len(specs):
            coefs[k - len(specs)] = coef
            continue
        term = conj_product((coef[:length], coef[length:]), specs[k])
        total = term if total is None else (total[0] + term[0], total[1] + term[1])
    total_kept[...] = jnp.concatenate(total, axis=0)
    for copy in started(sems, [(total_kept, out), (coefs, coefs_out), (c2, same)]):
        copy.wait()


def late_tokens_kernel(c3, c4, split, early_in, coefs_in, inverse_in, out, early, coefs, inverse, sems):
    copies = started(sems, [(coefs_in, coefs), (early_in, early), (inverse_in, inverse)])
    table = split[...]
    specs = [packed_spectrum(table, ref[...]) for ref in (c3, c4)]
    copies[0].wait()
    terms = [conj_product(halved(coefs.at[k]), spec) for k, spec in enumerate(specs)]
    copies[1].wait()
    total = [a + b + c for a, b, c in zip(halved(early), *terms)]
    copies[2].wait()
    length = c3.shape[0]
    out[...] = times_stacked(inverse[...], jnp.concatenate(total, axis=0)) * (1.0 / length)


def first_sum_kernel(slots, value, early, out):
    chunk = out.shape[0] // slots
    total = value[:chunk, :]
    for o in range(1, value.shape[0] // chunk):
        total = total + value[o * chunk:(o + 1) * chunk, :]
    for i in range(slots):
        out[i * chunk:(i + 1) * chunk, :] = total


def choose_kernel(core, relayed, block, out):
    out[...] = jnp.where(core[0] == 0, relayed[...].astype(jnp.float32), block[...].astype(jnp.float32)).astype(
        out.dtype
    )


def second_sum_kernel(own, slots, line, value, block, out, same):
    same[...] = block[...]
    lines = slots // CORES
    place = line[0]
    chunk = value.shape[0] // slots
    coef = jnp.zeros((own, value.shape[1]), jnp.float32)
    rest = jnp.zeros((chunk - own, value.shape[1]), jnp.float32)
    for i in range(slots):
        coef = coef + jnp.where(place == i % lines, value[i * chunk:i * chunk + own, :], 0.0)
        rest = rest + value[i * chunk + own:(i + 1) * chunk, :]
    for o in range(out.shape[0] // chunk):
        out[o * chunk:o * chunk + own, :] = coef
        out[o * chunk + own:(o + 1) * chunk, :] = rest


def unpack_kernel(own, owners, value, coef, lift, bias):
    units = value.shape[1]
    chunk = value.shape[0] // owners
    each = coef.shape[0] // own
    rows = chunk - own - 1
    for o in range(owners):
        column, row = o // each, o % each
        coef[row * own:(row + 1) * own, column * units:(column + 1) * units] = value[
            o * chunk:o * chunk + own, :
        ]
        lift[o * rows:(o + 1) * rows, :] = value[o * chunk + own:(o + 1) * chunk - 1, :]
    bias[...] = value[chunk - 1:chunk, :]


def called(kernel, mebibytes, shapes, *operands, **options):
    return pl.pallas_call(
        kernel,
        out_shape=shapes,
        compiler_params=pltpu.CompilerParams(vmem_limit_bytes=mebibytes * 2 ** 20),
        **options,
    )(*operands)


def shards(tokens_in, cotangent, lift_weight, lift_bias, coef_weight):
    inputs = tokens_in[0]
    grads = cotangent[0]
    length, channels = inputs.shape
    lags = LAG_BLOCKS * length
    features, units = lift_weight.shape
    depth = coef_weight.shape[0]
    blocks_total = lax.axis_size("ctx")

    core = (lax.axis_index("ctx") % CORES).astype(jnp.int32).reshape(1)
    ahead2 = shifted(grads, "ctx", -CORES)
    behind2 = shifted(inputs, "ctx", CORES)
    ahead1 = shifted(grads, "ctx", -1)

    def real(*shape):
        return jax.ShapeDtypeStruct(shape, jnp.float32)

    def like(value):
        return jax.ShapeDtypeStruct(value.shape, value.dtype)

    scalar = pl.BlockSpec(memory_space=pltpu.SMEM)
    whole = pl.BlockSpec(memory_space=pltpu.VMEM)
    table = odd_table(length)
    split = jnp.asarray(halves(table))
    inverse = jnp.asarray(halves(table.T))
    features_table = lag_features(lags, features)
    embed = jnp.asarray(halves(features_table.T).T)
    embed_turned = jnp.asarray(halves(features_table.T))

    def held(value):
        return pltpu.with_memory_space_constraint(value, pltpu.HBM)

    def room(value):
        return pltpu.VMEM(value.shape, value.dtype)

    def sems(count):
        return pltpu.SemaphoreType.DMA((count,))

    far_off = pl.BlockSpec(memory_space=pltpu.HBM)
    bias_row = lift_bias[None]
    first_operands = (embed, lift_weight, bias_row, inverse, split, grads, inputs, coef_weight)
    net, slope, coef, mix, split = called(
        prepare_kernel,
        24,
        (
            real((LAG_BLOCKS + 1) * units, 2 * length),
            real(lags, units),
            real(depth, channels),
            real(2 * length, units),
            like(split),
        ),
        *[held(value) for value in first_operands],
        in_specs=[far_off] * 8,
        scratch_shapes=[room(value) for value in first_operands if value is not split] + [sems(8)],
    )
    planes, columns = device_groups()
    owners, slots = len(planes[0]), len(columns[0])
    own = channels // units * depth // owners
    chunk = own + features // owners + 1
    scale = 1.0 / math.sqrt(lax.axis_size("dp") * length * blocks_total) / length

    def rows_of(count):
        return real(count * chunk, units)

    packed, ahead1 = called(
        lambda *refs: lag_kernel(scale, own, *refs),
        32,
        (pltpu.HBM((owners * chunk, units), jnp.float32), pltpu.HBM(ahead1.shape, ahead1.dtype)),
        ahead2, behind2, ahead1, coef, mix, net, slope, split,
        *[held(value) for value in (inputs, coef_weight, inverse, embed_turned)],
        in_specs=[whole] * 8 + [far_off] * 4,
        out_specs=[far_off] * 2,
        scratch_shapes=[room(value) for value in (inputs, coef_weight, inverse, embed_turned)]
        + [pltpu.VMEM((owners * chunk, units), jnp.float32), sems(6)],
    )
    summed = exchanged(packed, ("dp", "ctx"), planes)
    kept = ((2 * length, channels), (2, 2 * length, channels))
    early, coefs, ahead2 = called(
        early_tokens_kernel,
        24,
        tuple(pltpu.HBM(shape, jnp.float32) for shape in kept) + (pltpu.HBM(ahead2.shape, ahead2.dtype),),
        ahead2, net, split,
        *[held(value) for value in (grads, ahead1, coef_weight)],
        behind2,
        in_specs=[whole] * 3 + [far_off] * 3 + [pl.BlockSpec(memory_space=pl.ANY)],
        out_specs=[far_off] * 3,
        scratch_shapes=[room(value) for value in (grads, ahead1, coef_weight)]
        + [pltpu.VMEM(shape, jnp.float32) for shape in kept]
        + [sems(3)],
    )
    summed = called(
        lambda *refs: first_sum_kernel(slots, *refs),
        8,
        rows_of(slots),
        summed, held(early),
        in_specs=[whole, far_off],
    )
    last = shifted(ahead2, "ctx", -CORES)
    ahead3 = swapped(
        called(choose_kernel, 8, like(last), core, last, ahead2, in_specs=[scalar] + [whole] * 2)
    )
    summed = exchanged(summed, ("ctx", "ch"), columns)
    line = lax.axis_index("ch").astype(jnp.int32).reshape(1)
    spread, ahead3 = called(
        lambda *refs: second_sum_kernel(own, slots, *refs),
        8,
        (rows_of(owners), like(last)),
        line, summed, ahead3,
        in_specs=[scalar] + [whole] * 2,
    )
    full = exchanged(spread, ("dp", "ctx"), planes)
    coef_weight_grad, lift_weight_grad, lift_bias_grad = called(
        lambda *refs: unpack_kernel(own, owners, *refs),
        8,
        (
            jax.ShapeDtypeStruct((depth, channels), jnp.float32),
            jax.ShapeDtypeStruct((features, units), jnp.float32),
            jax.ShapeDtypeStruct((1, units), jnp.float32),
        ),
        full,
    )
    tokens_grad = called(
        late_tokens_kernel,
        16,
        real(length, channels),
        ahead3, last, split,
        *[held(value) for value in (early, coefs, inverse)],
        in_specs=[whole] * 3 + [far_off] * 3,
        scratch_shapes=[room(value) for value in (early, coefs, inverse)] + [sems(3)],
    )
    return (tokens_grad[None], lift_weight_grad, lift_bias_grad[0], coef_weight_grad)


def solution(mesh):
    in_specs = (P("dp", "ctx", "ch"), P("dp", "ctx", "ch"), P(), P(), P(None, "ch"))
    out_specs = (P("dp", "ctx", "ch"), P(), P(), P(None, "ch"))
    return jax.shard_map(shards, mesh=mesh, in_specs=in_specs, out_specs=out_specs, check_vma=False)
```

```python
import math

import jax
import jax.numpy as jnp
import numpy as np
from jax import lax
from jax.experimental import pallas as pl
from jax.experimental.pallas import tpu as pltpu
from jax.sharding import PartitionSpec as P

LAG_BLOCKS = 4
Z_HIGH = 4
CORES = 2


def shifted(value, axis, steps):
    count = lax.axis_size(axis)
    initial, last = (max(0, -steps), min(count, count - steps))
    return lax.ppermute(value, axis, [(source, source + steps) for source in range(initial, last)])


def swapped(value):
    count = lax.axis_size("ctx")
    return lax.ppermute(value, "ctx", [(i, i ^ 1) for i in range(count)])


def lag_features(count, width):
    halfway = width // 2
    rates = np.float32(3.0) * np.exp(np.arange(halfway, dtype=np.float32) * np.float32(-math.log(count) / halfway))
    angles = np.arange(count, dtype=np.float32)[:, None] * rates[None, :].astype(np.float32)
    angles = angles.astype(np.float32).astype(np.float64)
    return np.concatenate([np.sin(angles), np.cos(angles)], axis=1)


def odd_table(length):
    phase = (2 * np.arange(length)[:, None] + 1) * np.arange(length)[None, :] % (4 * length)
    angles = phase * (2.0 * math.pi / (4 * length))
    return np.concatenate([np.cos(angles), -np.sin(angles)], axis=0)


def halves(table):
    upper = table.astype(jnp.bfloat16)
    lower = (table - upper.astype(np.float64)).astype(jnp.bfloat16)
    return np.concatenate([upper, lower], axis=0)


def turned(value, axis):
    rows = value.shape[axis] // 2
    shape = [1, 1]
    shape[axis] = rows
    parity = jnp.where(lax.broadcasted_iota(jnp.int32, shape, axis) % 2 == 0, 1.0, -1.0)
    real, imag = jnp.split(value, 2, axis=axis)
    return jnp.concatenate([-parity * imag, parity * real], axis=axis)


def device_groups():
    count, rows, lines = lax.axis_size("ctx"), lax.axis_size("dp"), lax.axis_size("ch")
    wide = count // (CORES * Z_HIGH)
    planes = [
        [d * count + (x * Z_HIGH + z) * CORES + c for x in range(wide) for z in range(Z_HIGH) for d in range(rows)]
        for c in range(CORES)
    ]
    columns = [
        [(s * CORES + c) * lines + y for c in range(CORES) for y in range(lines)]
        for s in range(wide * Z_HIGH)
    ]
    return planes, columns


def exchanged(value, axes, groups):
    chunks = value.reshape(len(groups[0]), 1, -1)
    return lax.all_to_all(
        chunks, axes, split_axis=0, concat_axis=0, axis_index_groups=groups, tiled=True
    ).reshape(value.shape)


def parts(value):
    upper = value.astype(jnp.bfloat16)
    return upper, (value - upper.astype(jnp.float32)).astype(jnp.bfloat16)


def times(first, second):
    return jnp.dot(first, second, preferred_element_type=jnp.float32)


def times_stacked(stacked, second):
    rows = stacked.shape[0] // 2
    upper, lower = parts(second)
    both = times(stacked, upper)
    return both[:rows] + both[rows:] + times(stacked[:rows], lower)


def spectrum(table, block):
    both = times(table, block)
    rows = both.shape[0] // 2
    return both[:rows], both[rows:], rows // 2


def packed_spectrum(table, block):
    upper, lower, rows = spectrum(table, block)
    total = upper + lower
    return total[:rows], total[rows:]


def conj_product(first, second):
    real_a, imag_a = first
    real_b, imag_b = second
    return real_a * real_b + imag_a * imag_b, real_a * imag_b - imag_a * real_b


def pair_products(first, second, net, weight):
    units = weight.shape[0]
    pair = jnp.concatenate(conj_product(first, second), axis=0)
    upper, lower = parts(pair)
    net_hi, net_lo = parts(net)
    both = times(jnp.concatenate([net_hi, net_lo], axis=0), upper)
    coef = both[:units] + both[units:] + times(net_hi, lower)
    weight_hi, weight_lo = parts(weight)
    last = (((1,), (1,)), ((), ()))
    both = lax.dot_general(
        upper, jnp.concatenate([weight_hi, weight_lo], axis=0), last, preferred_element_type=jnp.float32
    )
    mix = both[:, :units] + both[:, units:] + lax.dot_general(
        lower, weight_hi, last, preferred_element_type=jnp.float32
    )
    return coef, mix


def started(sems, pairs):
    copies = [
        pltpu.make_async_copy(source, target, sems.at[i]) for i, (source, target) in enumerate(pairs)
    ]
    for copy in copies:
        copy.start()
    return copies


def prepare_kernel(
    embed_in, lift_weight_in, lift_bias_in, inverse_in, split_in, c0_in, x0_in, weight_in,
    net, slope, coef, mix, split,
    embed, lift_weight, lift_bias, inverse, c0, x0, weight, sems,
):
    copies = started(
        sems,
        [
            (embed_in, embed), (lift_weight_in, lift_weight), (lift_bias_in, lift_bias),
            (inverse_in, inverse), (split_in, split), (c0_in, c0), (x0_in, x0), (weight_in, weight),
        ],
    )
    units = lift_weight.shape[1]
    length = inverse.shape[0] // 2
    for copy in copies[:3]:
        copy.wait()
    features = lift_weight.shape[0]
    lift_hi, lift_lo = parts(lift_weight[...])
    preact = (
        times(embed[...], jnp.concatenate([lift_hi, lift_hi], axis=0))
        + times(embed[:, :features], lift_lo)
        + lift_bias[...]
    )
    logistic = jax.nn.sigmoid(preact)
    hidden = preact * logistic
    slope[...] = logistic * (1.0 + preact * (1.0 - logistic))
    rows = jnp.concatenate(
        [hidden[k * length:(k + 1) * length].T for k in range(LAG_BLOCKS)], axis=0
    )
    upper, lower = parts(rows)
    count = rows.shape[0]
    copies[3].wait()
    both = times(jnp.concatenate([upper, lower], axis=0), inverse[:length, :])
    plain = both[:count] + both[count:] + times(upper, inverse[length:, :])
    moved = turned(plain, 1)
    net[:units, :] = plain[:units]
    net[units:count, :] = plain[units:] + moved[:-units]
    net[count:, :] = moved[-units:]
    for copy in copies[4:]:
        copy.wait()
    own = packed_spectrum(split[...], c0[...])
    source = packed_spectrum(split[...], x0[...])
    coef[...], mix[...] = pair_products(source, own, plain[:units], weight[...])


def halved(ref):
    rows = ref.shape[0] // 2
    return ref[:rows, :], ref[rows:, :]


def lag_kernel(
    scale, own,
    c2, x2, c1, first_coef, first_mix, net, slope, split,
    x0_in, weight_in, inverse_in, embed_in, out, same,
    x0, weight, inverse, embed, packed, sems,
):
    copies = started(
        sems,
        [(x0_in, x0), (weight_in, weight), (inverse_in, inverse), (embed_in, embed), (c1, same)],
    )
    units, channels = weight.shape
    table = split[...]
    next_spec, ahead_spec, back_spec = [packed_spectrum(table, ref[...]) for ref in (c1, c2, x2)]
    for copy in copies[:2]:
        copy.wait()
    in_spec = packed_spectrum(table, x0[...])
    products = [
        (in_spec, next_spec),
        (in_spec, ahead_spec),
        (back_spec, next_spec),
        (back_spec, ahead_spec),
    ]
    coef = first_coef[...]
    mixes = [first_mix[...]]
    for k, (first, second) in enumerate(products, 1):
        part, mix = pair_products(first, second, net[k * units:(k + 1) * units, :], weight[...])
        coef = coef + part
        mixes.append(mix)
    coef = coef * scale
    sides = jnp.concatenate([coef[:, k * units:(k + 1) * units] for k in range(channels // units)], axis=0)
    owners = sides.shape[0] // own
    chunk = packed.shape[0] // owners
    for o in range(owners):
        packed[o * chunk:o * chunk + own, :] = sides[o * own:(o + 1) * own]
    for copy in copies[2:]:
        copy.wait()
    sides = jnp.concatenate(
        [mixes[k] - turned(mixes[k + 1], 0) for k in range(LAG_BLOCKS)], axis=1
    )
    lagged = times_stacked(inverse[...], sides)
    grads = jnp.concatenate(
        [lagged[:, k * units:(k + 1) * units] for k in range(LAG_BLOCKS)], axis=0
    ) * (slope[...] * scale)
    lift = times_stacked(embed[...], grads)
    bias = jnp.sum(grads, axis=0, keepdims=True)
    lift_rows = chunk - own - 1
    for o in range(owners):
        packed[o * chunk + own:(o + 1) * chunk - 1, :] = lift[o * lift_rows:(o + 1) * lift_rows]
        packed[(o + 1) * chunk - 1:(o + 1) * chunk, :] = bias
    copy = pltpu.make_async_copy(packed, out, sems.at[len(copies)])
    copy.start()
    copy.wait()


def pass_kernel(block, behind, packed, out, sems):
    for copy in started(sems, [(block, out)]):
        copy.wait()


def tokens_kernel(
    c3, c4, net, split, c0_in, c1_in, c2_in, weight_in, inverse_in, out, c0, c1, c2, weight, inverse, sems
):
    copies = started(
        sems, [(weight_in, weight), (c0_in, c0), (c1_in, c1), (c2_in, c2), (inverse_in, inverse)]
    )
    length = c3.shape[0]
    table = split[...]
    units = weight.shape[0]
    specs = [packed_spectrum(table, ref[...]) for ref in (c4, c3)]
    for copy in copies[:4]:
        copy.wait()
    specs += [packed_spectrum(table, ref[...]) for ref in (c2, c1, c0)]
    weight_hi, weight_lo = parts(weight[...])
    doubled = jnp.concatenate([weight_hi, weight_hi], axis=0)
    total = None
    for k, spec in enumerate(reversed(specs)):
        net_hi, net_lo = parts(net[k * units:(k + 1) * units, :].T)
        coef = times(jnp.concatenate([net_hi, net_lo], axis=1), doubled) + times(net_hi, weight_lo)
        term = conj_product((coef[:length], coef[length:]), spec)
        total = term if total is None else (total[0] + term[0], total[1] + term[1])
    copies[4].wait()
    out[...] = times_stacked(inverse[...], jnp.concatenate(total, axis=0)) * (1.0 / length)


def first_sum_kernel(slots, value, block, out):
    chunk = out.shape[0] // slots
    total = value[:chunk, :]
    for o in range(1, value.shape[0] // chunk):
        total = total + value[o * chunk:(o + 1) * chunk, :]
    for i in range(slots):
        out[i * chunk:(i + 1) * chunk, :] = total


def choose_kernel(core, relayed, block, out):
    out[...] = jnp.where(core[0] == 0, relayed[...].astype(jnp.float32), block[...].astype(jnp.float32)).astype(
        out.dtype
    )


def second_sum_kernel(own, slots, line, value, block, out, same):
    same[...] = block[...]
    lines = slots // CORES
    place = line[0]
    chunk = value.shape[0] // slots
    coef = jnp.zeros((own, value.shape[1]), jnp.float32)
    rest = jnp.zeros((chunk - own, value.shape[1]), jnp.float32)
    for i in range(slots):
        coef = coef + jnp.where(place == i % lines, value[i * chunk:i * chunk + own, :], 0.0)
        rest = rest + value[i * chunk + own:(i + 1) * chunk, :]
    for o in range(out.shape[0] // chunk):
        out[o * chunk:o * chunk + own, :] = coef
        out[o * chunk + own:(o + 1) * chunk, :] = rest


def unpack_kernel(own, owners, value, coef, lift, bias):
    units = value.shape[1]
    chunk = value.shape[0] // owners
    each = coef.shape[0] // own
    rows = chunk - own - 1
    for o in range(owners):
        column, row = o // each, o % each
        coef[row * own:(row + 1) * own, column * units:(column + 1) * units] = value[
            o * chunk:o * chunk + own, :
        ]
        lift[o * rows:(o + 1) * rows, :] = value[o * chunk + own:(o + 1) * chunk - 1, :]
    bias[...] = value[chunk - 1:chunk, :]


def called(kernel, mebibytes, shapes, *operands, **options):
    return pl.pallas_call(
        kernel,
        out_shape=shapes,
        compiler_params=pltpu.CompilerParams(vmem_limit_bytes=mebibytes * 2 ** 20),
        **options,
    )(*operands)


def shards(tokens_in, cotangent, lift_weight, lift_bias, coef_weight):
    inputs = tokens_in[0]
    grads = cotangent[0]
    length, channels = inputs.shape
    lags = LAG_BLOCKS * length
    features, units = lift_weight.shape
    depth = coef_weight.shape[0]
    blocks_total = lax.axis_size("ctx")

    core = (lax.axis_index("ctx") % CORES).astype(jnp.int32).reshape(1)
    ahead2 = shifted(grads, "ctx", -CORES)
    behind2 = shifted(inputs, "ctx", CORES)
    ahead1 = shifted(grads, "ctx", -1)

    def real(*shape):
        return jax.ShapeDtypeStruct(shape, jnp.float32)

    def like(value):
        return jax.ShapeDtypeStruct(value.shape, value.dtype)

    scalar = pl.BlockSpec(memory_space=pltpu.SMEM)
    whole = pl.BlockSpec(memory_space=pltpu.VMEM)
    table = odd_table(length)
    split = jnp.asarray(halves(table))
    inverse = jnp.asarray(halves(table.T))
    features_table = lag_features(lags, features)
    embed = jnp.asarray(halves(features_table.T).T)
    embed_turned = jnp.asarray(halves(features_table.T))

    def held(value):
        return pltpu.with_memory_space_constraint(value, pltpu.HBM)

    def room(value):
        return pltpu.VMEM(value.shape, value.dtype)

    def sems(count):
        return pltpu.SemaphoreType.DMA((count,))

    far_off = pl.BlockSpec(memory_space=pltpu.HBM)
    bias_row = lift_bias[None]
    first_operands = (embed, lift_weight, bias_row, inverse, split, grads, inputs, coef_weight)
    net, slope, coef, mix, split = called(
        prepare_kernel,
        24,
        (
            real((LAG_BLOCKS + 1) * units, 2 * length),
            real(lags, units),
            real(depth, channels),
            real(2 * length, units),
            like(split),
        ),
        *[held(value) for value in first_operands],
        in_specs=[far_off] * 8,
        scratch_shapes=[room(value) for value in first_operands if value is not split] + [sems(8)],
    )
    planes, columns = device_groups()
    owners, slots = len(planes[0]), len(columns[0])
    own = channels // units * depth // owners
    chunk = own + features // owners + 1
    scale = 1.0 / math.sqrt(lax.axis_size("dp") * length * blocks_total) / length

    def rows_of(count):
        return real(count * chunk, units)

    packed, ahead1 = called(
        lambda *refs: lag_kernel(scale, own, *refs),
        32,
        (pltpu.HBM((owners * chunk, units), jnp.float32), pltpu.HBM(ahead1.shape, ahead1.dtype)),
        ahead2, behind2, ahead1, coef, mix, net, slope, split,
        *[held(value) for value in (inputs, coef_weight, inverse, embed_turned)],
        in_specs=[whole] * 8 + [far_off] * 4,
        out_specs=[far_off] * 2,
        scratch_shapes=[room(value) for value in (inputs, coef_weight, inverse, embed_turned)]
        + [pltpu.VMEM((owners * chunk, units), jnp.float32), sems(6)],
    )
    summed = exchanged(packed, ("dp", "ctx"), planes)
    either = pl.BlockSpec(memory_space=pl.ANY)
    relayed = called(
        pass_kernel,
        8,
        pltpu.HBM(grads.shape, grads.dtype),
        ahead2, behind2, held(ahead1),
        in_specs=[whole, either, far_off],
        out_specs=far_off,
        scratch_shapes=[sems(1)],
    )
    summed = called(
        lambda *refs: first_sum_kernel(slots, *refs),
        8,
        rows_of(slots),
        summed, held(relayed),
        in_specs=[whole, far_off],
    )
    last = shifted(relayed, "ctx", -CORES)
    ahead3 = swapped(
        called(choose_kernel, 8, like(last), core, last, ahead2, in_specs=[scalar] + [whole] * 2)
    )
    summed = exchanged(summed, ("ctx", "ch"), columns)
    line = lax.axis_index("ch").astype(jnp.int32).reshape(1)
    spread, ahead3 = called(
        lambda *refs: second_sum_kernel(own, slots, *refs),
        8,
        (rows_of(owners), like(last)),
        line, summed, ahead3,
        in_specs=[scalar] + [whole] * 2,
    )
    full = exchanged(spread, ("dp", "ctx"), planes)
    coef_weight_grad, lift_weight_grad, lift_bias_grad = called(
        lambda *refs: unpack_kernel(own, owners, *refs),
        8,
        (
            jax.ShapeDtypeStruct((depth, channels), jnp.float32),
            jax.ShapeDtypeStruct((features, units), jnp.float32),
            jax.ShapeDtypeStruct((1, units), jnp.float32),
        ),
        full,
    )
    tokens_grad = called(
        tokens_kernel,
        24,
        real(length, channels),
        ahead3, last, net, split,
        *[held(value) for value in (grads, ahead1, relayed, coef_weight, inverse)],
        in_specs=[whole] * 4 + [far_off] * 5,
        scratch_shapes=[room(value) for value in (grads, ahead1, relayed, coef_weight, inverse)] + [sems(5)],
    )
    return (tokens_grad[None], lift_weight_grad, lift_bias_grad[0], coef_weight_grad)


def solution(mesh):
    in_specs = (P("dp", "ctx", "ch"), P("dp", "ctx", "ch"), P(), P(), P(None, "ch"))
    out_specs = (P("dp", "ctx", "ch"), P(), P(), P(None, "ch"))
    return jax.shard_map(shards, mesh=mesh, in_specs=in_specs, out_specs=out_specs, check_vma=False)
```

```python
import math

import jax
import jax.numpy as jnp
import numpy as np
from jax import lax
from jax.experimental import pallas as pl
from jax.experimental.pallas import tpu as pltpu
from jax.sharding import PartitionSpec as P

LAG_BLOCKS = 4
Z_HIGH = 4
CORES = 2


def shifted(value, axis, steps):
    count = lax.axis_size(axis)
    initial, last = (max(0, -steps), min(count, count - steps))
    return lax.ppermute(value, axis, [(source, source + steps) for source in range(initial, last)])


def moved(value, even, odd):
    count = lax.axis_size("ctx")
    pairs = [(i, i + (odd if i % CORES else even)) for i in range(count)]
    return lax.ppermute(value, "ctx", [(i, j) for i, j in pairs if i != j and 0 <= j < count])


def swapped(value):
    count = lax.axis_size("ctx")
    return lax.ppermute(value, "ctx", [(i, i ^ 1) for i in range(count)])


def lag_features(count, width):
    halfway = width // 2
    rates = np.float32(3.0) * np.exp(np.arange(halfway, dtype=np.float32) * np.float32(-math.log(count) / halfway))
    angles = np.arange(count, dtype=np.float32)[:, None] * rates[None, :].astype(np.float32)
    angles = angles.astype(np.float32).astype(np.float64)
    return np.concatenate([np.sin(angles), np.cos(angles)], axis=1)


def odd_table(length):
    phase = (2 * np.arange(length)[:, None] + 1) * np.arange(length)[None, :] % (4 * length)
    angles = phase * (2.0 * math.pi / (4 * length))
    return np.concatenate([np.cos(angles), -np.sin(angles)], axis=0)


def halves(table):
    upper = table.astype(jnp.bfloat16)
    lower = (table - upper.astype(np.float64)).astype(jnp.bfloat16)
    return np.concatenate([upper, lower], axis=0)


def turned(value, axis):
    rows = value.shape[axis] // 2
    shape = [1, 1]
    shape[axis] = rows
    parity = jnp.where(lax.broadcasted_iota(jnp.int32, shape, axis) % 2 == 0, 1.0, -1.0)
    real, imag = jnp.split(value, 2, axis=axis)
    return jnp.concatenate([-parity * imag, parity * real], axis=axis)


def device_groups():
    count, rows, lines = lax.axis_size("ctx"), lax.axis_size("dp"), lax.axis_size("ch")
    wide = count // (CORES * Z_HIGH)
    planes = [
        [d * count + (x * Z_HIGH + z) * CORES + c for x in range(wide) for z in range(Z_HIGH) for d in range(rows)]
        for c in range(CORES)
    ]
    columns = [
        [(s * CORES + c) * lines + y for c in range(CORES) for y in range(lines)]
        for s in range(wide * Z_HIGH)
    ]
    return planes, columns


def exchanged(value, axes, groups):
    chunks = value.reshape(len(groups[0]), 1, -1)
    return lax.all_to_all(
        chunks, axes, split_axis=0, concat_axis=0, axis_index_groups=groups, tiled=True
    ).reshape(value.shape)


def parts(value):
    upper = value.astype(jnp.bfloat16)
    return upper, (value - upper.astype(jnp.float32)).astype(jnp.bfloat16)


def times(first, second):
    return jnp.dot(first, second, preferred_element_type=jnp.float32)


def times_stacked(stacked, second):
    rows = stacked.shape[0] // 2
    upper, lower = parts(second)
    both = times(stacked, upper)
    return both[:rows] + both[rows:] + times(stacked[:rows], lower)


def spectrum(table, block):
    both = times(table, block)
    rows = both.shape[0] // 2
    return both[:rows], both[rows:], rows // 2


def packed_spectrum(table, block):
    upper, lower, rows = spectrum(table, block)
    total = upper + lower
    return total[:rows], total[rows:]


def conj_product(first, second):
    real_a, imag_a = first
    real_b, imag_b = second
    return real_a * real_b + imag_a * imag_b, real_a * imag_b - imag_a * real_b


def pair_products(first, second, net, weight):
    units = weight.shape[0]
    pair = jnp.concatenate(conj_product(first, second), axis=0)
    upper, lower = parts(pair)
    net_hi, net_lo = parts(net)
    both = times(jnp.concatenate([net_hi, net_lo], axis=0), upper)
    coef = both[:units] + both[units:] + times(net_hi, lower)
    weight_hi, weight_lo = parts(weight)
    last = (((1,), (1,)), ((), ()))
    both = lax.dot_general(
        upper, jnp.concatenate([weight_hi, weight_lo], axis=0), last, preferred_element_type=jnp.float32
    )
    mix = both[:, :units] + both[:, units:] + lax.dot_general(
        lower, weight_hi, last, preferred_element_type=jnp.float32
    )
    return coef, mix


def started(sems, pairs):
    copies = [
        pltpu.make_async_copy(source, target, sems.at[i]) for i, (source, target) in enumerate(pairs)
    ]
    for copy in copies:
        copy.start()
    return copies


def selected(flag, one, other):
    return jnp.where(flag, one.astype(jnp.float32), other.astype(jnp.float32)).astype(one.dtype)


def cross_kernel(core, c0_in, x0_in, out, c0, x0, sems):
    for copy in started(sems, [(c0_in, c0), (x0_in, x0)]):
        copy.wait()
    out[...] = selected(core[0] == 0, x0[...], c0[...])


def swap_kernel(core, first_cots, crossing, first_tokens, out):
    out[...] = selected(core[0] == 0, first_cots[...], crossing[...])


def prepare_kernel(
    embed_in, lift_weight_in, lift_bias_in, inverse_in, split_in, c0_in, x0_in, weight_in,
    net, slope, coef, mix, split,
    embed, lift_weight, lift_bias, inverse, c0, x0, weight, sems,
):
    copies = started(
        sems,
        [
            (embed_in, embed), (lift_weight_in, lift_weight), (lift_bias_in, lift_bias),
            (inverse_in, inverse), (split_in, split), (c0_in, c0), (x0_in, x0), (weight_in, weight),
        ],
    )
    units = lift_weight.shape[1]
    length = inverse.shape[0] // 2
    for copy in copies[:3]:
        copy.wait()
    features = lift_weight.shape[0]
    lift_hi, lift_lo = parts(lift_weight[...])
    preact = (
        times(embed[...], jnp.concatenate([lift_hi, lift_hi], axis=0))
        + times(embed[:, :features], lift_lo)
        + lift_bias[...]
    )
    logistic = jax.nn.sigmoid(preact)
    hidden = preact * logistic
    slope[...] = logistic * (1.0 + preact * (1.0 - logistic))
    rows = jnp.concatenate(
        [hidden[k * length:(k + 1) * length].T for k in range(LAG_BLOCKS)], axis=0
    )
    upper, lower = parts(rows)
    count = rows.shape[0]
    copies[3].wait()
    both = times(jnp.concatenate([upper, lower], axis=0), inverse[:length, :])
    plain = both[:count] + both[count:] + times(upper, inverse[length:, :])
    moved = turned(plain, 1)
    net[:units, :] = plain[:units]
    net[units:count, :] = plain[units:] + moved[:-units]
    net[count:, :] = moved[-units:]
    for copy in copies[4:]:
        copy.wait()
    own = packed_spectrum(split[...], c0[...])
    source = packed_spectrum(split[...], x0[...])
    coef[...], mix[...] = pair_products(source, own, plain[:units], weight[...])


def halved(ref):
    rows = ref.shape[0] // 2
    return ref[:rows, :], ref[rows:, :]


def lag_kernel(
    scale, own,
    core, first_cots, crossed, first_tokens, c1, first_coef, first_mix, net, slope, split,
    x0_in, weight_in, inverse_in, embed_in, out, same1, same2,
    x0, weight, inverse, embed, c2, packed, sems,
):
    c2[...] = selected(core[0] == 0, first_cots[...], crossed[...])
    copies = started(
        sems,
        [(x0_in, x0), (weight_in, weight), (inverse_in, inverse), (embed_in, embed), (c1, same1), (c2, same2)],
    )
    units, channels = weight.shape
    table = split[...]
    x2 = selected(core[0] == 0, crossed[...], first_tokens[...])
    next_spec, ahead_spec, back_spec = [packed_spectrum(table, block) for block in (c1[...], c2[...], x2)]
    for copy in copies[:2]:
        copy.wait()
    in_spec = packed_spectrum(table, x0[...])
    products = [
        (in_spec, next_spec),
        (in_spec, ahead_spec),
        (back_spec, next_spec),
        (back_spec, ahead_spec),
    ]
    coef = first_coef[...]
    mixes = [first_mix[...]]
    for k, (first, second) in enumerate(products, 1):
        part, mix = pair_products(first, second, net[k * units:(k + 1) * units, :], weight[...])
        coef = coef + part
        mixes.append(mix)
    coef = coef * scale
    sides = jnp.concatenate([coef[:, k * units:(k + 1) * units] for k in range(channels // units)], axis=0)
    owners = sides.shape[0] // own
    chunk = packed.shape[0] // owners
    for o in range(owners):
        packed[o * chunk:o * chunk + own, :] = sides[o * own:(o + 1) * own]
    for copy in copies[2:]:
        copy.wait()
    sides = jnp.concatenate(
        [mixes[k] - turned(mixes[k + 1], 0) for k in range(LAG_BLOCKS)], axis=1
    )
    lagged = times_stacked(inverse[...], sides)
    grads = jnp.concatenate(
        [lagged[:, k * units:(k + 1) * units] for k in range(LAG_BLOCKS)], axis=0
    ) * (slope[...] * scale)
    lift = times_stacked(embed[...], grads)
    bias = jnp.sum(grads, axis=0, keepdims=True)
    lift_rows = chunk - own - 1
    for o in range(owners):
        packed[o * chunk + own:(o + 1) * chunk - 1, :] = lift[o * lift_rows:(o + 1) * lift_rows]
        packed[(o + 1) * chunk - 1:(o + 1) * chunk, :] = bias
    copy = pltpu.make_async_copy(packed, out, sems.at[len(copies)])
    copy.start()
    copy.wait()


def early_tokens_kernel(
    net, split, c0_in, c1_in, c2_in, weight_in, out, coefs_out, same,
    c0, c1, c2, weight, total_kept, coefs, sems,
):
    copies = started(sems, [(c0_in, c0), (c1_in, c1), (c2_in, c2), (weight_in, weight)])
    length = c2.shape[0]
    units = weight.shape[0]
    for copy in copies:
        copy.wait()
    table = split[...]
    weight_hi, weight_lo = parts(weight[...])
    doubled = jnp.concatenate([weight_hi, weight_hi], axis=0)
    specs = [packed_spectrum(table, ref[...]) for ref in (c0, c1, c2)]
    total = None
    for k in range(LAG_BLOCKS + 1):
        net_hi, net_lo = parts(net[k * units:(k + 1) * units, :].T)
        coef = times(jnp.concatenate([net_hi, net_lo], axis=1), doubled) + times(net_hi, weight_lo)
        if k >= len(specs):
            coefs[k - len(specs)] = coef
            continue
        term = conj_product((coef[:length], coef[length:]), specs[k])
        total = term if total is None else (total[0] + term[0], total[1] + term[1])
    total_kept[...] = jnp.concatenate(total, axis=0)
    for copy in started(sems, [(total_kept, out), (coefs, coefs_out), (c2, same)]):
        copy.wait()


def late_tokens_kernel(c3, c4, split, early_in, coefs_in, inverse_in, out, early, coefs, inverse, sems):
    copies = started(sems, [(coefs_in, coefs), (early_in, early), (inverse_in, inverse)])
    table = split[...]
    specs = [packed_spectrum(table, ref[...]) for ref in (c3, c4)]
    copies[0].wait()
    terms = [conj_product(halved(coefs.at[k]), spec) for k, spec in enumerate(specs)]
    copies[1].wait()
    total = [a + b + c for a, b, c in zip(halved(early), *terms)]
    copies[2].wait()
    length = c3.shape[0]
    out[...] = times_stacked(inverse[...], jnp.concatenate(total, axis=0)) * (1.0 / length)


def first_sum_kernel(slots, value, early, out):
    chunk = out.shape[0] // slots
    total = value[:chunk, :]
    for o in range(1, value.shape[0] // chunk):
        total = total + value[o * chunk:(o + 1) * chunk, :]
    for i in range(slots):
        out[i * chunk:(i + 1) * chunk, :] = total


def choose_kernel(core, relayed, block, out):
    out[...] = selected(core[0] == 0, relayed[...], block[...])


def second_sum_kernel(own, slots, line, value, block, out, same):
    same[...] = block[...]
    lines = slots // CORES
    place = line[0]
    chunk = value.shape[0] // slots
    coef = jnp.zeros((own, value.shape[1]), jnp.float32)
    rest = jnp.zeros((chunk - own, value.shape[1]), jnp.float32)
    for i in range(slots):
        coef = coef + jnp.where(place == i % lines, value[i * chunk:i * chunk + own, :], 0.0)
        rest = rest + value[i * chunk + own:(i + 1) * chunk, :]
    for o in range(out.shape[0] // chunk):
        out[o * chunk:o * chunk + own, :] = coef
        out[o * chunk + own:(o + 1) * chunk, :] = rest


def unpack_kernel(own, owners, value, coef, lift, bias):
    units = value.shape[1]
    chunk = value.shape[0] // owners
    each = coef.shape[0] // own
    rows = chunk - own - 1
    for o in range(owners):
        column, row = o // each, o % each
        coef[row * own:(row + 1) * own, column * units:(column + 1) * units] = value[
            o * chunk:o * chunk + own, :
        ]
        lift[o * rows:(o + 1) * rows, :] = value[o * chunk + own:(o + 1) * chunk - 1, :]
    bias[...] = value[chunk - 1:chunk, :]


def called(kernel, mebibytes, shapes, *operands, **options):
    return pl.pallas_call(
        kernel,
        out_shape=shapes,
        compiler_params=pltpu.CompilerParams(vmem_limit_bytes=mebibytes * 2 ** 20),
        **options,
    )(*operands)


def shards(tokens_in, cotangent, lift_weight, lift_bias, coef_weight):
    inputs = tokens_in[0]
    grads = cotangent[0]
    length, channels = inputs.shape
    lags = LAG_BLOCKS * length
    features, units = lift_weight.shape
    depth = coef_weight.shape[0]
    blocks_total = lax.axis_size("ctx")

    core = (lax.axis_index("ctx") % CORES).astype(jnp.int32).reshape(1)
    first_cots = moved(grads, -CORES, 0)
    first_tokens = moved(inputs, 0, CORES)

    def real(*shape):
        return jax.ShapeDtypeStruct(shape, jnp.float32)

    def like(value):
        return jax.ShapeDtypeStruct(value.shape, value.dtype)

    scalar = pl.BlockSpec(memory_space=pltpu.SMEM)
    whole = pl.BlockSpec(memory_space=pltpu.VMEM)
    table = odd_table(length)
    split = jnp.asarray(halves(table))
    inverse = jnp.asarray(halves(table.T))
    features_table = lag_features(lags, features)
    embed = jnp.asarray(halves(features_table.T).T)
    embed_turned = jnp.asarray(halves(features_table.T))

    def held(value):
        return pltpu.with_memory_space_constraint(value, pltpu.HBM)

    def room(value):
        return pltpu.VMEM(value.shape, value.dtype)

    def sems(count):
        return pltpu.SemaphoreType.DMA((count,))

    far_off = pl.BlockSpec(memory_space=pltpu.HBM)
    bias_row = lift_bias[None]
    crossing = called(
        cross_kernel, 8, like(grads), core, held(grads), held(inputs),
        in_specs=[scalar] + [far_off] * 2,
        scratch_shapes=[room(grads), room(inputs), sems(2)],
    )
    crossed = moved(crossing, CORES, -CORES)
    ahead1 = swapped(
        called(
            swap_kernel, 8, like(grads), core, first_cots, crossing, first_tokens,
            in_specs=[scalar] + [whole] * 2 + [pl.BlockSpec(memory_space=pl.ANY)],
        )
    )
    first_operands = (embed, lift_weight, bias_row, inverse, split, grads, inputs, coef_weight)
    net, slope, coef, mix, split = called(
        prepare_kernel,
        24,
        (
            real((LAG_BLOCKS + 1) * units, 2 * length),
            real(lags, units),
            real(depth, channels),
            real(2 * length, units),
            like(split),
        ),
        *[held(value) for value in first_operands],
        in_specs=[far_off] * 8,
        scratch_shapes=[room(value) for value in first_operands if value is not split] + [sems(8)],
    )
    planes, columns = device_groups()
    owners, slots = len(planes[0]), len(columns[0])
    own = channels // units * depth // owners
    chunk = own + features // owners + 1
    scale = 1.0 / math.sqrt(lax.axis_size("dp") * length * blocks_total) / length

    def rows_of(count):
        return real(count * chunk, units)

    packed, ahead1, ahead2 = called(
        lambda *refs: lag_kernel(scale, own, *refs),
        32,
        (
            pltpu.HBM((owners * chunk, units), jnp.float32),
            pltpu.HBM(grads.shape, grads.dtype),
            pltpu.HBM(grads.shape, grads.dtype),
        ),
        core, first_cots, crossed, first_tokens, ahead1, coef, mix, net, slope, split,
        *[held(value) for value in (inputs, coef_weight, inverse, embed_turned)],
        in_specs=[scalar] + [whole] * 9 + [far_off] * 4,
        out_specs=[far_off] * 3,
        scratch_shapes=[room(value) for value in (inputs, coef_weight, inverse, embed_turned, grads)]
        + [pltpu.VMEM((owners * chunk, units), jnp.float32), sems(7)],
    )
    summed = exchanged(packed, ("dp", "ctx"), planes)
    kept = ((2 * length, channels), (2, 2 * length, channels))
    early, coefs, ahead2 = called(
        early_tokens_kernel,
        24,
        tuple(pltpu.HBM(shape, jnp.float32) for shape in kept) + (pltpu.HBM(ahead2.shape, ahead2.dtype),),
        net, split,
        *[held(value) for value in (grads, ahead1, ahead2, coef_weight)],
        in_specs=[whole] * 2 + [far_off] * 4,
        out_specs=[far_off] * 3,
        scratch_shapes=[room(value) for value in (grads, ahead1, ahead2, coef_weight)]
        + [pltpu.VMEM(shape, jnp.float32) for shape in kept]
        + [sems(4)],
    )
    summed = called(
        lambda *refs: first_sum_kernel(slots, *refs),
        8,
        rows_of(slots),
        summed, held(early),
        in_specs=[whole, far_off],
    )
    last = shifted(ahead2, "ctx", -CORES)
    ahead3 = swapped(
        called(choose_kernel, 8, like(last), core, last, ahead2, in_specs=[scalar] + [whole] * 2)
    )
    summed = exchanged(summed, ("ctx", "ch"), columns)
    line = lax.axis_index("ch").astype(jnp.int32).reshape(1)
    spread, ahead3 = called(
        lambda *refs: second_sum_kernel(own, slots, *refs),
        8,
        (rows_of(owners), like(last)),
        line, summed, ahead3,
        in_specs=[scalar] + [whole] * 2,
    )
    full = exchanged(spread, ("dp", "ctx"), planes)
    coef_weight_grad, lift_weight_grad, lift_bias_grad = called(
        lambda *refs: unpack_kernel(own, owners, *refs),
        8,
        (
            jax.ShapeDtypeStruct((depth, channels), jnp.float32),
            jax.ShapeDtypeStruct((features, units), jnp.float32),
            jax.ShapeDtypeStruct((1, units), jnp.float32),
        ),
        full,
    )
    tokens_grad = called(
        late_tokens_kernel,
        16,
        real(length, channels),
        ahead3, last, split,
        *[held(value) for value in (early, coefs, inverse)],
        in_specs=[whole] * 3 + [far_off] * 3,
        scratch_shapes=[room(value) for value in (early, coefs, inverse)] + [sems(3)],
    )
    return (tokens_grad[None], lift_weight_grad, lift_bias_grad[0], coef_weight_grad)


def solution(mesh):
    in_specs = (P("dp", "ctx", "ch"), P("dp", "ctx", "ch"), P(), P(), P(None, "ch"))
    out_specs = (P("dp", "ctx", "ch"), P(), P(), P(None, "ch"))
    return jax.shard_map(shards, mesh=mesh, in_specs=in_specs, out_specs=out_specs, check_vma=False)
```

```python
import math

import jax
import jax.numpy as jnp
import numpy as np
from jax import lax
from jax.experimental import pallas as pl
from jax.experimental.pallas import tpu as pltpu
from jax.sharding import PartitionSpec as P

LAG_BLOCKS = 4
Z_HIGH = 4
CORES = 2


def shifted(value, axis, steps):
    count = lax.axis_size(axis)
    initial, last = (max(0, -steps), min(count, count - steps))
    return lax.ppermute(value, axis, [(source, source + steps) for source in range(initial, last)])


def swapped(value):
    count = lax.axis_size("ctx")
    return lax.ppermute(value, "ctx", [(i, i ^ 1) for i in range(count)])


def lag_features(count, width):
    halfway = width // 2
    rates = np.float32(3.0) * np.exp(np.arange(halfway, dtype=np.float32) * np.float32(-math.log(count) / halfway))
    angles = np.arange(count, dtype=np.float32)[:, None] * rates[None, :].astype(np.float32)
    angles = angles.astype(np.float32).astype(np.float64)
    return np.concatenate([np.sin(angles), np.cos(angles)], axis=1)


def odd_table(length):
    phase = (2 * np.arange(length)[:, None] + 1) * np.arange(length)[None, :] % (4 * length)
    angles = phase * (2.0 * math.pi / (4 * length))
    return np.concatenate([np.cos(angles), -np.sin(angles)], axis=0)


def halves(table):
    upper = table.astype(jnp.bfloat16)
    lower = (table - upper.astype(np.float64)).astype(jnp.bfloat16)
    return np.concatenate([upper, lower], axis=0)


def turned(value, axis):
    rows = value.shape[axis] // 2
    shape = [1, 1]
    shape[axis] = rows
    parity = jnp.where(lax.broadcasted_iota(jnp.int32, shape, axis) % 2 == 0, 1.0, -1.0)
    real, imag = jnp.split(value, 2, axis=axis)
    return jnp.concatenate([-parity * imag, parity * real], axis=axis)


def device_groups():
    count, rows, lines = lax.axis_size("ctx"), lax.axis_size("dp"), lax.axis_size("ch")
    wide = count // (CORES * Z_HIGH)
    planes = [
        [d * count + (x * Z_HIGH + z) * CORES + c for x in range(wide) for z in range(Z_HIGH) for d in range(rows)]
        for c in range(CORES)
    ]
    columns = [
        [(s * CORES + c) * lines + y for c in range(CORES) for y in range(lines)]
        for s in range(wide * Z_HIGH)
    ]
    return planes, columns


def exchanged(value, axes, groups):
    chunks = value.reshape(len(groups[0]), 1, -1)
    return lax.all_to_all(
        chunks, axes, split_axis=0, concat_axis=0, axis_index_groups=groups, tiled=True
    ).reshape(value.shape)


def parts(value):
    upper = value.astype(jnp.bfloat16)
    return upper, (value - upper.astype(jnp.float32)).astype(jnp.bfloat16)


def times(first, second):
    return jnp.dot(first, second, preferred_element_type=jnp.float32)


def times_stacked(stacked, second):
    rows = stacked.shape[0] // 2
    upper, lower = parts(second)
    both = times(stacked, upper)
    return both[:rows] + both[rows:] + times(stacked[:rows], lower)


def spectrum(table, block):
    both = times(table, block)
    rows = both.shape[0] // 2
    return both[:rows], both[rows:], rows // 2


def packed_spectrum(table, block):
    upper, lower, rows = spectrum(table, block)
    total = upper + lower
    return total[:rows], total[rows:]


def conj_product(first, second):
    real_a, imag_a = first
    real_b, imag_b = second
    return real_a * real_b + imag_a * imag_b, real_a * imag_b - imag_a * real_b


def pair_products(first, second, net, weight):
    units = weight.shape[0]
    pair = jnp.concatenate(conj_product(first, second), axis=0)
    upper, lower = parts(pair)
    net_hi, net_lo = parts(net)
    both = times(jnp.concatenate([net_hi, net_lo], axis=0), upper)
    coef = both[:units] + both[units:] + times(net_hi, lower)
    weight_hi, weight_lo = parts(weight)
    last = (((1,), (1,)), ((), ()))
    both = lax.dot_general(
        upper, jnp.concatenate([weight_hi, weight_lo], axis=0), last, preferred_element_type=jnp.float32
    )
    mix = both[:, :units] + both[:, units:] + lax.dot_general(
        lower, weight_hi, last, preferred_element_type=jnp.float32
    )
    return coef, mix


def started(sems, pairs):
    copies = [
        pltpu.make_async_copy(source, target, sems.at[i]) for i, (source, target) in enumerate(pairs)
    ]
    for copy in copies:
        copy.start()
    return copies


def prepare_kernel(
    embed_in, lift_weight_in, lift_bias_in, inverse_in, split_in, c0_in, x0_in, weight_in,
    net, slope, coef, mix, split,
    embed, lift_weight, lift_bias, inverse, c0, x0, weight, sems,
):
    copies = started(
        sems,
        [
            (embed_in, embed), (lift_weight_in, lift_weight), (lift_bias_in, lift_bias),
            (inverse_in, inverse), (split_in, split), (c0_in, c0), (x0_in, x0), (weight_in, weight),
        ],
    )
    units = lift_weight.shape[1]
    length = inverse.shape[0] // 2
    for copy in copies[:3]:
        copy.wait()
    features = lift_weight.shape[0]
    lift_hi, lift_lo = parts(lift_weight[...])
    preact = (
        times(embed[...], jnp.concatenate([lift_hi, lift_hi], axis=0))
        + times(embed[:, :features], lift_lo)
        + lift_bias[...]
    )
    logistic = jax.nn.sigmoid(preact)
    hidden = preact * logistic
    slope[...] = logistic * (1.0 + preact * (1.0 - logistic))
    rows = jnp.concatenate(
        [hidden[k * length:(k + 1) * length].T for k in range(LAG_BLOCKS)], axis=0
    )
    upper, lower = parts(rows)
    count = rows.shape[0]
    copies[3].wait()
    both = times(jnp.concatenate([upper, lower], axis=0), inverse[:length, :])
    plain = both[:count] + both[count:] + times(upper, inverse[length:, :])
    moved = turned(plain, 1)
    net[:units, :] = plain[:units]
    net[units:count, :] = plain[units:] + moved[:-units]
    net[count:, :] = moved[-units:]
    for copy in copies[4:]:
        copy.wait()
    own = packed_spectrum(split[...], c0[...])
    source = packed_spectrum(split[...], x0[...])
    coef[...], mix[...] = pair_products(source, own, plain[:units], weight[...])


def halved(ref):
    rows = ref.shape[0] // 2
    return ref[:rows, :], ref[rows:, :]


def lag_kernel(
    scale, own,
    c2, x2, c1, first_coef, first_mix, net, slope, split,
    x0_in, weight_in, inverse_in, embed_in, out, same,
    x0, weight, inverse, embed, packed, sems,
):
    copies = started(
        sems,
        [(x0_in, x0), (weight_in, weight), (inverse_in, inverse), (embed_in, embed), (c1, same)],
    )
    units, channels = weight.shape
    table = split[...]
    next_spec, ahead_spec, back_spec = [packed_spectrum(table, ref[...]) for ref in (c1, c2, x2)]
    for copy in copies[:2]:
        copy.wait()
    in_spec = packed_spectrum(table, x0[...])
    products = [
        (in_spec, next_spec),
        (in_spec, ahead_spec),
        (back_spec, next_spec),
        (back_spec, ahead_spec),
    ]
    coef = first_coef[...]
    mixes = [first_mix[...]]
    for k, (first, second) in enumerate(products, 1):
        part, mix = pair_products(first, second, net[k * units:(k + 1) * units, :], weight[...])
        coef = coef + part
        mixes.append(mix)
    coef = coef * scale
    sides = jnp.concatenate([coef[:, k * units:(k + 1) * units] for k in range(channels // units)], axis=0)
    owners = sides.shape[0] // own
    chunk = packed.shape[0] // owners
    for o in range(owners):
        packed[o * chunk:o * chunk + own, :] = sides[o * own:(o + 1) * own]
    for copy in copies[2:]:
        copy.wait()
    sides = jnp.concatenate(
        [mixes[k] - turned(mixes[k + 1], 0) for k in range(LAG_BLOCKS)], axis=1
    )
    lagged = times_stacked(inverse[...], sides)
    grads = jnp.concatenate(
        [lagged[:, k * units:(k + 1) * units] for k in range(LAG_BLOCKS)], axis=0
    ) * (slope[...] * scale)
    lift = times_stacked(embed[...], grads)
    bias = jnp.sum(grads, axis=0, keepdims=True)
    lift_rows = chunk - own - 1
    for o in range(owners):
        packed[o * chunk + own:(o + 1) * chunk - 1, :] = lift[o * lift_rows:(o + 1) * lift_rows]
        packed[(o + 1) * chunk - 1:(o + 1) * chunk, :] = bias
    copy = pltpu.make_async_copy(packed, out, sems.at[len(copies)])
    copy.start()
    copy.wait()


def pass_kernel(block, behind, packed, out, sems):
    for copy in started(sems, [(block, out)]):
        copy.wait()


def tokens_kernel(
    c3, c4, net, split, c0_in, c1_in, c2_in, weight_in, inverse_in, out, c0, c1, c2, weight, inverse, sems
):
    copies = started(
        sems, [(weight_in, weight), (c0_in, c0), (c1_in, c1), (c2_in, c2), (inverse_in, inverse)]
    )
    length = c3.shape[0]
    table = split[...]
    units = weight.shape[0]
    specs = [packed_spectrum(table, ref[...]) for ref in (c4, c3)]
    for copy in copies[:4]:
        copy.wait()
    specs += [packed_spectrum(table, ref[...]) for ref in (c2, c1, c0)]
    weight_hi, weight_lo = parts(weight[...])
    doubled = jnp.concatenate([weight_hi, weight_hi], axis=0)
    total = None
    for k, spec in enumerate(reversed(specs)):
        net_hi, net_lo = parts(net[k * units:(k + 1) * units, :].T)
        coef = times(jnp.concatenate([net_hi, net_lo], axis=1), doubled) + times(net_hi, weight_lo)
        term = conj_product((coef[:length], coef[length:]), spec)
        total = term if total is None else (total[0] + term[0], total[1] + term[1])
    copies[4].wait()
    out[...] = times_stacked(inverse[...], jnp.concatenate(total, axis=0)) * (1.0 / length)


def first_sum_kernel(slots, value, block, out):
    chunk = out.shape[0] // slots
    total = value[:chunk, :]
    for o in range(1, value.shape[0] // chunk):
        total = total + value[o * chunk:(o + 1) * chunk, :]
    for i in range(slots):
        out[i * chunk:(i + 1) * chunk, :] = total


def choose_kernel(core, relayed, block, out):
    out[...] = jnp.where(core[0] == 0, relayed[...].astype(jnp.float32), block[...].astype(jnp.float32)).astype(
        out.dtype
    )


def second_sum_kernel(own, slots, line, value, block, out, same):
    same[...] = block[...]
    lines = slots // CORES
    place = line[0]
    chunk = value.shape[0] // slots
    coef = jnp.zeros((own, value.shape[1]), jnp.float32)
    rest = jnp.zeros((chunk - own, value.shape[1]), jnp.float32)
    for i in range(slots):
        coef = coef + jnp.where(place == i % lines, value[i * chunk:i * chunk + own, :], 0.0)
        rest = rest + value[i * chunk + own:(i + 1) * chunk, :]
    for o in range(out.shape[0] // chunk):
        out[o * chunk:o * chunk + own, :] = coef
        out[o * chunk + own:(o + 1) * chunk, :] = rest


def unpack_kernel(own, owners, value, coef, lift, bias):
    units = value.shape[1]
    chunk = value.shape[0] // owners
    each = coef.shape[0] // own
    rows = chunk - own - 1
    for o in range(owners):
        column, row = o // each, o % each
        coef[row * own:(row + 1) * own, column * units:(column + 1) * units] = value[
            o * chunk:o * chunk + own, :
        ]
        lift[o * rows:(o + 1) * rows, :] = value[o * chunk + own:(o + 1) * chunk - 1, :]
    bias[...] = value[chunk - 1:chunk, :]


def called(kernel, mebibytes, shapes, *operands, **options):
    return pl.pallas_call(
        kernel,
        out_shape=shapes,
        compiler_params=pltpu.CompilerParams(vmem_limit_bytes=mebibytes * 2 ** 20),
        **options,
    )(*operands)


def shards(tokens_in, cotangent, lift_weight, lift_bias, coef_weight):
    inputs = tokens_in[0]
    grads = cotangent[0]
    length, channels = inputs.shape
    lags = LAG_BLOCKS * length
    features, units = lift_weight.shape
    depth = coef_weight.shape[0]
    blocks_total = lax.axis_size("ctx")

    core = (lax.axis_index("ctx") % CORES).astype(jnp.int32).reshape(1)
    ahead2 = shifted(grads, "ctx", -CORES)
    behind2 = shifted(inputs, "ctx", CORES)
    ahead1 = shifted(grads, "ctx", -1)

    def real(*shape):
        return jax.ShapeDtypeStruct(shape, jnp.float32)

    def like(value):
        return jax.ShapeDtypeStruct(value.shape, value.dtype)

    scalar = pl.BlockSpec(memory_space=pltpu.SMEM)
    whole = pl.BlockSpec(memory_space=pltpu.VMEM)
    table = odd_table(length)
    split = jnp.asarray(halves(table))
    inverse = jnp.asarray(halves(table.T))
    features_table = lag_features(lags, features)
    embed = jnp.asarray(halves(features_table.T).T)
    embed_turned = jnp.asarray(halves(features_table.T))

    def held(value):
        return pltpu.with_memory_space_constraint(value, pltpu.HBM)

    def room(value):
        return pltpu.VMEM(value.shape, value.dtype)

    def sems(count):
        return pltpu.SemaphoreType.DMA((count,))

    far_off = pl.BlockSpec(memory_space=pltpu.HBM)
    bias_row = lift_bias[None]
    first_operands = (embed, lift_weight, bias_row, inverse, split, grads, inputs, coef_weight)
    net, slope, coef, mix, split = called(
        prepare_kernel,
        24,
        (
            real((LAG_BLOCKS + 1) * units, 2 * length),
            real(lags, units),
            real(depth, channels),
            real(2 * length, units),
            like(split),
        ),
        *[held(value) for value in first_operands],
        in_specs=[far_off] * 8,
        scratch_shapes=[room(value) for value in first_operands if value is not split] + [sems(8)],
    )
    planes, columns = device_groups()
    owners, slots = len(planes[0]), len(columns[0])
    own = channels // units * depth // owners
    chunk = own + features // owners + 1
    scale = 1.0 / math.sqrt(lax.axis_size("dp") * length * blocks_total) / length

    def rows_of(count):
        return real(count * chunk, units)

    packed, ahead1 = called(
        lambda *refs: lag_kernel(scale, own, *refs),
        32,
        (pltpu.HBM((owners * chunk, units), jnp.float32), pltpu.HBM(ahead1.shape, ahead1.dtype)),
        ahead2, behind2, ahead1, coef, mix, net, slope, split,
        *[held(value) for value in (inputs, coef_weight, inverse, embed_turned)],
        in_specs=[whole] * 8 + [far_off] * 4,
        out_specs=[far_off] * 2,
        scratch_shapes=[room(value) for value in (inputs, coef_weight, inverse, embed_turned)]
        + [pltpu.VMEM((owners * chunk, units), jnp.float32), sems(6)],
    )
    summed = exchanged(packed, ("dp", "ctx"), planes)
    either = pl.BlockSpec(memory_space=pl.ANY)
    relayed = called(
        pass_kernel,
        8,
        pltpu.HBM(grads.shape, grads.dtype),
        ahead2, behind2, held(ahead1),
        in_specs=[whole, either, far_off],
        out_specs=far_off,
        scratch_shapes=[sems(1)],
    )
    summed = called(
        lambda *refs: first_sum_kernel(slots, *refs),
        8,
        rows_of(slots),
        summed, held(relayed),
        in_specs=[whole, far_off],
    )
    last = shifted(relayed, "ctx", -CORES)
    ahead3 = swapped(
        called(choose_kernel, 8, like(last), core, last, relayed, in_specs=[scalar] + [whole] * 2)
    )
    summed = exchanged(summed, ("ctx", "ch"), columns)
    line = lax.axis_index("ch").astype(jnp.int32).reshape(1)
    spread, ahead3 = called(
        lambda *refs: second_sum_kernel(own, slots, *refs),
        8,
        (rows_of(owners), like(last)),
        line, summed, ahead3,
        in_specs=[scalar] + [whole] * 2,
    )
    full = exchanged(spread, ("dp", "ctx"), planes)
    coef_weight_grad, lift_weight_grad, lift_bias_grad = called(
        lambda *refs: unpack_kernel(own, owners, *refs),
        8,
        (
            jax.ShapeDtypeStruct((depth, channels), jnp.float32),
            jax.ShapeDtypeStruct((features, units), jnp.float32),
            jax.ShapeDtypeStruct((1, units), jnp.float32),
        ),
        full,
    )
    tokens_grad = called(
        tokens_kernel,
        24,
        real(length, channels),
        ahead3, last, net, split,
        *[held(value) for value in (grads, ahead1, relayed, coef_weight, inverse)],
        in_specs=[whole] * 4 + [far_off] * 5,
        scratch_shapes=[room(value) for value in (grads, ahead1, relayed, coef_weight, inverse)] + [sems(5)],
    )
    return (tokens_grad[None], lift_weight_grad, lift_bias_grad[0], coef_weight_grad)


def solution(mesh):
    in_specs = (P("dp", "ctx", "ch"), P("dp", "ctx", "ch"), P(), P(), P(None, "ch"))
    out_specs = (P("dp", "ctx", "ch"), P(), P(), P(None, "ch"))
    return jax.shard_map(shards, mesh=mesh, in_specs=in_specs, out_specs=out_specs, check_vma=False)
```

```python
import math

import jax
import jax.numpy as jnp
import numpy as np
from jax import lax
from jax.experimental import pallas as pl
from jax.experimental.pallas import tpu as pltpu
from jax.sharding import PartitionSpec as P

LAG_BLOCKS = 4
Z_HIGH = 4
CORES = 2


def shifted(value, axis, steps):
    count = lax.axis_size(axis)
    initial, last = (max(0, -steps), min(count, count - steps))
    return lax.ppermute(value, axis, [(source, source + steps) for source in range(initial, last)])


def swapped(value):
    count = lax.axis_size("ctx")
    return lax.ppermute(value, "ctx", [(i, i ^ 1) for i in range(count)])


def lag_features(count, width):
    halfway = width // 2
    rates = np.float32(3.0) * np.exp(np.arange(halfway, dtype=np.float32) * np.float32(-math.log(count) / halfway))
    angles = np.arange(count, dtype=np.float32)[:, None] * rates[None, :].astype(np.float32)
    angles = angles.astype(np.float32).astype(np.float64)
    return np.concatenate([np.sin(angles), np.cos(angles)], axis=1)


def odd_table(length):
    phase = (2 * np.arange(length)[:, None] + 1) * np.arange(length)[None, :] % (4 * length)
    angles = phase * (2.0 * math.pi / (4 * length))
    return np.concatenate([np.cos(angles), -np.sin(angles)], axis=0)


def halves(table):
    upper = table.astype(jnp.bfloat16)
    lower = (table - upper.astype(np.float64)).astype(jnp.bfloat16)
    return np.concatenate([upper, lower], axis=0)


def turned(value, axis):
    rows = value.shape[axis] // 2
    shape = [1, 1]
    shape[axis] = rows
    parity = jnp.where(lax.broadcasted_iota(jnp.int32, shape, axis) % 2 == 0, 1.0, -1.0)
    real, imag = jnp.split(value, 2, axis=axis)
    return jnp.concatenate([-parity * imag, parity * real], axis=axis)


def device_groups():
    count, rows, lines = lax.axis_size("ctx"), lax.axis_size("dp"), lax.axis_size("ch")
    wide = count // (CORES * Z_HIGH)
    planes = [
        [d * count + (x * Z_HIGH + z) * CORES + c for x in range(wide) for z in range(Z_HIGH) for d in range(rows)]
        for c in range(CORES)
    ]
    columns = [
        [(s * CORES + c) * lines + y for c in range(CORES) for y in range(lines)]
        for s in range(wide * Z_HIGH)
    ]
    return planes, columns


def exchanged(value, axes, groups):
    chunks = value.reshape(len(groups[0]), 1, -1)
    return lax.all_to_all(
        chunks, axes, split_axis=0, concat_axis=0, axis_index_groups=groups, tiled=True
    ).reshape(value.shape)


def parts(value):
    upper = value.astype(jnp.bfloat16)
    return upper, (value - upper.astype(jnp.float32)).astype(jnp.bfloat16)


def times(first, second):
    return jnp.dot(first, second, preferred_element_type=jnp.float32)


def times_stacked(stacked, second):
    rows = stacked.shape[0] // 2
    upper, lower = parts(second)
    both = times(stacked, upper)
    return both[:rows] + both[rows:] + times(stacked[:rows], lower)


def spectrum(table, block):
    both = times(table, block)
    rows = both.shape[0] // 2
    return both[:rows], both[rows:], rows // 2


def packed_spectrum(table, block):
    upper, lower, rows = spectrum(table, block)
    total = upper + lower
    return total[:rows], total[rows:]


def conj_product(first, second):
    real_a, imag_a = first
    real_b, imag_b = second
    return real_a * real_b + imag_a * imag_b, real_a * imag_b - imag_a * real_b


def pair_products(first, second, net, weight):
    units = weight.shape[0]
    pair = jnp.concatenate(conj_product(first, second), axis=0)
    upper, lower = parts(pair)
    net_hi, net_lo = parts(net)
    both = times(jnp.concatenate([net_hi, net_lo], axis=0), upper)
    coef = both[:units] + both[units:] + times(net_hi, lower)
    weight_hi, weight_lo = parts(weight)
    last = (((1,), (1,)), ((), ()))
    both = lax.dot_general(
        upper, jnp.concatenate([weight_hi, weight_lo], axis=0), last, preferred_element_type=jnp.float32
    )
    mix = both[:, :units] + both[:, units:] + lax.dot_general(
        lower, weight_hi, last, preferred_element_type=jnp.float32
    )
    return coef, mix


def started(sems, pairs):
    copies = [
        pltpu.make_async_copy(source, target, sems.at[i]) for i, (source, target) in enumerate(pairs)
    ]
    for copy in copies:
        copy.start()
    return copies


def prepare_kernel(
    embed_in, lift_weight_in, lift_bias_in, inverse_in, split_in, c0_in, x0_in, weight_in,
    net, slope, coef, mix, split,
    embed, lift_weight, lift_bias, inverse, c0, x0, weight, sems,
):
    copies = started(
        sems,
        [
            (embed_in, embed), (lift_weight_in, lift_weight), (lift_bias_in, lift_bias),
            (inverse_in, inverse), (split_in, split), (c0_in, c0), (x0_in, x0), (weight_in, weight),
        ],
    )
    units = lift_weight.shape[1]
    length = inverse.shape[0] // 2
    for copy in copies[:3]:
        copy.wait()
    features = lift_weight.shape[0]
    lift_hi, lift_lo = parts(lift_weight[...])
    preact = (
        times(embed[...], jnp.concatenate([lift_hi, lift_hi], axis=0))
        + times(embed[:, :features], lift_lo)
        + lift_bias[...]
    )
    logistic = jax.nn.sigmoid(preact)
    hidden = preact * logistic
    slope[...] = logistic * (1.0 + preact * (1.0 - logistic))
    rows = jnp.concatenate(
        [hidden[k * length:(k + 1) * length].T for k in range(LAG_BLOCKS)], axis=0
    )
    upper, lower = parts(rows)
    count = rows.shape[0]
    copies[3].wait()
    both = times(jnp.concatenate([upper, lower], axis=0), inverse[:length, :])
    plain = both[:count] + both[count:] + times(upper, inverse[length:, :])
    moved = turned(plain, 1)
    net[:units, :] = plain[:units]
    net[units:count, :] = plain[units:] + moved[:-units]
    net[count:, :] = moved[-units:]
    for copy in copies[4:]:
        copy.wait()
    own = packed_spectrum(split[...], c0[...])
    source = packed_spectrum(split[...], x0[...])
    coef[...], mix[...] = pair_products(source, own, plain[:units], weight[...])


def halved(ref):
    rows = ref.shape[0] // 2
    return ref[:rows, :], ref[rows:, :]


def lag_kernel(
    scale, own,
    c2, x2, c1, first_coef, first_mix, net, slope, split,
    x0_in, weight_in, inverse_in, embed_in, out, same,
    x0, weight, inverse, embed, packed, sems,
):
    copies = started(
        sems,
        [(x0_in, x0), (weight_in, weight), (inverse_in, inverse), (embed_in, embed), (c1, same)],
    )
    units, channels = weight.shape
    table = split[...]
    next_spec, ahead_spec, back_spec = [packed_spectrum(table, ref[...]) for ref in (c1, c2, x2)]
    for copy in copies[:2]:
        copy.wait()
    in_spec = packed_spectrum(table, x0[...])
    products = [
        (in_spec, next_spec),
        (in_spec, ahead_spec),
        (back_spec, next_spec),
        (back_spec, ahead_spec),
    ]
    coef = first_coef[...]
    mixes = [first_mix[...]]
    for k, (first, second) in enumerate(products, 1):
        part, mix = pair_products(first, second, net[k * units:(k + 1) * units, :], weight[...])
        coef = coef + part
        mixes.append(mix)
    coef = coef * scale
    sides = jnp.concatenate([coef[:, k * units:(k + 1) * units] for k in range(channels // units)], axis=0)
    owners = sides.shape[0] // own
    chunk = packed.shape[0] // owners
    for o in range(owners):
        packed[o * chunk:o * chunk + own, :] = sides[o * own:(o + 1) * own]
    for copy in copies[2:]:
        copy.wait()
    sides = jnp.concatenate(
        [mixes[k] - turned(mixes[k + 1], 0) for k in range(LAG_BLOCKS)], axis=1
    )
    lagged = times_stacked(inverse[...], sides)
    grads = jnp.concatenate(
        [lagged[:, k * units:(k + 1) * units] for k in range(LAG_BLOCKS)], axis=0
    ) * (slope[...] * scale)
    lift = times_stacked(embed[...], grads)
    bias = jnp.sum(grads, axis=0, keepdims=True)
    lift_rows = chunk - own - 1
    for o in range(owners):
        packed[o * chunk + own:(o + 1) * chunk - 1, :] = lift[o * lift_rows:(o + 1) * lift_rows]
        packed[(o + 1) * chunk - 1:(o + 1) * chunk, :] = bias
    copy = pltpu.make_async_copy(packed, out, sems.at[len(copies)])
    copy.start()
    copy.wait()


def tokens_terms(net, weight, specs):
    units = weight.shape[0]
    weight_hi, weight_lo = parts(weight)
    doubled = jnp.concatenate([weight_hi, weight_hi], axis=0)
    total = None
    for k, spec in enumerate(specs):
        net_hi, net_lo = parts(net[k * units:(k + 1) * units, :].T)
        coef = times(jnp.concatenate([net_hi, net_lo], axis=1), doubled) + times(net_hi, weight_lo)
        half = coef.shape[0] // 2
        term = conj_product((coef[:half], coef[half:]), spec)
        total = term if total is None else (total[0] + term[0], total[1] + term[1])
    return total


def early_tokens_kernel(
    c2, net, split, c0_in, c1_in, weight_in, behind, out, same,
    c0, c1, weight, total_kept, sems,
):
    copies = started(sems, [(c0_in, c0), (c1_in, c1), (weight_in, weight), (c2, same)])
    for copy in copies[:3]:
        copy.wait()
    table = split[...]
    specs = [packed_spectrum(table, ref[...]) for ref in (c0, c1)]
    total = tokens_terms(net[:len(specs) * weight.shape[0], :], weight[...], specs)
    total_kept[...] = jnp.concatenate(total, axis=0)
    copies[3].wait()
    for copy in started(sems, [(total_kept, out)]):
        copy.wait()


def late_tokens_kernel(
    c3, c4, net, split, c2_in, weight_in, early_in, inverse_in, out, c2, weight, early, inverse, sems
):
    copies = started(sems, [(c2_in, c2), (weight_in, weight), (early_in, early), (inverse_in, inverse)])
    table = split[...]
    later = [packed_spectrum(table, ref[...]) for ref in (c3, c4)]
    for copy in copies[:2]:
        copy.wait()
    specs = [packed_spectrum(table, c2[...])] + later
    done = net.shape[0] - len(specs) * weight.shape[0]
    terms = tokens_terms(net[done:, :], weight[...], specs)
    copies[2].wait()
    total = [a + b for a, b in zip(halved(early), terms)]
    copies[3].wait()
    length = c3.shape[0]
    out[...] = times_stacked(inverse[...], jnp.concatenate(total, axis=0)) * (1.0 / length)


def first_sum_kernel(slots, value, early, out):
    chunk = out.shape[0] // slots
    total = value[:chunk, :]
    for o in range(1, value.shape[0] // chunk):
        total = total + value[o * chunk:(o + 1) * chunk, :]
    for i in range(slots):
        out[i * chunk:(i + 1) * chunk, :] = total


def choose_kernel(core, relayed, block, out):
    out[...] = jnp.where(core[0] == 0, relayed[...].astype(jnp.float32), block[...].astype(jnp.float32)).astype(
        out.dtype
    )


def second_sum_kernel(own, slots, line, value, block, out, same):
    same[...] = block[...]
    lines = slots // CORES
    place = line[0]
    chunk = value.shape[0] // slots
    coef = jnp.zeros((own, value.shape[1]), jnp.float32)
    rest = jnp.zeros((chunk - own, value.shape[1]), jnp.float32)
    for i in range(slots):
        coef = coef + jnp.where(place == i % lines, value[i * chunk:i * chunk + own, :], 0.0)
        rest = rest + value[i * chunk + own:(i + 1) * chunk, :]
    for o in range(out.shape[0] // chunk):
        out[o * chunk:o * chunk + own, :] = coef
        out[o * chunk + own:(o + 1) * chunk, :] = rest


def unpack_kernel(own, owners, value, coef, lift, bias):
    units = value.shape[1]
    chunk = value.shape[0] // owners
    each = coef.shape[0] // own
    rows = chunk - own - 1
    for o in range(owners):
        column, row = o // each, o % each
        coef[row * own:(row + 1) * own, column * units:(column + 1) * units] = value[
            o * chunk:o * chunk + own, :
        ]
        lift[o * rows:(o + 1) * rows, :] = value[o * chunk + own:(o + 1) * chunk - 1, :]
    bias[...] = value[chunk - 1:chunk, :]


def called(kernel, mebibytes, shapes, *operands, **options):
    return pl.pallas_call(
        kernel,
        out_shape=shapes,
        compiler_params=pltpu.CompilerParams(vmem_limit_bytes=mebibytes * 2 ** 20),
        **options,
    )(*operands)


def shards(tokens_in, cotangent, lift_weight, lift_bias, coef_weight):
    inputs = tokens_in[0]
    grads = cotangent[0]
    length, channels = inputs.shape
    lags = LAG_BLOCKS * length
    features, units = lift_weight.shape
    depth = coef_weight.shape[0]
    blocks_total = lax.axis_size("ctx")

    core = (lax.axis_index("ctx") % CORES).astype(jnp.int32).reshape(1)
    ahead2 = shifted(grads, "ctx", -CORES)
    behind2 = shifted(inputs, "ctx", CORES)
    ahead1 = shifted(grads, "ctx", -1)

    def real(*shape):
        return jax.ShapeDtypeStruct(shape, jnp.float32)

    def like(value):
        return jax.ShapeDtypeStruct(value.shape, value.dtype)

    scalar = pl.BlockSpec(memory_space=pltpu.SMEM)
    whole = pl.BlockSpec(memory_space=pltpu.VMEM)
    table = odd_table(length)
    split = jnp.asarray(halves(table))
    inverse = jnp.asarray(halves(table.T))
    features_table = lag_features(lags, features)
    embed = jnp.asarray(halves(features_table.T).T)
    embed_turned = jnp.asarray(halves(features_table.T))

    def held(value):
        return pltpu.with_memory_space_constraint(value, pltpu.HBM)

    def room(value):
        return pltpu.VMEM(value.shape, value.dtype)

    def sems(count):
        return pltpu.SemaphoreType.DMA((count,))

    far_off = pl.BlockSpec(memory_space=pltpu.HBM)
    bias_row = lift_bias[None]
    first_operands = (embed, lift_weight, bias_row, inverse, split, grads, inputs, coef_weight)
    net, slope, coef, mix, split = called(
        prepare_kernel,
        24,
        (
            real((LAG_BLOCKS + 1) * units, 2 * length),
            real(lags, units),
            real(depth, channels),
            real(2 * length, units),
            like(split),
        ),
        *[held(value) for value in first_operands],
        in_specs=[far_off] * 8,
        scratch_shapes=[room(value) for value in first_operands if value is not split] + [sems(8)],
    )
    planes, columns = device_groups()
    owners, slots = len(planes[0]), len(columns[0])
    own = channels // units * depth // owners
    chunk = own + features // owners + 1
    scale = 1.0 / math.sqrt(lax.axis_size("dp") * length * blocks_total) / length

    def rows_of(count):
        return real(count * chunk, units)

    packed, ahead1 = called(
        lambda *refs: lag_kernel(scale, own, *refs),
        32,
        (pltpu.HBM((owners * chunk, units), jnp.float32), pltpu.HBM(ahead1.shape, ahead1.dtype)),
        ahead2, behind2, ahead1, coef, mix, net, slope, split,
        *[held(value) for value in (inputs, coef_weight, inverse, embed_turned)],
        in_specs=[whole] * 8 + [far_off] * 4,
        out_specs=[far_off] * 2,
        scratch_shapes=[room(value) for value in (inputs, coef_weight, inverse, embed_turned)]
        + [pltpu.VMEM((owners * chunk, units), jnp.float32), sems(6)],
    )
    summed = exchanged(packed, ("dp", "ctx"), planes)
    early, ahead2 = called(
        early_tokens_kernel,
        24,
        (pltpu.HBM((2 * length, channels), jnp.float32), pltpu.HBM(ahead2.shape, ahead2.dtype)),
        ahead2, net, split,
        *[held(value) for value in (grads, ahead1, coef_weight)],
        behind2,
        in_specs=[whole] * 3 + [far_off] * 3 + [pl.BlockSpec(memory_space=pl.ANY)],
        out_specs=[far_off] * 2,
        scratch_shapes=[room(value) for value in (grads, ahead1, coef_weight)]
        + [pltpu.VMEM((2 * length, channels), jnp.float32), sems(4)],
    )
    summed = called(
        lambda *refs: first_sum_kernel(slots, *refs),
        8,
        rows_of(slots),
        summed, held(early),
        in_specs=[whole, far_off],
    )
    last = shifted(ahead2, "ctx", -CORES)
    ahead3 = swapped(
        called(choose_kernel, 8, like(last), core, last, ahead2, in_specs=[scalar] + [whole] * 2)
    )
    summed = exchanged(summed, ("ctx", "ch"), columns)
    line = lax.axis_index("ch").astype(jnp.int32).reshape(1)
    spread, ahead3 = called(
        lambda *refs: second_sum_kernel(own, slots, *refs),
        8,
        (rows_of(owners), like(last)),
        line, summed, ahead3,
        in_specs=[scalar] + [whole] * 2,
    )
    full = exchanged(spread, ("dp", "ctx"), planes)
    coef_weight_grad, lift_weight_grad, lift_bias_grad = called(
        lambda *refs: unpack_kernel(own, owners, *refs),
        8,
        (
            jax.ShapeDtypeStruct((depth, channels), jnp.float32),
            jax.ShapeDtypeStruct((features, units), jnp.float32),
            jax.ShapeDtypeStruct((1, units), jnp.float32),
        ),
        full,
    )
    tokens_grad = called(
        late_tokens_kernel,
        24,
        real(length, channels),
        ahead3, last, net, split,
        *[held(value) for value in (ahead2, coef_weight, early, inverse)],
        in_specs=[whole] * 4 + [far_off] * 4,
        scratch_shapes=[room(value) for value in (ahead2, coef_weight, early, inverse)] + [sems(4)],
    )
    return (tokens_grad[None], lift_weight_grad, lift_bias_grad[0], coef_weight_grad)


def solution(mesh):
    in_specs = (P("dp", "ctx", "ch"), P("dp", "ctx", "ch"), P(), P(), P(None, "ch"))
    out_specs = (P("dp", "ctx", "ch"), P(), P(), P(None, "ch"))
    return jax.shard_map(shards, mesh=mesh, in_specs=in_specs, out_specs=out_specs, check_vma=False)
```

```python
import math

import jax
import jax.numpy as jnp
import numpy as np
from jax import lax
from jax.experimental import pallas as pl
from jax.experimental.pallas import tpu as pltpu
from jax.sharding import PartitionSpec as P

LAG_BLOCKS = 4
Z_HIGH = 4
CORES = 2


def shifted(value, axis, steps):
    count = lax.axis_size(axis)
    initial, last = (max(0, -steps), min(count, count - steps))
    return lax.ppermute(value, axis, [(source, source + steps) for source in range(initial, last)])


def swapped(value):
    count = lax.axis_size("ctx")
    return lax.ppermute(value, "ctx", [(i, i ^ 1) for i in range(count)])


def lag_features(count, width):
    halfway = width // 2
    rates = np.float32(3.0) * np.exp(np.arange(halfway, dtype=np.float32) * np.float32(-math.log(count) / halfway))
    angles = np.arange(count, dtype=np.float32)[:, None] * rates[None, :].astype(np.float32)
    angles = angles.astype(np.float32).astype(np.float64)
    return np.concatenate([np.sin(angles), np.cos(angles)], axis=1)


def odd_table(length):
    phase = (2 * np.arange(length)[:, None] + 1) * np.arange(length)[None, :] % (4 * length)
    angles = phase * (2.0 * math.pi / (4 * length))
    return np.concatenate([np.cos(angles), -np.sin(angles)], axis=0)


def halves(table):
    upper = table.astype(jnp.bfloat16)
    lower = (table - upper.astype(np.float64)).astype(jnp.bfloat16)
    return np.concatenate([upper, lower], axis=0)


def turned(value, axis):
    rows = value.shape[axis] // 2
    shape = [1, 1]
    shape[axis] = rows
    parity = jnp.where(lax.broadcasted_iota(jnp.int32, shape, axis) % 2 == 0, 1.0, -1.0)
    real, imag = jnp.split(value, 2, axis=axis)
    return jnp.concatenate([-parity * imag, parity * real], axis=axis)


def device_groups():
    count, rows, lines = lax.axis_size("ctx"), lax.axis_size("dp"), lax.axis_size("ch")
    wide = count // (CORES * Z_HIGH)
    planes = [
        [d * count + (x * Z_HIGH + z) * CORES + c for x in range(wide) for z in range(Z_HIGH) for d in range(rows)]
        for c in range(CORES)
    ]
    columns = [
        [(s * CORES + c) * lines + y for c in range(CORES) for y in range(lines)]
        for s in range(wide * Z_HIGH)
    ]
    return planes, columns


def exchanged(value, axes, groups):
    chunks = value.reshape(len(groups[0]), 1, -1)
    return lax.all_to_all(
        chunks, axes, split_axis=0, concat_axis=0, axis_index_groups=groups, tiled=True
    ).reshape(value.shape)


def parts(value):
    upper = value.astype(jnp.bfloat16)
    return upper, (value - upper.astype(jnp.float32)).astype(jnp.bfloat16)


def times(first, second):
    return jnp.dot(first, second, preferred_element_type=jnp.float32)


def times_stacked(stacked, second):
    rows = stacked.shape[0] // 2
    upper, lower = parts(second)
    both = times(stacked, upper)
    return both[:rows] + both[rows:] + times(stacked[:rows], lower)


def spectrum(table, block):
    both = times(table, block)
    rows = both.shape[0] // 2
    return both[:rows], both[rows:], rows // 2


def packed_spectrum(table, block):
    upper, lower, rows = spectrum(table, block)
    total = upper + lower
    return total[:rows], total[rows:]


def conj_product(first, second):
    real_a, imag_a = first
    real_b, imag_b = second
    return real_a * real_b + imag_a * imag_b, real_a * imag_b - imag_a * real_b


def pair_products(first, second, net, weight):
    units = weight.shape[0]
    pair = jnp.concatenate(conj_product(first, second), axis=0)
    upper, lower = parts(pair)
    net_hi, net_lo = parts(net)
    both = times(jnp.concatenate([net_hi, net_lo], axis=0), upper)
    coef = both[:units] + both[units:] + times(net_hi, lower)
    weight_hi, weight_lo = parts(weight)
    last = (((1,), (1,)), ((), ()))
    both = lax.dot_general(
        upper, jnp.concatenate([weight_hi, weight_lo], axis=0), last, preferred_element_type=jnp.float32
    )
    mix = both[:, :units] + both[:, units:] + lax.dot_general(
        lower, weight_hi, last, preferred_element_type=jnp.float32
    )
    return coef, mix


def started(sems, pairs):
    copies = [
        pltpu.make_async_copy(source, target, sems.at[i]) for i, (source, target) in enumerate(pairs)
    ]
    for copy in copies:
        copy.start()
    return copies


def prepare_kernel(
    embed_in, lift_weight_in, lift_bias_in, inverse_in, split_in,
    net, split, slope,
    embed, lift_weight, lift_bias, inverse, slope_kept, sems,
):
    copies = started(
        sems,
        [
            (embed_in, embed), (lift_weight_in, lift_weight), (lift_bias_in, lift_bias),
            (inverse_in, inverse), (split_in, split),
        ],
    )
    length = inverse.shape[0] // 2
    features, units = lift_weight.shape
    for copy in copies[:3]:
        copy.wait()
    lift_hi, lift_lo = parts(lift_weight[...])
    preact = (
        times(embed[...], jnp.concatenate([lift_hi, lift_hi], axis=0))
        + times(embed[:, :features], lift_lo)
        + lift_bias[...]
    )
    logistic = jax.nn.sigmoid(preact)
    hidden = preact * logistic
    slope_kept[...] = logistic * (1.0 + preact * (1.0 - logistic))
    slope_copy = pltpu.make_async_copy(slope_kept, slope, sems.at[len(copies)])
    slope_copy.start()
    rows = jnp.concatenate(
        [hidden[k * length:(k + 1) * length].T for k in range(LAG_BLOCKS)], axis=0
    )
    upper, lower = parts(rows)
    count = rows.shape[0]
    copies[3].wait()
    both = times(jnp.concatenate([upper, lower], axis=0), inverse[:length, :])
    plain = both[:count] + both[count:] + times(upper, inverse[length:, :])
    moved = turned(plain, 1)
    net[:units, :] = plain[:units]
    net[units:count, :] = plain[units:] + moved[:-units]
    net[count:, :] = moved[-units:]
    copies[4].wait()
    slope_copy.wait()


def even_kernel(
    c2, x2, net, split, c0_in, x0_in, weight_in, inverse_in, coef, lagged,
    c0, x0, weight, inverse, sems,
):
    copies = started(sems, [(c0_in, c0), (x0_in, x0), (weight_in, weight), (inverse_in, inverse)])
    table = split[...]
    units = weight.shape[0]
    ahead_spec, back_spec = [packed_spectrum(table, ref[...]) for ref in (c2, x2)]
    for copy in copies[:3]:
        copy.wait()
    own_spec, in_spec = [packed_spectrum(table, ref[...]) for ref in (c0, x0)]
    products = {0: (in_spec, own_spec), 2: (in_spec, ahead_spec), 4: (back_spec, ahead_spec)}
    total = None
    mixes = {}
    for k, (first, second) in products.items():
        part, mixes[k] = pair_products(first, second, net[k * units:(k + 1) * units, :], weight[...])
        total = part if total is None else total + part
    coef[...] = total
    copies[3].wait()
    sides = jnp.concatenate([mixes[0], -turned(mixes[2], 0), mixes[2], -turned(mixes[4], 0)], axis=1)
    lagged[...] = times_stacked(inverse[...], sides)


def halved(ref):
    rows = ref.shape[0] // 2
    return ref[:rows, :], ref[rows:, :]


def lag_kernel(
    scale, own,
    ahead, x2, c1, first_coef, first_lagged, net, split,
    x0_in, weight_in, inverse_in, embed_in, slope_in, out, same,
    x0, weight, inverse, embed, slope, packed, sems,
):
    copies = started(
        sems,
        [
            (x0_in, x0), (weight_in, weight), (inverse_in, inverse), (embed_in, embed), (slope_in, slope),
            (c1, same),
        ],
    )
    units, channels = weight.shape
    table = split[...]
    next_spec, back_spec = [packed_spectrum(table, ref[...]) for ref in (c1, x2)]
    for copy in copies[:2]:
        copy.wait()
    in_spec = packed_spectrum(table, x0[...])
    coef = first_coef[...]
    mixes = {}
    for k, first in {1: in_spec, 3: back_spec}.items():
        part, mixes[k] = pair_products(first, next_spec, net[k * units:(k + 1) * units, :], weight[...])
        coef = coef + part
    coef = coef * scale
    sides = jnp.concatenate([coef[:, k * units:(k + 1) * units] for k in range(channels // units)], axis=0)
    owners = sides.shape[0] // own
    chunk = packed.shape[0] // owners
    for o in range(owners):
        packed[o * chunk:o * chunk + own, :] = sides[o * own:(o + 1) * own]
    for copy in copies[2:]:
        copy.wait()
    sides = jnp.concatenate([-turned(mixes[1], 0), mixes[1], -turned(mixes[3], 0), mixes[3]], axis=1)
    lagged = first_lagged[...] + times_stacked(inverse[...], sides)
    grads = jnp.concatenate(
        [lagged[:, k * units:(k + 1) * units] for k in range(LAG_BLOCKS)], axis=0
    ) * (slope[...] * scale)
    lift = times_stacked(embed[...], grads)
    bias = jnp.sum(grads, axis=0, keepdims=True)
    lift_rows = chunk - own - 1
    for o in range(owners):
        packed[o * chunk + own:(o + 1) * chunk - 1, :] = lift[o * lift_rows:(o + 1) * lift_rows]
        packed[(o + 1) * chunk - 1:(o + 1) * chunk, :] = bias
    copy = pltpu.make_async_copy(packed, out, sems.at[len(copies)])
    copy.start()
    copy.wait()


def tokens_terms(net, weight, specs):
    units = weight.shape[0]
    weight_hi, weight_lo = parts(weight)
    doubled = jnp.concatenate([weight_hi, weight_hi], axis=0)
    total = None
    for k, spec in enumerate(specs):
        net_hi, net_lo = parts(net[k * units:(k + 1) * units, :].T)
        coef = times(jnp.concatenate([net_hi, net_lo], axis=1), doubled) + times(net_hi, weight_lo)
        half = coef.shape[0] // 2
        term = conj_product((coef[:half], coef[half:]), spec)
        total = term if total is None else (total[0] + term[0], total[1] + term[1])
    return total


def early_tokens_kernel(
    c2, net, split, c0_in, c1_in, weight_in, behind, out, same,
    c0, c1, weight, total_kept, sems,
):
    copies = started(sems, [(c0_in, c0), (c1_in, c1), (weight_in, weight), (c2, same)])
    for copy in copies[:3]:
        copy.wait()
    table = split[...]
    specs = [packed_spectrum(table, ref[...]) for ref in (c0, c1)]
    total = tokens_terms(net[:len(specs) * weight.shape[0], :], weight[...], specs)
    total_kept[...] = jnp.concatenate(total, axis=0)
    copies[3].wait()
    for copy in started(sems, [(total_kept, out)]):
        copy.wait()


def late_tokens_kernel(
    c3, c4, net, split, c2_in, weight_in, early_in, inverse_in, out, c2, weight, early, inverse, sems
):
    copies = started(sems, [(c2_in, c2), (weight_in, weight), (early_in, early), (inverse_in, inverse)])
    table = split[...]
    later = [packed_spectrum(table, ref[...]) for ref in (c3, c4)]
    for copy in copies[:2]:
        copy.wait()
    specs = [packed_spectrum(table, c2[...])] + later
    done = net.shape[0] - len(specs) * weight.shape[0]
    terms = tokens_terms(net[done:, :], weight[...], specs)
    copies[2].wait()
    total = [a + b for a, b in zip(halved(early), terms)]
    copies[3].wait()
    length = c3.shape[0]
    out[...] = times_stacked(inverse[...], jnp.concatenate(total, axis=0)) * (1.0 / length)


def first_sum_kernel(slots, value, early, out):
    chunk = out.shape[0] // slots
    total = value[:chunk, :]
    for o in range(1, value.shape[0] // chunk):
        total = total + value[o * chunk:(o + 1) * chunk, :]
    for i in range(slots):
        out[i * chunk:(i + 1) * chunk, :] = total


def choose_kernel(core, relayed, block, out):
    out[...] = jnp.where(core[0] == 0, relayed[...].astype(jnp.float32), block[...].astype(jnp.float32)).astype(
        out.dtype
    )


def second_sum_kernel(own, slots, line, value, block, out, same):
    same[...] = block[...]
    lines = slots // CORES
    place = line[0]
    chunk = value.shape[0] // slots
    coef = jnp.zeros((own, value.shape[1]), jnp.float32)
    rest = jnp.zeros((chunk - own, value.shape[1]), jnp.float32)
    for i in range(slots):
        coef = coef + jnp.where(place == i % lines, value[i * chunk:i * chunk + own, :], 0.0)
        rest = rest + value[i * chunk + own:(i + 1) * chunk, :]
    for o in range(out.shape[0] // chunk):
        out[o * chunk:o * chunk + own, :] = coef
        out[o * chunk + own:(o + 1) * chunk, :] = rest


def unpack_kernel(own, owners, value, coef, lift, bias):
    units = value.shape[1]
    chunk = value.shape[0] // owners
    each = coef.shape[0] // own
    rows = chunk - own - 1
    for o in range(owners):
        column, row = o // each, o % each
        coef[row * own:(row + 1) * own, column * units:(column + 1) * units] = value[
            o * chunk:o * chunk + own, :
        ]
        lift[o * rows:(o + 1) * rows, :] = value[o * chunk + own:(o + 1) * chunk - 1, :]
    bias[...] = value[chunk - 1:chunk, :]


def called(kernel, mebibytes, shapes, *operands, **options):
    return pl.pallas_call(
        kernel,
        out_shape=shapes,
        compiler_params=pltpu.CompilerParams(vmem_limit_bytes=mebibytes * 2 ** 20),
        **options,
    )(*operands)


def shards(tokens_in, cotangent, lift_weight, lift_bias, coef_weight):
    inputs = tokens_in[0]
    grads = cotangent[0]
    length, channels = inputs.shape
    lags = LAG_BLOCKS * length
    features, units = lift_weight.shape
    depth = coef_weight.shape[0]
    blocks_total = lax.axis_size("ctx")

    core = (lax.axis_index("ctx") % CORES).astype(jnp.int32).reshape(1)
    ahead2 = shifted(grads, "ctx", -CORES)
    behind2 = shifted(inputs, "ctx", CORES)
    ahead1 = shifted(grads, "ctx", -1)

    def real(*shape):
        return jax.ShapeDtypeStruct(shape, jnp.float32)

    def like(value):
        return jax.ShapeDtypeStruct(value.shape, value.dtype)

    scalar = pl.BlockSpec(memory_space=pltpu.SMEM)
    whole = pl.BlockSpec(memory_space=pltpu.VMEM)
    table = odd_table(length)
    split = jnp.asarray(halves(table))
    inverse = jnp.asarray(halves(table.T))
    features_table = lag_features(lags, features)
    embed = jnp.asarray(halves(features_table.T).T)
    embed_turned = jnp.asarray(halves(features_table.T))

    def held(value):
        return pltpu.with_memory_space_constraint(value, pltpu.HBM)

    def room(value):
        return pltpu.VMEM(value.shape, value.dtype)

    def sems(count):
        return pltpu.SemaphoreType.DMA((count,))

    far_off = pl.BlockSpec(memory_space=pltpu.HBM)
    bias_row = lift_bias[None]
    first_operands = (embed, lift_weight, bias_row, inverse, split)
    split_table = split
    net, split, slope = called(
        prepare_kernel,
        24,
        (
            real((LAG_BLOCKS + 1) * units, 2 * length),
            like(split),
            pltpu.HBM((lags, units), jnp.float32),
        ),
        *[held(value) for value in first_operands],
        in_specs=[far_off] * 5,
        out_specs=[whole] * 2 + [far_off],
        scratch_shapes=[room(value) for value in first_operands if value is not split_table]
        + [pltpu.VMEM((lags, units), jnp.float32), sems(6)],
    )
    even_operands = (grads, inputs, coef_weight, inverse)
    coef, lagged = called(
        even_kernel,
        24,
        (real(depth, channels), real(length, LAG_BLOCKS * units)),
        ahead2, behind2, net, split,
        *[held(value) for value in even_operands],
        in_specs=[whole] * 4 + [far_off] * 4,
        scratch_shapes=[room(value) for value in even_operands] + [sems(4)],
    )

    planes, columns = device_groups()
    owners, slots = len(planes[0]), len(columns[0])
    own = channels // units * depth // owners
    chunk = own + features // owners + 1
    scale = 1.0 / math.sqrt(lax.axis_size("dp") * length * blocks_total) / length

    def rows_of(count):
        return real(count * chunk, units)

    packed, ahead1 = called(
        lambda *refs: lag_kernel(scale, own, *refs),
        32,
        (pltpu.HBM((owners * chunk, units), jnp.float32), pltpu.HBM(ahead1.shape, ahead1.dtype)),
        ahead2, behind2, ahead1, coef, lagged, net, split,
        *[held(value) for value in (inputs, coef_weight, inverse, embed_turned, slope)],
        in_specs=[pl.BlockSpec(memory_space=pl.ANY)] + [whole] * 6 + [far_off] * 5,
        out_specs=[far_off] * 2,
        scratch_shapes=[room(value) for value in (inputs, coef_weight, inverse, embed_turned, slope)]
        + [pltpu.VMEM((owners * chunk, units), jnp.float32), sems(7)],
    )
    summed = exchanged(packed, ("dp", "ctx"), planes)
    early, ahead2 = called(
        early_tokens_kernel,
        24,
        (pltpu.HBM((2 * length, channels), jnp.float32), pltpu.HBM(ahead2.shape, ahead2.dtype)),
        ahead2, net, split,
        *[held(value) for value in (grads, ahead1, coef_weight)],
        behind2,
        in_specs=[whole] * 3 + [far_off] * 3 + [pl.BlockSpec(memory_space=pl.ANY)],
        out_specs=[far_off] * 2,
        scratch_shapes=[room(value) for value in (grads, ahead1, coef_weight)]
        + [pltpu.VMEM((2 * length, channels), jnp.float32), sems(4)],
    )
    summed = called(
        lambda *refs: first_sum_kernel(slots, *refs),
        8,
        rows_of(slots),
        summed, held(early),
        in_specs=[whole, far_off],
    )
    last = shifted(ahead2, "ctx", -CORES)
    ahead3 = swapped(
        called(choose_kernel, 8, like(last), core, last, ahead2, in_specs=[scalar] + [whole] * 2)
    )
    summed = exchanged(summed, ("ctx", "ch"), columns)
    line = lax.axis_index("ch").astype(jnp.int32).reshape(1)
    spread, ahead3 = called(
        lambda *refs: second_sum_kernel(own, slots, *refs),
        8,
        (rows_of(owners), like(last)),
        line, summed, ahead3,
        in_specs=[scalar] + [whole] * 2,
    )
    full = exchanged(spread, ("dp", "ctx"), planes)
    coef_weight_grad, lift_weight_grad, lift_bias_grad = called(
        lambda *refs: unpack_kernel(own, owners, *refs),
        8,
        (
            jax.ShapeDtypeStruct((depth, channels), jnp.float32),
            jax.ShapeDtypeStruct((features, units), jnp.float32),
            jax.ShapeDtypeStruct((1, units), jnp.float32),
        ),
        full,
    )
    tokens_grad = called(
        late_tokens_kernel,
        24,
        real(length, channels),
        ahead3, last, net, split,
        *[held(value) for value in (ahead2, coef_weight, early, inverse)],
        in_specs=[whole] * 4 + [far_off] * 4,
        scratch_shapes=[room(value) for value in (ahead2, coef_weight, early, inverse)] + [sems(4)],
    )
    return (tokens_grad[None], lift_weight_grad, lift_bias_grad[0], coef_weight_grad)


def solution(mesh):
    in_specs = (P("dp", "ctx", "ch"), P("dp", "ctx", "ch"), P(), P(), P(None, "ch"))
    out_specs = (P("dp", "ctx", "ch"), P(), P(), P(None, "ch"))
    return jax.shard_map(shards, mesh=mesh, in_specs=in_specs, out_specs=out_specs, check_vma=False)
```

```python
import math

import jax
import jax.numpy as jnp
import numpy as np
from jax import lax
from jax.experimental import pallas as pl
from jax.experimental.pallas import tpu as pltpu
from jax.sharding import PartitionSpec as P

LAG_BLOCKS = 4
Z_HIGH = 4
CORES = 2


def shifted(value, axis, steps):
    count = lax.axis_size(axis)
    initial, last = (max(0, -steps), min(count, count - steps))
    return lax.ppermute(value, axis, [(source, source + steps) for source in range(initial, last)])


def swapped(value):
    count = lax.axis_size("ctx")
    return lax.ppermute(value, "ctx", [(i, i ^ 1) for i in range(count)])


def lag_features(count, width):
    halfway = width // 2
    rates = np.float32(3.0) * np.exp(np.arange(halfway, dtype=np.float32) * np.float32(-math.log(count) / halfway))
    angles = np.arange(count, dtype=np.float32)[:, None] * rates[None, :].astype(np.float32)
    angles = angles.astype(np.float32).astype(np.float64)
    return np.concatenate([np.sin(angles), np.cos(angles)], axis=1)


def odd_table(length):
    phase = (2 * np.arange(length)[:, None] + 1) * np.arange(length)[None, :] % (4 * length)
    angles = phase * (2.0 * math.pi / (4 * length))
    return np.concatenate([np.cos(angles), -np.sin(angles)], axis=0)


def halves(table):
    upper = table.astype(jnp.bfloat16)
    lower = (table - upper.astype(np.float64)).astype(jnp.bfloat16)
    return np.concatenate([upper, lower], axis=0)


def turned(value, axis):
    rows = value.shape[axis] // 2
    shape = [1, 1]
    shape[axis] = rows
    parity = jnp.where(lax.broadcasted_iota(jnp.int32, shape, axis) % 2 == 0, 1.0, -1.0)
    real, imag = jnp.split(value, 2, axis=axis)
    return jnp.concatenate([-parity * imag, parity * real], axis=axis)


def device_groups():
    count, rows, lines = lax.axis_size("ctx"), lax.axis_size("dp"), lax.axis_size("ch")
    wide = count // (CORES * Z_HIGH)
    planes = [
        [d * count + (x * Z_HIGH + z) * CORES + c for x in range(wide) for z in range(Z_HIGH) for d in range(rows)]
        for c in range(CORES)
    ]
    columns = [
        [(s * CORES + c) * lines + y for c in range(CORES) for y in range(lines)]
        for s in range(wide * Z_HIGH)
    ]
    return planes, columns


def exchanged(value, axes, groups):
    chunks = value.reshape(len(groups[0]), 1, -1)
    return lax.all_to_all(
        chunks, axes, split_axis=0, concat_axis=0, axis_index_groups=groups, tiled=True
    ).reshape(value.shape)


def parts(value):
    upper = value.astype(jnp.bfloat16)
    return upper, (value - upper.astype(jnp.float32)).astype(jnp.bfloat16)


def times(first, second):
    return jnp.dot(first, second, preferred_element_type=jnp.float32)


def times_stacked(stacked, second):
    rows = stacked.shape[0] // 2
    upper, lower = parts(second)
    both = times(stacked, upper)
    return both[:rows] + both[rows:] + times(stacked[:rows], lower)


def spectrum(table, block):
    both = times(table, block)
    rows = both.shape[0] // 2
    return both[:rows], both[rows:], rows // 2


def packed_spectrum(table, block):
    upper, lower, rows = spectrum(table, block)
    total = upper + lower
    return total[:rows], total[rows:]


def conj_product(first, second):
    real_a, imag_a = first
    real_b, imag_b = second
    return real_a * real_b + imag_a * imag_b, real_a * imag_b - imag_a * real_b


def pair_products(first, second, net, weight):
    units = weight.shape[0]
    pair = jnp.concatenate(conj_product(first, second), axis=0)
    upper, lower = parts(pair)
    net_hi, net_lo = parts(net)
    both = times(jnp.concatenate([net_hi, net_lo], axis=0), upper)
    coef = both[:units] + both[units:] + times(net_hi, lower)
    weight_hi, weight_lo = parts(weight)
    last = (((1,), (1,)), ((), ()))
    both = lax.dot_general(
        upper, jnp.concatenate([weight_hi, weight_lo], axis=0), last, preferred_element_type=jnp.float32
    )
    mix = both[:, :units] + both[:, units:] + lax.dot_general(
        lower, weight_hi, last, preferred_element_type=jnp.float32
    )
    return coef, mix


def started(sems, pairs):
    copies = [
        pltpu.make_async_copy(source, target, sems.at[i]) for i, (source, target) in enumerate(pairs)
    ]
    for copy in copies:
        copy.start()
    return copies


def prepare_kernel(
    embed_in, lift_weight_in, lift_bias_in, inverse_in, split_in, c0_in, x0_in, weight_in,
    net, slope, coef, mix, split, in_spec,
    embed, lift_weight, lift_bias, inverse, c0, x0, weight, slope_kept, sems,
):
    copies = started(
        sems,
        [
            (embed_in, embed), (lift_weight_in, lift_weight), (lift_bias_in, lift_bias),
            (inverse_in, inverse), (split_in, split), (c0_in, c0), (x0_in, x0), (weight_in, weight),
        ],
    )
    units = lift_weight.shape[1]
    length = inverse.shape[0] // 2
    for copy in copies[:3]:
        copy.wait()
    features = lift_weight.shape[0]
    lift_hi, lift_lo = parts(lift_weight[...])
    preact = (
        times(embed[...], jnp.concatenate([lift_hi, lift_hi], axis=0))
        + times(embed[:, :features], lift_lo)
        + lift_bias[...]
    )
    logistic = jax.nn.sigmoid(preact)
    hidden = preact * logistic
    slope_kept[...] = logistic * (1.0 + preact * (1.0 - logistic))
    slope_copy = pltpu.make_async_copy(slope_kept, slope, sems.at[len(copies)])
    slope_copy.start()
    rows = jnp.concatenate(
        [hidden[k * length:(k + 1) * length].T for k in range(LAG_BLOCKS)], axis=0
    )
    upper, lower = parts(rows)
    count = rows.shape[0]
    copies[3].wait()
    both = times(jnp.concatenate([upper, lower], axis=0), inverse[:length, :])
    plain = both[:count] + both[count:] + times(upper, inverse[length:, :])
    moved = turned(plain, 1)
    net[:units, :] = plain[:units]
    net[units:count, :] = plain[units:] + moved[:-units]
    net[count:, :] = moved[-units:]
    for copy in copies[4:]:
        copy.wait()
    own = packed_spectrum(split[...], c0[...])
    source = packed_spectrum(split[...], x0[...])
    in_spec[...] = jnp.concatenate(source, axis=0)
    coef[...], mix[...] = pair_products(source, own, plain[:units], weight[...])
    slope_copy.wait()


def halved(ref):
    rows = ref.shape[0] // 2
    return ref[:rows, :], ref[rows:, :]


def lag_kernel(
    scale, own,
    c2, x2, c1, first_coef, first_mix, net, in_ref, split,
    x0_in, weight_in, inverse_in, embed_in, slope_in, out, same,
    weight, inverse, embed, slope, packed, sems,
):
    copies = started(
        sems,
        [(weight_in, weight), (inverse_in, inverse), (embed_in, embed), (slope_in, slope), (c1, same)],
    )
    units, channels = weight.shape
    table = split[...]
    next_spec, ahead_spec, back_spec = [packed_spectrum(table, ref[...]) for ref in (c1, c2, x2)]
    in_spec = halved(in_ref)
    copies[0].wait()
    products = [
        (in_spec, next_spec),
        (in_spec, ahead_spec),
        (back_spec, next_spec),
        (back_spec, ahead_spec),
    ]
    coef = first_coef[...]
    mixes = [first_mix[...]]
    for k, (first, second) in enumerate(products, 1):
        part, mix = pair_products(first, second, net[k * units:(k + 1) * units, :], weight[...])
        coef = coef + part
        mixes.append(mix)
    coef = coef * scale
    sides = jnp.concatenate([coef[:, k * units:(k + 1) * units] for k in range(channels // units)], axis=0)
    owners = sides.shape[0] // own
    chunk = packed.shape[0] // owners
    for o in range(owners):
        packed[o * chunk:o * chunk + own, :] = sides[o * own:(o + 1) * own]
    for copy in copies[1:]:
        copy.wait()
    sides = jnp.concatenate(
        [mixes[k] - turned(mixes[k + 1], 0) for k in range(LAG_BLOCKS)], axis=1
    )
    lagged = times_stacked(inverse[...], sides)
    grads = jnp.concatenate(
        [lagged[:, k * units:(k + 1) * units] for k in range(LAG_BLOCKS)], axis=0
    ) * (slope[...] * scale)
    lift = times_stacked(embed[...], grads)
    bias = jnp.sum(grads, axis=0, keepdims=True)
    lift_rows = chunk - own - 1
    for o in range(owners):
        packed[o * chunk + own:(o + 1) * chunk - 1, :] = lift[o * lift_rows:(o + 1) * lift_rows]
        packed[(o + 1) * chunk - 1:(o + 1) * chunk, :] = bias
    copy = pltpu.make_async_copy(packed, out, sems.at[len(copies)])
    copy.start()
    copy.wait()


def tokens_terms(net, weight, specs):
    units = weight.shape[0]
    weight_hi, weight_lo = parts(weight)
    doubled = jnp.concatenate([weight_hi, weight_hi], axis=0)
    total = None
    for k, spec in enumerate(specs):
        net_hi, net_lo = parts(net[k * units:(k + 1) * units, :].T)
        coef = times(jnp.concatenate([net_hi, net_lo], axis=1), doubled) + times(net_hi, weight_lo)
        half = coef.shape[0] // 2
        term = conj_product((coef[:half], coef[half:]), spec)
        total = term if total is None else (total[0] + term[0], total[1] + term[1])
    return total


def early_tokens_kernel(
    c2, net, split, c0_in, c1_in, weight_in, behind, out, same,
    c0, c1, weight, total_kept, sems,
):
    copies = started(sems, [(c0_in, c0), (c1_in, c1), (weight_in, weight), (c2, same)])
    for copy in copies[:3]:
        copy.wait()
    table = split[...]
    specs = [packed_spectrum(table, ref[...]) for ref in (c0, c1)]
    total = tokens_terms(net[:len(specs) * weight.shape[0], :], weight[...], specs)
    total_kept[...] = jnp.concatenate(total, axis=0)
    copies[3].wait()
    for copy in started(sems, [(total_kept, out)]):
        copy.wait()


def late_tokens_kernel(
    c3, c4, net, split, c2_in, weight_in, early_in, inverse_in, out, c2, weight, early, inverse, sems
):
    copies = started(sems, [(c2_in, c2), (weight_in, weight), (early_in, early), (inverse_in, inverse)])
    table = split[...]
    later = [packed_spectrum(table, ref[...]) for ref in (c3, c4)]
    for copy in copies[:2]:
        copy.wait()
    specs = [packed_spectrum(table, c2[...])] + later
    done = net.shape[0] - len(specs) * weight.shape[0]
    terms = tokens_terms(net[done:, :], weight[...], specs)
    copies[2].wait()
    total = [a + b for a, b in zip(halved(early), terms)]
    copies[3].wait()
    length = c3.shape[0]
    out[...] = times_stacked(inverse[...], jnp.concatenate(total, axis=0)) * (1.0 / length)


def first_sum_kernel(slots, value, early, out):
    chunk = out.shape[0] // slots
    total = value[:chunk, :]
    for o in range(1, value.shape[0] // chunk):
        total = total + value[o * chunk:(o + 1) * chunk, :]
    for i in range(slots):
        out[i * chunk:(i + 1) * chunk, :] = total


def choose_kernel(core, relayed, block, out):
    out[...] = jnp.where(core[0] == 0, relayed[...].astype(jnp.float32), block[...].astype(jnp.float32)).astype(
        out.dtype
    )


def second_sum_kernel(own, slots, line, value, block, out, same):
    same[...] = block[...]
    lines = slots // CORES
    place = line[0]
    chunk = value.shape[0] // slots
    coef = jnp.zeros((own, value.shape[1]), jnp.float32)
    rest = jnp.zeros((chunk - own, value.shape[1]), jnp.float32)
    for i in range(slots):
        coef = coef + jnp.where(place == i % lines, value[i * chunk:i * chunk + own, :], 0.0)
        rest = rest + value[i * chunk + own:(i + 1) * chunk, :]
    for o in range(out.shape[0] // chunk):
        out[o * chunk:o * chunk + own, :] = coef
        out[o * chunk + own:(o + 1) * chunk, :] = rest


def unpack_kernel(own, owners, value, coef, lift, bias):
    units = value.shape[1]
    chunk = value.shape[0] // owners
    each = coef.shape[0] // own
    rows = chunk - own - 1
    for o in range(owners):
        column, row = o // each, o % each
        coef[row * own:(row + 1) * own, column * units:(column + 1) * units] = value[
            o * chunk:o * chunk + own, :
        ]
        lift[o * rows:(o + 1) * rows, :] = value[o * chunk + own:(o + 1) * chunk - 1, :]
    bias[...] = value[chunk - 1:chunk, :]


def called(kernel, mebibytes, shapes, *operands, **options):
    return pl.pallas_call(
        kernel,
        out_shape=shapes,
        compiler_params=pltpu.CompilerParams(vmem_limit_bytes=mebibytes * 2 ** 20),
        **options,
    )(*operands)


def shards(tokens_in, cotangent, lift_weight, lift_bias, coef_weight):
    inputs = tokens_in[0]
    grads = cotangent[0]
    length, channels = inputs.shape
    lags = LAG_BLOCKS * length
    features, units = lift_weight.shape
    depth = coef_weight.shape[0]
    blocks_total = lax.axis_size("ctx")

    core = (lax.axis_index("ctx") % CORES).astype(jnp.int32).reshape(1)
    ahead2 = shifted(grads, "ctx", -CORES)
    behind2 = shifted(inputs, "ctx", CORES)
    ahead1 = shifted(grads, "ctx", -1)

    def real(*shape):
        return jax.ShapeDtypeStruct(shape, jnp.float32)

    def like(value):
        return jax.ShapeDtypeStruct(value.shape, value.dtype)

    scalar = pl.BlockSpec(memory_space=pltpu.SMEM)
    whole = pl.BlockSpec(memory_space=pltpu.VMEM)
    table = odd_table(length)
    split = jnp.asarray(halves(table))
    inverse = jnp.asarray(halves(table.T))
    features_table = lag_features(lags, features)
    embed = jnp.asarray(halves(features_table.T).T)
    embed_turned = jnp.asarray(halves(features_table.T))

    def held(value):
        return pltpu.with_memory_space_constraint(value, pltpu.HBM)

    def room(value):
        return pltpu.VMEM(value.shape, value.dtype)

    def sems(count):
        return pltpu.SemaphoreType.DMA((count,))

    far_off = pl.BlockSpec(memory_space=pltpu.HBM)
    bias_row = lift_bias[None]
    first_operands = (embed, lift_weight, bias_row, inverse, split, grads, inputs, coef_weight)
    net, slope, coef, mix, split, in_spec = called(
        prepare_kernel,
        24,
        (
            real((LAG_BLOCKS + 1) * units, 2 * length),
            pltpu.HBM((lags, units), jnp.float32),
            real(depth, channels),
            real(2 * length, units),
            like(split),
            real(2 * length, channels),
        ),
        *[held(value) for value in first_operands],
        in_specs=[far_off] * 8,
        out_specs=[whole, far_off] + [whole] * 4,
        scratch_shapes=[room(value) for value in first_operands if value is not split]
        + [pltpu.VMEM((lags, units), jnp.float32), sems(9)],
    )
    planes, columns = device_groups()
    owners, slots = len(planes[0]), len(columns[0])
    own = channels // units * depth // owners
    chunk = own + features // owners + 1
    scale = 1.0 / math.sqrt(lax.axis_size("dp") * length * blocks_total) / length

    def rows_of(count):
        return real(count * chunk, units)

    packed, ahead1 = called(
        lambda *refs: lag_kernel(scale, own, *refs),
        32,
        (pltpu.HBM((owners * chunk, units), jnp.float32), pltpu.HBM(ahead1.shape, ahead1.dtype)),
        ahead2, behind2, ahead1, coef, mix, net, in_spec, split,
        *[held(value) for value in (inputs, coef_weight, inverse, embed_turned, slope)],
        in_specs=[whole] * 8 + [far_off] * 5,
        out_specs=[far_off] * 2,
        scratch_shapes=[room(value) for value in (coef_weight, inverse, embed_turned, slope)]
        + [pltpu.VMEM((owners * chunk, units), jnp.float32), sems(6)],
    )
    summed = exchanged(packed, ("dp", "ctx"), planes)
    early, ahead2 = called(
        early_tokens_kernel,
        24,
        (pltpu.HBM((2 * length, channels), jnp.float32), pltpu.HBM(ahead2.shape, ahead2.dtype)),
        ahead2, net, split,
        *[held(value) for value in (grads, ahead1, coef_weight)],
        behind2,
        in_specs=[whole] * 3 + [far_off] * 3 + [pl.BlockSpec(memory_space=pl.ANY)],
        out_specs=[far_off] * 2,
        scratch_shapes=[room(value) for value in (grads, ahead1, coef_weight)]
        + [pltpu.VMEM((2 * length, channels), jnp.float32), sems(4)],
    )
    summed = called(
        lambda *refs: first_sum_kernel(slots, *refs),
        8,
        rows_of(slots),
        summed, held(early),
        in_specs=[whole, far_off],
    )
    last = shifted(ahead2, "ctx", -CORES)
    ahead3 = swapped(
        called(choose_kernel, 8, like(last), core, last, ahead2, in_specs=[scalar] + [whole] * 2)
    )
    summed = exchanged(summed, ("ctx", "ch"), columns)
    line = lax.axis_index("ch").astype(jnp.int32).reshape(1)
    spread, ahead3 = called(
        lambda *refs: second_sum_kernel(own, slots, *refs),
        8,
        (rows_of(owners), like(last)),
        line, summed, ahead3,
        in_specs=[scalar] + [whole] * 2,
    )
    full = exchanged(spread, ("dp", "ctx"), planes)
    coef_weight_grad, lift_weight_grad, lift_bias_grad = called(
        lambda *refs: unpack_kernel(own, owners, *refs),
        8,
        (
            jax.ShapeDtypeStruct((depth, channels), jnp.float32),
            jax.ShapeDtypeStruct((features, units), jnp.float32),
            jax.ShapeDtypeStruct((1, units), jnp.float32),
        ),
        full,
    )
    tokens_grad = called(
        late_tokens_kernel,
        24,
        real(length, channels),
        ahead3, last, net, split,
        *[held(value) for value in (ahead2, coef_weight, early, inverse)],
        in_specs=[whole] * 4 + [far_off] * 4,
        scratch_shapes=[room(value) for value in (ahead2, coef_weight, early, inverse)] + [sems(4)],
    )
    return (tokens_grad[None], lift_weight_grad, lift_bias_grad[0], coef_weight_grad)


def solution(mesh):
    in_specs = (P("dp", "ctx", "ch"), P("dp", "ctx", "ch"), P(), P(), P(None, "ch"))
    out_specs = (P("dp", "ctx", "ch"), P(), P(), P(None, "ch"))
    return jax.shard_map(shards, mesh=mesh, in_specs=in_specs, out_specs=out_specs, check_vma=False)
```

```python
import math

import jax
import jax.numpy as jnp
import numpy as np
from jax import lax
from jax.experimental import pallas as pl
from jax.experimental.pallas import tpu as pltpu
from jax.sharding import PartitionSpec as P

LAG_BLOCKS = 4
Z_HIGH = 4
CORES = 2


def shifted(value, axis, steps):
    count = lax.axis_size(axis)
    initial, last = (max(0, -steps), min(count, count - steps))
    return lax.ppermute(value, axis, [(source, source + steps) for source in range(initial, last)])


def swapped(value):
    count = lax.axis_size("ctx")
    return lax.ppermute(value, "ctx", [(i, i ^ 1) for i in range(count)])


def lag_features(count, width):
    halfway = width // 2
    rates = np.float32(3.0) * np.exp(np.arange(halfway, dtype=np.float32) * np.float32(-math.log(count) / halfway))
    angles = np.arange(count, dtype=np.float32)[:, None] * rates[None, :].astype(np.float32)
    angles = angles.astype(np.float32).astype(np.float64)
    return np.concatenate([np.sin(angles), np.cos(angles)], axis=1)


def odd_table(length):
    phase = (2 * np.arange(length)[:, None] + 1) * np.arange(length)[None, :] % (4 * length)
    angles = phase * (2.0 * math.pi / (4 * length))
    return np.concatenate([np.cos(angles), -np.sin(angles)], axis=0)


def halves(table):
    upper = table.astype(jnp.bfloat16)
    lower = (table - upper.astype(np.float64)).astype(jnp.bfloat16)
    return np.concatenate([upper, lower], axis=0)


def turned(value, axis):
    rows = value.shape[axis] // 2
    shape = [1, 1]
    shape[axis] = rows
    parity = jnp.where(lax.broadcasted_iota(jnp.int32, shape, axis) % 2 == 0, 1.0, -1.0)
    real, imag = jnp.split(value, 2, axis=axis)
    return jnp.concatenate([-parity * imag, parity * real], axis=axis)


def device_groups():
    count, rows, lines = lax.axis_size("ctx"), lax.axis_size("dp"), lax.axis_size("ch")
    wide = count // (CORES * Z_HIGH)
    planes = [
        [d * count + (x * Z_HIGH + z) * CORES + c for x in range(wide) for z in range(Z_HIGH) for d in range(rows)]
        for c in range(CORES)
    ]
    columns = [
        [(s * CORES + c) * lines + y for c in range(CORES) for y in range(lines)]
        for s in range(wide * Z_HIGH)
    ]
    return planes, columns


def exchanged(value, axes, groups):
    chunks = value.reshape(len(groups[0]), 1, -1)
    return lax.all_to_all(
        chunks, axes, split_axis=0, concat_axis=0, axis_index_groups=groups, tiled=True
    ).reshape(value.shape)


def parts(value):
    upper = value.astype(jnp.bfloat16)
    return upper, (value - upper.astype(jnp.float32)).astype(jnp.bfloat16)


def times(first, second):
    return jnp.dot(first, second, preferred_element_type=jnp.float32)


def times_stacked(stacked, second):
    rows = stacked.shape[0] // 2
    upper, lower = parts(second)
    both = times(stacked, upper)
    return both[:rows] + both[rows:] + times(stacked[:rows], lower)


def spectrum(table, block):
    both = times(table, block)
    rows = both.shape[0] // 2
    return both[:rows], both[rows:], rows // 2


def packed_spectrum(table, block):
    upper, lower, rows = spectrum(table, block)
    total = upper + lower
    return total[:rows], total[rows:]


def conj_product(first, second):
    real_a, imag_a = first
    real_b, imag_b = second
    return real_a * real_b + imag_a * imag_b, real_a * imag_b - imag_a * real_b


def pair_products(first, second, net, weight):
    units = weight.shape[0]
    pair = jnp.concatenate(conj_product(first, second), axis=0)
    upper, lower = parts(pair)
    net_hi, net_lo = parts(net)
    both = times(jnp.concatenate([net_hi, net_lo], axis=0), upper)
    coef = both[:units] + both[units:] + times(net_hi, lower)
    weight_hi, weight_lo = parts(weight)
    last = (((1,), (1,)), ((), ()))
    both = lax.dot_general(
        upper, jnp.concatenate([weight_hi, weight_lo], axis=0), last, preferred_element_type=jnp.float32
    )
    mix = both[:, :units] + both[:, units:] + lax.dot_general(
        lower, weight_hi, last, preferred_element_type=jnp.float32
    )
    return coef, mix


def started(sems, pairs):
    copies = [
        pltpu.make_async_copy(source, target, sems.at[i]) for i, (source, target) in enumerate(pairs)
    ]
    for copy in copies:
        copy.start()
    return copies


def prepare_kernel(
    embed_in, lift_weight_in, lift_bias_in, inverse_in, split_in, c0_in, x0_in, weight_in,
    net, slope, coef, mix, split, in_spec,
    embed, lift_weight, lift_bias, inverse, c0, x0, weight, slope_kept, sems,
):
    copies = started(
        sems,
        [
            (embed_in, embed), (lift_weight_in, lift_weight), (lift_bias_in, lift_bias),
            (inverse_in, inverse), (split_in, split), (c0_in, c0), (x0_in, x0), (weight_in, weight),
        ],
    )
    units = lift_weight.shape[1]
    length = inverse.shape[0] // 2
    for copy in copies[:3]:
        copy.wait()
    features = lift_weight.shape[0]
    lift_hi, lift_lo = parts(lift_weight[...])
    preact = (
        times(embed[...], jnp.concatenate([lift_hi, lift_hi], axis=0))
        + times(embed[:, :features], lift_lo)
        + lift_bias[...]
    )
    logistic = jax.nn.sigmoid(preact)
    hidden = preact * logistic
    slope_kept[...] = logistic * (1.0 + preact * (1.0 - logistic))
    slope_copy = pltpu.make_async_copy(slope_kept, slope, sems.at[len(copies)])
    slope_copy.start()
    rows = jnp.concatenate(
        [hidden[k * length:(k + 1) * length].T for k in range(LAG_BLOCKS)], axis=0
    )
    upper, lower = parts(rows)
    count = rows.shape[0]
    copies[3].wait()
    both = times(jnp.concatenate([upper, lower], axis=0), inverse[:length, :])
    plain = both[:count] + both[count:] + times(upper, inverse[length:, :])
    moved = turned(plain, 1)
    net[:units, :] = plain[:units]
    net[units:count, :] = plain[units:] + moved[:-units]
    net[count:, :] = moved[-units:]
    for copy in copies[4:]:
        copy.wait()
    own = packed_spectrum(split[...], c0[...])
    source = packed_spectrum(split[...], x0[...])
    in_spec[...] = jnp.concatenate(source, axis=0)
    coef[...], mix[...] = pair_products(source, own, plain[:units], weight[...])
    slope_copy.wait()


def halved(ref):
    rows = ref.shape[0] // 2
    return ref[:rows, :], ref[rows:, :]


def lag_kernel(
    scale, own,
    c2, x2, c1, first_coef, first_mix, net, in_ref, split,
    x0_in, weight_in, inverse_in, embed_in, slope_in, out, same,
    weight, inverse, embed, slope, packed, sems,
):
    copies = started(
        sems,
        [(weight_in, weight), (inverse_in, inverse), (embed_in, embed), (slope_in, slope), (c1, same)],
    )
    units, channels = weight.shape
    table = split[...]
    next_spec, ahead_spec, back_spec = [packed_spectrum(table, ref[...]) for ref in (c1, c2, x2)]
    in_spec = halved(in_ref)
    copies[0].wait()
    products = [
        (in_spec, next_spec),
        (in_spec, ahead_spec),
        (back_spec, next_spec),
        (back_spec, ahead_spec),
    ]
    coef = first_coef[...]
    mixes = [first_mix[...]]
    for k, (first, second) in enumerate(products, 1):
        part, mix = pair_products(first, second, net[k * units:(k + 1) * units, :], weight[...])
        coef = coef + part
        mixes.append(mix)
    coef = coef * scale
    sides = jnp.concatenate([coef[:, k * units:(k + 1) * units] for k in range(channels // units)], axis=0)
    owners = sides.shape[0] // own
    chunk = packed.shape[0] // owners
    for o in range(owners):
        packed[o * chunk:o * chunk + own, :] = sides[o * own:(o + 1) * own]
    for copy in copies[1:]:
        copy.wait()
    sides = jnp.concatenate(
        [mixes[k] - turned(mixes[k + 1], 0) for k in range(LAG_BLOCKS)], axis=1
    )
    lagged = times_stacked(inverse[...], sides)
    grads = jnp.concatenate(
        [lagged[:, k * units:(k + 1) * units] for k in range(LAG_BLOCKS)], axis=0
    ) * (slope[...] * scale)
    lift = times_stacked(embed[...], grads)
    bias = jnp.sum(grads, axis=0, keepdims=True)
    lift_rows = chunk - own - 1
    for o in range(owners):
        packed[o * chunk + own:(o + 1) * chunk - 1, :] = lift[o * lift_rows:(o + 1) * lift_rows]
        packed[(o + 1) * chunk - 1:(o + 1) * chunk, :] = bias
    copy = pltpu.make_async_copy(packed, out, sems.at[len(copies)])
    copy.start()
    copy.wait()


def tokens_terms(net, weight, specs):
    units = weight.shape[0]
    weight_hi, weight_lo = parts(weight)
    doubled = jnp.concatenate([weight_hi, weight_hi], axis=0)
    total = None
    for k, spec in enumerate(specs):
        net_hi, net_lo = parts(net[k * units:(k + 1) * units, :].T)
        coef = times(jnp.concatenate([net_hi, net_lo], axis=1), doubled) + times(net_hi, weight_lo)
        half = coef.shape[0] // 2
        term = conj_product((coef[:half], coef[half:]), spec)
        total = term if total is None else (total[0] + term[0], total[1] + term[1])
    return total


def early_tokens_kernel(
    c2, net, split, c0_in, c1_in, weight_in, behind, out, same,
    c0, weight, total_kept, sems,
):
    copies = started(sems, [(c0_in, c0), (weight_in, weight), (c2, same)])
    for copy in copies[:2]:
        copy.wait()
    table = split[...]
    specs = [packed_spectrum(table, c0[...])]
    total = tokens_terms(net[:len(specs) * weight.shape[0], :], weight[...], specs)
    total_kept[...] = jnp.concatenate(total, axis=0)
    copies[2].wait()
    for copy in started(sems, [(total_kept, out)]):
        copy.wait()


def late_tokens_kernel(
    c3, c4, net, split, c1_in, c2_in, weight_in, early_in, inverse_in, out, c1, c2, weight, early, inverse, sems
):
    copies = started(
        sems, [(c1_in, c1), (c2_in, c2), (weight_in, weight), (early_in, early), (inverse_in, inverse)]
    )
    table = split[...]
    later = [packed_spectrum(table, ref[...]) for ref in (c3, c4)]
    for copy in copies[:3]:
        copy.wait()
    specs = [packed_spectrum(table, ref[...]) for ref in (c1, c2)] + later
    done = net.shape[0] - len(specs) * weight.shape[0]
    terms = tokens_terms(net[done:, :], weight[...], specs)
    copies[3].wait()
    total = [a + b for a, b in zip(halved(early), terms)]
    copies[4].wait()
    length = c3.shape[0]
    out[...] = times_stacked(inverse[...], jnp.concatenate(total, axis=0)) * (1.0 / length)


def first_sum_kernel(slots, value, early, out):
    chunk = out.shape[0] // slots
    total = value[:chunk, :]
    for o in range(1, value.shape[0] // chunk):
        total = total + value[o * chunk:(o + 1) * chunk, :]
    for i in range(slots):
        out[i * chunk:(i + 1) * chunk, :] = total


def choose_kernel(core, relayed, block, out):
    out[...] = jnp.where(core[0] == 0, relayed[...].astype(jnp.float32), block[...].astype(jnp.float32)).astype(
        out.dtype
    )


def second_sum_kernel(own, slots, line, value, block, out, same):
    same[...] = block[...]
    lines = slots // CORES
    place = line[0]
    chunk = value.shape[0] // slots
    coef = jnp.zeros((own, value.shape[1]), jnp.float32)
    rest = jnp.zeros((chunk - own, value.shape[1]), jnp.float32)
    for i in range(slots):
        coef = coef + jnp.where(place == i % lines, value[i * chunk:i * chunk + own, :], 0.0)
        rest = rest + value[i * chunk + own:(i + 1) * chunk, :]
    for o in range(out.shape[0] // chunk):
        out[o * chunk:o * chunk + own, :] = coef
        out[o * chunk + own:(o + 1) * chunk, :] = rest


def unpack_kernel(own, owners, value, coef, lift, bias):
    units = value.shape[1]
    chunk = value.shape[0] // owners
    each = coef.shape[0] // own
    rows = chunk - own - 1
    for o in range(owners):
        column, row = o // each, o % each
        coef[row * own:(row + 1) * own, column * units:(column + 1) * units] = value[
            o * chunk:o * chunk + own, :
        ]
        lift[o * rows:(o + 1) * rows, :] = value[o * chunk + own:(o + 1) * chunk - 1, :]
    bias[...] = value[chunk - 1:chunk, :]


def called(kernel, mebibytes, shapes, *operands, **options):
    return pl.pallas_call(
        kernel,
        out_shape=shapes,
        compiler_params=pltpu.CompilerParams(vmem_limit_bytes=mebibytes * 2 ** 20),
        **options,
    )(*operands)


def shards(tokens_in, cotangent, lift_weight, lift_bias, coef_weight):
    inputs = tokens_in[0]
    grads = cotangent[0]
    length, channels = inputs.shape
    lags = LAG_BLOCKS * length
    features, units = lift_weight.shape
    depth = coef_weight.shape[0]
    blocks_total = lax.axis_size("ctx")

    core = (lax.axis_index("ctx") % CORES).astype(jnp.int32).reshape(1)
    ahead2 = shifted(grads, "ctx", -CORES)
    behind2 = shifted(inputs, "ctx", CORES)
    ahead1 = shifted(grads, "ctx", -1)

    def real(*shape):
        return jax.ShapeDtypeStruct(shape, jnp.float32)

    def like(value):
        return jax.ShapeDtypeStruct(value.shape, value.dtype)

    scalar = pl.BlockSpec(memory_space=pltpu.SMEM)
    whole = pl.BlockSpec(memory_space=pltpu.VMEM)
    table = odd_table(length)
    split = jnp.asarray(halves(table))
    inverse = jnp.asarray(halves(table.T))
    features_table = lag_features(lags, features)
    embed = jnp.asarray(halves(features_table.T).T)
    embed_turned = jnp.asarray(halves(features_table.T))

    def held(value):
        return pltpu.with_memory_space_constraint(value, pltpu.HBM)

    def room(value):
        return pltpu.VMEM(value.shape, value.dtype)

    def sems(count):
        return pltpu.SemaphoreType.DMA((count,))

    far_off = pl.BlockSpec(memory_space=pltpu.HBM)
    bias_row = lift_bias[None]
    first_operands = (embed, lift_weight, bias_row, inverse, split, grads, inputs, coef_weight)
    net, slope, coef, mix, split, in_spec = called(
        prepare_kernel,
        24,
        (
            real((LAG_BLOCKS + 1) * units, 2 * length),
            pltpu.HBM((lags, units), jnp.float32),
            real(depth, channels),
            real(2 * length, units),
            like(split),
            real(2 * length, channels),
        ),
        *[held(value) for value in first_operands],
        in_specs=[far_off] * 8,
        out_specs=[whole, far_off] + [whole] * 4,
        scratch_shapes=[room(value) for value in first_operands if value is not split]
        + [pltpu.VMEM((lags, units), jnp.float32), sems(9)],
    )
    planes, columns = device_groups()
    owners, slots = len(planes[0]), len(columns[0])
    own = channels // units * depth // owners
    chunk = own + features // owners + 1
    scale = 1.0 / math.sqrt(lax.axis_size("dp") * length * blocks_total) / length

    def rows_of(count):
        return real(count * chunk, units)

    packed, ahead1 = called(
        lambda *refs: lag_kernel(scale, own, *refs),
        32,
        (pltpu.HBM((owners * chunk, units), jnp.float32), pltpu.HBM(ahead1.shape, ahead1.dtype)),
        ahead2, behind2, ahead1, coef, mix, net, in_spec, split,
        *[held(value) for value in (inputs, coef_weight, inverse, embed_turned, slope)],
        in_specs=[whole] * 8 + [far_off] * 5,
        out_specs=[far_off] * 2,
        scratch_shapes=[room(value) for value in (coef_weight, inverse, embed_turned, slope)]
        + [pltpu.VMEM((owners * chunk, units), jnp.float32), sems(6)],
    )
    summed = exchanged(packed, ("dp", "ctx"), planes)
    early, ahead2 = called(
        early_tokens_kernel,
        24,
        (pltpu.HBM((2 * length, channels), jnp.float32), pltpu.HBM(ahead2.shape, ahead2.dtype)),
        ahead2, net, split,
        *[held(value) for value in (grads, ahead1, coef_weight)],
        behind2,
        in_specs=[whole] * 3 + [far_off] * 3 + [pl.BlockSpec(memory_space=pl.ANY)],
        out_specs=[far_off] * 2,
        scratch_shapes=[room(value) for value in (grads, coef_weight)]
        + [pltpu.VMEM((2 * length, channels), jnp.float32), sems(3)],
    )
    summed = called(
        lambda *refs: first_sum_kernel(slots, *refs),
        8,
        rows_of(slots),
        summed, held(early),
        in_specs=[whole, far_off],
    )
    last = shifted(ahead2, "ctx", -CORES)
    ahead3 = swapped(
        called(choose_kernel, 8, like(last), core, last, ahead2, in_specs=[scalar] + [whole] * 2)
    )
    summed = exchanged(summed, ("ctx", "ch"), columns)
    line = lax.axis_index("ch").astype(jnp.int32).reshape(1)
    spread, ahead3 = called(
        lambda *refs: second_sum_kernel(own, slots, *refs),
        8,
        (rows_of(owners), like(last)),
        line, summed, ahead3,
        in_specs=[scalar] + [whole] * 2,
    )
    full = exchanged(spread, ("dp", "ctx"), planes)
    coef_weight_grad, lift_weight_grad, lift_bias_grad = called(
        lambda *refs: unpack_kernel(own, owners, *refs),
        8,
        (
            jax.ShapeDtypeStruct((depth, channels), jnp.float32),
            jax.ShapeDtypeStruct((features, units), jnp.float32),
            jax.ShapeDtypeStruct((1, units), jnp.float32),
        ),
        full,
    )
    tokens_grad = called(
        late_tokens_kernel,
        24,
        real(length, channels),
        ahead3, last, net, split,
        *[held(value) for value in (ahead1, ahead2, coef_weight, early, inverse)],
        in_specs=[whole] * 4 + [far_off] * 5,
        scratch_shapes=[room(value) for value in (ahead1, ahead2, coef_weight, early, inverse)] + [sems(5)],
    )
    return (tokens_grad[None], lift_weight_grad, lift_bias_grad[0], coef_weight_grad)


def solution(mesh):
    in_specs = (P("dp", "ctx", "ch"), P("dp", "ctx", "ch"), P(), P(), P(None, "ch"))
    out_specs = (P("dp", "ctx", "ch"), P(), P(), P(None, "ch"))
    return jax.shard_map(shards, mesh=mesh, in_specs=in_specs, out_specs=out_specs, check_vma=False)
```

```python
import math

import jax
import jax.numpy as jnp
import numpy as np
from jax import lax
from jax.experimental import pallas as pl
from jax.experimental.pallas import tpu as pltpu
from jax.sharding import PartitionSpec as P

LAG_BLOCKS = 4
Z_HIGH = 4
CORES = 2


def shifted(value, axis, steps):
    count = lax.axis_size(axis)
    initial, last = (max(0, -steps), min(count, count - steps))
    return lax.ppermute(value, axis, [(source, source + steps) for source in range(initial, last)])


def swapped(value):
    count = lax.axis_size("ctx")
    return lax.ppermute(value, "ctx", [(i, i ^ 1) for i in range(count)])


def lag_features(count, width):
    halfway = width // 2
    rates = np.float32(3.0) * np.exp(np.arange(halfway, dtype=np.float32) * np.float32(-math.log(count) / halfway))
    angles = np.arange(count, dtype=np.float32)[:, None] * rates[None, :].astype(np.float32)
    angles = angles.astype(np.float32).astype(np.float64)
    return np.concatenate([np.sin(angles), np.cos(angles)], axis=1)


def odd_table(length):
    phase = (2 * np.arange(length)[:, None] + 1) * np.arange(length)[None, :] % (4 * length)
    angles = phase * (2.0 * math.pi / (4 * length))
    return np.concatenate([np.cos(angles), -np.sin(angles)], axis=0)


def halves(table):
    upper = table.astype(jnp.bfloat16)
    lower = (table - upper.astype(np.float64)).astype(jnp.bfloat16)
    return np.concatenate([upper, lower], axis=0)


def turned(value, axis):
    rows = value.shape[axis] // 2
    shape = [1, 1]
    shape[axis] = rows
    parity = jnp.where(lax.broadcasted_iota(jnp.int32, shape, axis) % 2 == 0, 1.0, -1.0)
    real, imag = jnp.split(value, 2, axis=axis)
    return jnp.concatenate([-parity * imag, parity * real], axis=axis)


def device_groups():
    count, rows, lines = lax.axis_size("ctx"), lax.axis_size("dp"), lax.axis_size("ch")
    wide = count // (CORES * Z_HIGH)
    planes = [
        [d * count + (x * Z_HIGH + z) * CORES + c for x in range(wide) for z in range(Z_HIGH) for d in range(rows)]
        for c in range(CORES)
    ]
    columns = [
        [(s * CORES + c) * lines + y for c in range(CORES) for y in range(lines)]
        for s in range(wide * Z_HIGH)
    ]
    return planes, columns


def exchanged(value, axes, groups):
    chunks = value.reshape(len(groups[0]), 1, -1)
    return lax.all_to_all(
        chunks, axes, split_axis=0, concat_axis=0, axis_index_groups=groups, tiled=True
    ).reshape(value.shape)


def parts(value):
    upper = value.astype(jnp.bfloat16)
    return upper, (value - upper.astype(jnp.float32)).astype(jnp.bfloat16)


def times(first, second):
    return jnp.dot(first, second, preferred_element_type=jnp.float32)


def times_stacked(stacked, second):
    rows = stacked.shape[0] // 2
    upper, lower = parts(second)
    both = times(stacked, upper)
    return both[:rows] + both[rows:] + times(stacked[:rows], lower)


def spectrum(table, block):
    both = times(table, block)
    rows = both.shape[0] // 2
    return both[:rows], both[rows:], rows // 2


def packed_spectrum(table, block):
    upper, lower, rows = spectrum(table, block)
    total = upper + lower
    return total[:rows], total[rows:]


def conj_product(first, second):
    real_a, imag_a = first
    real_b, imag_b = second
    return real_a * real_b + imag_a * imag_b, real_a * imag_b - imag_a * real_b


def pair_products(first, second, net, weight):
    units = weight.shape[0]
    pair = jnp.concatenate(conj_product(first, second), axis=0)
    upper, lower = parts(pair)
    net_hi, net_lo = parts(net)
    both = times(jnp.concatenate([net_hi, net_lo], axis=0), upper)
    coef = both[:units] + both[units:] + times(net_hi, lower)
    weight_hi, weight_lo = parts(weight)
    last = (((1,), (1,)), ((), ()))
    both = lax.dot_general(
        upper, jnp.concatenate([weight_hi, weight_lo], axis=0), last, preferred_element_type=jnp.float32
    )
    mix = both[:, :units] + both[:, units:] + lax.dot_general(
        lower, weight_hi, last, preferred_element_type=jnp.float32
    )
    return coef, mix


def started(sems, pairs):
    copies = [
        pltpu.make_async_copy(source, target, sems.at[i]) for i, (source, target) in enumerate(pairs)
    ]
    for copy in copies:
        copy.start()
    return copies


def prepare_kernel(
    embed_in, lift_weight_in, lift_bias_in, inverse_in, split_in, c0_in, x0_in, weight_in,
    net, slope, coef, mix, split, in_spec,
    embed, lift_weight, lift_bias, inverse, c0, x0, weight, slope_kept, sems,
):
    copies = started(
        sems,
        [
            (embed_in, embed), (lift_weight_in, lift_weight), (lift_bias_in, lift_bias),
            (inverse_in, inverse), (split_in, split), (c0_in, c0), (x0_in, x0), (weight_in, weight),
        ],
    )
    units = lift_weight.shape[1]
    length = inverse.shape[0] // 2
    for copy in copies[:3]:
        copy.wait()
    features = lift_weight.shape[0]
    lift_hi, lift_lo = parts(lift_weight[...])
    preact = (
        times(embed[...], jnp.concatenate([lift_hi, lift_hi], axis=0))
        + times(embed[:, :features], lift_lo)
        + lift_bias[...]
    )
    logistic = jax.nn.sigmoid(preact)
    hidden = preact * logistic
    slope_kept[...] = logistic * (1.0 + preact * (1.0 - logistic))
    slope_copy = pltpu.make_async_copy(slope_kept, slope, sems.at[len(copies)])
    slope_copy.start()
    rows = jnp.concatenate(
        [hidden[k * length:(k + 1) * length].T for k in range(LAG_BLOCKS)], axis=0
    )
    upper, lower = parts(rows)
    count = rows.shape[0]
    copies[3].wait()
    both = times(jnp.concatenate([upper, lower], axis=0), inverse[:length, :])
    plain = both[:count] + both[count:] + times(upper, inverse[length:, :])
    moved = turned(plain, 1)
    net[:units, :] = plain[:units]
    net[units:count, :] = plain[units:] + moved[:-units]
    net[count:, :] = moved[-units:]
    for copy in copies[4:]:
        copy.wait()
    own = packed_spectrum(split[...], c0[...])
    source = packed_spectrum(split[...], x0[...])
    in_spec[...] = jnp.concatenate(source, axis=0)
    coef[...], mix[...] = pair_products(source, own, plain[:units], weight[...])
    slope_copy.wait()


def halved(ref):
    rows = ref.shape[0] // 2
    return ref[:rows, :], ref[rows:, :]


def lag_kernel(
    scale, own,
    c2, x2, c1, first_coef, first_mix, net, in_ref, split,
    x0_in, weight_in, inverse_in, embed_in, slope_in, out, same,
    weight, inverse, embed, slope, packed, sems,
):
    copies = started(
        sems,
        [(weight_in, weight), (inverse_in, inverse), (embed_in, embed), (slope_in, slope), (c1, same)],
    )
    units, channels = weight.shape
    table = split[...]
    next_spec, ahead_spec, back_spec = [packed_spectrum(table, ref[...]) for ref in (c1, c2, x2)]
    in_spec = halved(in_ref)
    copies[0].wait()
    products = [
        (in_spec, next_spec),
        (in_spec, ahead_spec),
        (back_spec, next_spec),
        (back_spec, ahead_spec),
    ]
    coef = first_coef[...]
    mixes = [first_mix[...]]
    for k, (first, second) in enumerate(products, 1):
        part, mix = pair_products(first, second, net[k * units:(k + 1) * units, :], weight[...])
        coef = coef + part
        mixes.append(mix)
    coef = coef * scale
    sides = jnp.concatenate([coef[:, k * units:(k + 1) * units] for k in range(channels // units)], axis=0)
    owners = sides.shape[0] // own
    chunk = packed.shape[0] // owners
    for o in range(owners):
        packed[o * chunk:o * chunk + own, :] = sides[o * own:(o + 1) * own]
    for copy in copies[1:]:
        copy.wait()
    sides = jnp.concatenate(
        [mixes[k] - turned(mixes[k + 1], 0) for k in range(LAG_BLOCKS)], axis=1
    )
    lagged = times_stacked(inverse[...], sides)
    grads = jnp.concatenate(
        [lagged[:, k * units:(k + 1) * units] for k in range(LAG_BLOCKS)], axis=0
    ) * (slope[...] * scale)
    lift = times_stacked(embed[...], grads)
    bias = jnp.sum(grads, axis=0, keepdims=True)
    lift_rows = chunk - own - 1
    half = owners // 2
    sent = []
    for o in range(owners):
        packed[o * chunk + own:(o + 1) * chunk - 1, :] = lift[o * lift_rows:(o + 1) * lift_rows]
        packed[(o + 1) * chunk - 1:(o + 1) * chunk, :] = bias
        if o % half == half - 1:
            rows = pl.ds((o + 1 - half) * chunk, half * chunk)
            sent.append(pltpu.make_async_copy(packed.at[rows], out.at[rows], sems.at[len(copies) + len(sent)]))
            sent[-1].start()
    for copy in sent:
        copy.wait()


def tokens_terms(net, weight, specs):
    units = weight.shape[0]
    weight_hi, weight_lo = parts(weight)
    doubled = jnp.concatenate([weight_hi, weight_hi], axis=0)
    total = None
    for k, spec in enumerate(specs):
        net_hi, net_lo = parts(net[k * units:(k + 1) * units, :].T)
        coef = times(jnp.concatenate([net_hi, net_lo], axis=1), doubled) + times(net_hi, weight_lo)
        half = coef.shape[0] // 2
        term = conj_product((coef[:half], coef[half:]), spec)
        total = term if total is None else (total[0] + term[0], total[1] + term[1])
    return total


def early_tokens_kernel(
    c2, net, split, c0_in, c1_in, weight_in, behind, out, same,
    c0, c1, weight, total_kept, sems,
):
    copies = started(sems, [(c0_in, c0), (c1_in, c1), (weight_in, weight), (c2, same)])
    for copy in copies[:3]:
        copy.wait()
    table = split[...]
    specs = [packed_spectrum(table, ref[...]) for ref in (c0, c1)]
    total = tokens_terms(net[:len(specs) * weight.shape[0], :], weight[...], specs)
    total_kept[...] = jnp.concatenate(total, axis=0)
    copies[3].wait()
    for copy in started(sems, [(total_kept, out)]):
        copy.wait()


def late_tokens_kernel(
    c3, c4, net, split, c2_in, weight_in, early_in, inverse_in, out, c2, weight, early, inverse, sems
):
    copies = started(sems, [(c2_in, c2), (weight_in, weight), (early_in, early), (inverse_in, inverse)])
    table = split[...]
    later = [packed_spectrum(table, ref[...]) for ref in (c3, c4)]
    for copy in copies[:2]:
        copy.wait()
    specs = [packed_spectrum(table, c2[...])] + later
    done = net.shape[0] - len(specs) * weight.shape[0]
    terms = tokens_terms(net[done:, :], weight[...], specs)
    copies[2].wait()
    total = [a + b for a, b in zip(halved(early), terms)]
    copies[3].wait()
    length = c3.shape[0]
    out[...] = times_stacked(inverse[...], jnp.concatenate(total, axis=0)) * (1.0 / length)


def first_sum_kernel(slots, value, early, out):
    chunk = out.shape[0] // slots
    total = value[:chunk, :]
    for o in range(1, value.shape[0] // chunk):
        total = total + value[o * chunk:(o + 1) * chunk, :]
    for i in range(slots):
        out[i * chunk:(i + 1) * chunk, :] = total


def choose_kernel(core, relayed, block, out):
    out[...] = jnp.where(core[0] == 0, relayed[...].astype(jnp.float32), block[...].astype(jnp.float32)).astype(
        out.dtype
    )


def second_sum_kernel(own, slots, line, value, block, out, same):
    same[...] = block[...]
    lines = slots // CORES
    place = line[0]
    chunk = value.shape[0] // slots
    coef = jnp.zeros((own, value.shape[1]), jnp.float32)
    rest = jnp.zeros((chunk - own, value.shape[1]), jnp.float32)
    for i in range(slots):
        coef = coef + jnp.where(place == i % lines, value[i * chunk:i * chunk + own, :], 0.0)
        rest = rest + value[i * chunk + own:(i + 1) * chunk, :]
    for o in range(out.shape[0] // chunk):
        out[o * chunk:o * chunk + own, :] = coef
        out[o * chunk + own:(o + 1) * chunk, :] = rest


def unpack_kernel(own, owners, value, coef, lift, bias):
    units = value.shape[1]
    chunk = value.shape[0] // owners
    each = coef.shape[0] // own
    rows = chunk - own - 1
    for o in range(owners):
        column, row = o // each, o % each
        coef[row * own:(row + 1) * own, column * units:(column + 1) * units] = value[
            o * chunk:o * chunk + own, :
        ]
        lift[o * rows:(o + 1) * rows, :] = value[o * chunk + own:(o + 1) * chunk - 1, :]
    bias[...] = value[chunk - 1:chunk, :]


def called(kernel, mebibytes, shapes, *operands, **options):
    return pl.pallas_call(
        kernel,
        out_shape=shapes,
        compiler_params=pltpu.CompilerParams(vmem_limit_bytes=mebibytes * 2 ** 20),
        **options,
    )(*operands)


def shards(tokens_in, cotangent, lift_weight, lift_bias, coef_weight):
    inputs = tokens_in[0]
    grads = cotangent[0]
    length, channels = inputs.shape
    lags = LAG_BLOCKS * length
    features, units = lift_weight.shape
    depth = coef_weight.shape[0]
    blocks_total = lax.axis_size("ctx")

    core = (lax.axis_index("ctx") % CORES).astype(jnp.int32).reshape(1)
    ahead2 = shifted(grads, "ctx", -CORES)
    behind2 = shifted(inputs, "ctx", CORES)
    ahead1 = shifted(grads, "ctx", -1)

    def real(*shape):
        return jax.ShapeDtypeStruct(shape, jnp.float32)

    def like(value):
        return jax.ShapeDtypeStruct(value.shape, value.dtype)

    scalar = pl.BlockSpec(memory_space=pltpu.SMEM)
    whole = pl.BlockSpec(memory_space=pltpu.VMEM)
    table = odd_table(length)
    split = jnp.asarray(halves(table))
    inverse = jnp.asarray(halves(table.T))
    features_table = lag_features(lags, features)
    embed = jnp.asarray(halves(features_table.T).T)
    embed_turned = jnp.asarray(halves(features_table.T))

    def held(value):
        return pltpu.with_memory_space_constraint(value, pltpu.HBM)

    def room(value):
        return pltpu.VMEM(value.shape, value.dtype)

    def sems(count):
        return pltpu.SemaphoreType.DMA((count,))

    far_off = pl.BlockSpec(memory_space=pltpu.HBM)
    bias_row = lift_bias[None]
    first_operands = (embed, lift_weight, bias_row, inverse, split, grads, inputs, coef_weight)
    net, slope, coef, mix, split, in_spec = called(
        prepare_kernel,
        24,
        (
            real((LAG_BLOCKS + 1) * units, 2 * length),
            pltpu.HBM((lags, units), jnp.float32),
            real(depth, channels),
            real(2 * length, units),
            like(split),
            real(2 * length, channels),
        ),
        *[held(value) for value in first_operands],
        in_specs=[far_off] * 8,
        out_specs=[whole, far_off] + [whole] * 4,
        scratch_shapes=[room(value) for value in first_operands if value is not split]
        + [pltpu.VMEM((lags, units), jnp.float32), sems(9)],
    )
    planes, columns = device_groups()
    owners, slots = len(planes[0]), len(columns[0])
    own = channels // units * depth // owners
    chunk = own + features // owners + 1
    scale = 1.0 / math.sqrt(lax.axis_size("dp") * length * blocks_total) / length

    def rows_of(count):
        return real(count * chunk, units)

    packed, ahead1 = called(
        lambda *refs: lag_kernel(scale, own, *refs),
        32,
        (pltpu.HBM((owners * chunk, units), jnp.float32), pltpu.HBM(ahead1.shape, ahead1.dtype)),
        ahead2, behind2, ahead1, coef, mix, net, in_spec, split,
        *[held(value) for value in (inputs, coef_weight, inverse, embed_turned, slope)],
        in_specs=[whole] * 8 + [far_off] * 5,
        out_specs=[far_off] * 2,
        scratch_shapes=[room(value) for value in (coef_weight, inverse, embed_turned, slope)]
        + [pltpu.VMEM((owners * chunk, units), jnp.float32), sems(7)],
    )
    summed = exchanged(packed, ("dp", "ctx"), planes)
    early, ahead2 = called(
        early_tokens_kernel,
        24,
        (pltpu.HBM((2 * length, channels), jnp.float32), pltpu.HBM(ahead2.shape, ahead2.dtype)),
        ahead2, net, split,
        *[held(value) for value in (grads, ahead1, coef_weight)],
        behind2,
        in_specs=[whole] * 3 + [far_off] * 3 + [pl.BlockSpec(memory_space=pl.ANY)],
        out_specs=[far_off] * 2,
        scratch_shapes=[room(value) for value in (grads, ahead1, coef_weight)]
        + [pltpu.VMEM((2 * length, channels), jnp.float32), sems(4)],
    )
    summed = called(
        lambda *refs: first_sum_kernel(slots, *refs),
        8,
        rows_of(slots),
        summed, held(early),
        in_specs=[whole, far_off],
    )
    last = shifted(ahead2, "ctx", -CORES)
    ahead3 = swapped(
        called(choose_kernel, 8, like(last), core, last, ahead2, in_specs=[scalar] + [whole] * 2)
    )
    summed = exchanged(summed, ("ctx", "ch"), columns)
    line = lax.axis_index("ch").astype(jnp.int32).reshape(1)
    spread, ahead3 = called(
        lambda *refs: second_sum_kernel(own, slots, *refs),
        8,
        (rows_of(owners), like(last)),
        line, summed, ahead3,
        in_specs=[scalar] + [whole] * 2,
    )
    full = exchanged(spread, ("dp", "ctx"), planes)
    coef_weight_grad, lift_weight_grad, lift_bias_grad = called(
        lambda *refs: unpack_kernel(own, owners, *refs),
        8,
        (
            jax.ShapeDtypeStruct((depth, channels), jnp.float32),
            jax.ShapeDtypeStruct((features, units), jnp.float32),
            jax.ShapeDtypeStruct((1, units), jnp.float32),
        ),
        full,
    )
    tokens_grad = called(
        late_tokens_kernel,
        24,
        real(length, channels),
        ahead3, last, net, split,
        *[held(value) for value in (ahead2, coef_weight, early, inverse)],
        in_specs=[whole] * 4 + [far_off] * 4,
        scratch_shapes=[room(value) for value in (ahead2, coef_weight, early, inverse)] + [sems(4)],
    )
    return (tokens_grad[None], lift_weight_grad, lift_bias_grad[0], coef_weight_grad)


def solution(mesh):
    in_specs = (P("dp", "ctx", "ch"), P("dp", "ctx", "ch"), P(), P(), P(None, "ch"))
    out_specs = (P("dp", "ctx", "ch"), P(), P(), P(None, "ch"))
    return jax.shard_map(shards, mesh=mesh, in_specs=in_specs, out_specs=out_specs, check_vma=False)
```
